32 devices in a mesh: row: 8 (over z, x), col: 4 (over y, core).
Axes of the slice: x: 2, y: 2, z: 4, core: 2. Of those that a mesh axis runs over, the one named last changes fastest.
Arguments:
- block_values: bfloat16 [8, 4, 256, 128, 128], P('row', 'col')
- block_rows: int32 [8, 4, 256], P('row', 'col'), may hold values from -1 to 511, as said below
- block_cols: int32 [8, 4, 256], P('row', 'col'), may hold values from -1 to 511, as said below
- cost_vec: float32 [262144], P('col')
- demand: float32 [524288], P('row')
- lower: float32 [262144], P('col'), may hold values from -1.5 to -0.2
- upper: float32 [262144], P('col'), may hold values from 0.2 to 1.5
- bound_kind: int32 [262144], P('col'), may hold values from 0 to 3
- primal_start: float32 [262144], P('col'), may hold values from -4 to 4
- dual_start: float32 [524288], P('row'), may hold values from 0 to 1.5
Outputs:
- primal_out: float32 [262144], P('col')
- dual_out: float32 [524288], P('row')
The draws below stay inside these ranges and needn't reach their ends.
Inputs may be any that keep to these rules, and one draw needn't show every extreme that they name: A slot's block_rows and block_cols are both -1 exactly when the slot is empty; the live slots of a device come first, a device has at least 128 of them, and in every draw some device has all 256 slots live and some device has empty slots; every block row and every block column of the whole matrix is named by some live slot; a block place may be named by several slots. `block_cols`: as for block_rows.
All inputs are finite; a program needn't handle non-finite values.
Results may differ from the reference program's by a relative error of at most 0.0073.
Values sent between devices are 32-bit elements; how exact they have to be, the bound alone decides.
No kernel may reach another device: no remote copies, remote signals or barrier semaphores. Data moves between devices by JAX's collectives and lax.ppermute only.
A program may use at most 64 MiB of HBM per device.

```python
import math
import jax
import jax.numpy as jnp
from jax import lax

TILE = 128
ROW_TILES = 512
COL_TILES = 512
SLOTS = 256
RUIZ_PASSES = 2
ITERS = 2
ROW_GROUPS = 8
COL_GROUPS = 4
CONSTRAINTS = 524288
VARIABLES = 262144


def pattern(key):
    folded = jax.random.fold_in(key, 11)
    key_list = jax.random.split(folded, 4)
    devices = ROW_GROUPS * COL_GROUPS
    row_cover = ROW_TILES // COL_GROUPS
    col_cover = COL_TILES // ROW_GROUPS
    fewest = max(row_cover, col_cover)
    counts = jax.random.randint(key_list[0], (devices,), fewest, SLOTS + 1)
    busiest = jax.random.randint(key_list[1], (), 0, devices)
    device_ids = jnp.arange(devices)
    counts = jnp.where(device_ids == busiest, SLOTS, counts)
    counts = jnp.where(device_ids == (busiest + 1) % devices, fewest, counts)
    slot_ids = jnp.arange(SLOTS)[None, :]
    group_row = (device_ids // COL_GROUPS)[:, None]
    group_col = (device_ids % COL_GROUPS)[:, None]
    random_rows = jax.random.randint(key_list[2], (devices, SLOTS), 0, ROW_TILES)
    random_cols = jax.random.randint(key_list[3], (devices, SLOTS), 0, COL_TILES)
    row_ids = jnp.where(slot_ids < row_cover, slot_ids * COL_GROUPS + group_col, random_rows)
    col_ids = jnp.where(slot_ids < col_cover, slot_ids * ROW_GROUPS + group_row, random_cols)
    live_slot = slot_ids < counts[:, None]
    row_ids = jnp.where(live_slot, row_ids, -1).astype(jnp.int32)
    col_ids = jnp.where(live_slot, col_ids, -1).astype(jnp.int32)
    return (row_ids.reshape(ROW_GROUPS, COL_GROUPS, SLOTS), col_ids.reshape(ROW_GROUPS, COL_GROUPS, SLOTS))


def draw_block_rows(key, part):
    return pattern(key)[0]


def draw_block_cols(key, part):
    return pattern(key)[1]


def draw_block_values(key, part):
    key_list = jax.random.split(jax.random.fold_in(key, 3), 3)
    full_shape = (ROW_GROUPS, COL_GROUPS, SLOTS, TILE, TILE)
    entries = jax.random.normal(key_list[0], full_shape, jnp.float32)
    row_factor = jnp.exp(jax.random.uniform(key_list[1], (ROW_GROUPS, COL_GROUPS, SLOTS, TILE, 1), jnp.float32) * math.log(10.0))
    col_factor = jnp.exp(jax.random.uniform(key_list[2], (ROW_GROUPS, COL_GROUPS, SLOTS, 1, TILE), jnp.float32) * math.log(10.0))
    return (entries * row_factor * col_factor * 0.3).astype(jnp.bfloat16)


def rising_vector(key, length):
    position = jnp.arange(length).astype(jnp.float32) / max(length - 1, 1)
    rising = 1.0 + 2.0 * position
    entries = jax.random.normal(key, (length,), jnp.float32)
    return entries * rising


def draw_cost_vec(key, part):
    return rising_vector(jax.random.fold_in(key, 5), VARIABLES)


def draw_demand(key, part):
    return rising_vector(jax.random.fold_in(key, 7), CONSTRAINTS)


def with_ends(result, rng, least, top_value):
    index_at = [jax.random.randint(jax.random.fold_in(rng, axis), (), 0, length) for axis, length in enumerate(result.shape)]
    widest = result.shape.index(max(result.shape))
    beside = index_at[:widest] + [(index_at[widest] + 1) % result.shape[widest]] + index_at[widest + 1:]
    return result.at[tuple(index_at)].set(least).at[tuple(beside)].set(top_value)


def shard_levels(own_key, extent, cuts, least, largest):
    loudness = 1.0
    for dim, parts in cuts:
        steps = jax.random.uniform(jax.random.fold_in(jax.random.fold_in(own_key, 6), dim), (parts,), jnp.float32, least / len(cuts), largest / len(cuts))
        loudness = loudness * jnp.repeat(jnp.exp(steps), extent[dim] // parts).reshape((-1,) + (1,) * (len(extent) - 1 - dim))
    return loudness


def gaussian(key, dims, width, limit, cuts=(), held_as=jnp.bfloat16):
    gain = shard_levels(key, dims, cuts, -0.22, 0.18) if cuts else 1.0
    array = jax.random.normal(key, dims, jnp.float32) * width * gain
    return jnp.minimum(jnp.maximum(array, -limit), limit).astype(held_as)


def setup_inputs(seed: int = 0) -> dict:
    keys = jax.random.split(jax.random.key(seed), 11)
    return {
        "block_values": draw_block_values(jax.random.fold_in(keys[10], 71), 0),
        "block_rows": draw_block_rows(jax.random.fold_in(keys[10], 71), 0),
        "block_cols": draw_block_cols(jax.random.fold_in(keys[10], 71), 0),
        "cost_vec": draw_cost_vec(jax.random.fold_in(keys[10], 71), 0),
        "demand": draw_demand(jax.random.fold_in(keys[10], 71), 0),
        "lower": jnp.clip(-1.5 + 1.3 * jax.random.uniform(keys[5], (VARIABLES,), jnp.float32) ** shard_levels(keys[5], (VARIABLES,), ((0, 4),), -0.2, 0.2), -1.5, -0.2),
        "upper": jnp.clip(0.2 + 1.3 * jax.random.uniform(keys[6], (VARIABLES,), jnp.float32) ** shard_levels(keys[6], (VARIABLES,), ((0, 4),), -0.2, 0.2), 0.2, 1.5),
        "bound_kind": with_ends(jax.random.randint(keys[7], (VARIABLES,), 0, 4), jax.random.fold_in(keys[7], 1), 0, 3).astype(jnp.int32),
        "primal_start": gaussian(keys[8], (VARIABLES,), 0.7, 4.0, ((0, 4),), jnp.float32),
        "dual_start": jnp.clip(1.5 * jax.random.uniform(keys[9], (CONSTRAINTS,), jnp.float32) ** shard_levels(keys[9], (CONSTRAINTS,), ((0, 8),), -0.2, 0.2), 0.0, 1.5),
    }


SMALL_EPS = 1e-06
STEP_SCALE = 0.3

def pick_tiles(vector, slot_ids, tile_count):
    tile_width = vector.shape[0] // tile_count
    padded = jnp.concatenate([vector.reshape(tile_count, tile_width), jnp.zeros((1, tile_width), vector.dtype)], axis=0)
    return padded[slot_ids]

def tile_peaks(block_terms, slot_ids, tile_count):
    tile_width = block_terms.shape[1]
    return jnp.zeros((tile_count + 1, tile_width), jnp.float32).at[slot_ids].max(block_terms)[:tile_count].reshape(-1)

def tile_sums(block_terms, slot_ids, tile_count):
    tile_width = block_terms.shape[1]
    return jnp.zeros((tile_count + 1, tile_width), jnp.float32).at[slot_ids].add(block_terms)[:tile_count].reshape(-1)

def project_bounds(values, low_side, high_side, bound_types):
    lifted = jnp.where((bound_types == 1) | (bound_types == 3), jnp.maximum(values, low_side), values)
    return jnp.where((bound_types == 2) | (bound_types == 3), jnp.minimum(lifted, high_side), lifted)

def slots_of(row_ids, col_ids):
    live_slot = row_ids >= 0
    return (jnp.where(live_slot, row_ids, ROW_TILES).astype(jnp.int32), jnp.where(live_slot, col_ids, COL_TILES).astype(jnp.int32))

def reference(block_values, block_rows, block_cols, cost_vec, demand, lower, upper, bound_kind, primal_start, dual_start):
    devices = ROW_GROUPS * COL_GROUPS
    flat_values = block_values.reshape(devices, SLOTS, TILE, TILE)
    flat_rows = block_rows.reshape(devices, SLOTS)
    flat_cols = block_cols.reshape(devices, SLOTS)
    group_rows = (jnp.arange(devices) // COL_GROUPS).astype(jnp.int32)
    group_cols = (jnp.arange(devices) % COL_GROUPS).astype(jnp.int32)
    device_items = (flat_values, flat_rows, flat_cols, group_rows, group_cols)
    row_scale = jnp.ones((CONSTRAINTS,), jnp.float32)
    col_scale = jnp.ones((VARIABLES,), jnp.float32)
    for pass_index in range(RUIZ_PASSES):

        def device_peaks(device_item, row_scale=row_scale, col_scale=col_scale):
            values, row_ids, col_ids, row_group, col_group = device_item
            row_slot, col_slot = slots_of(row_ids, col_ids)
            row_part = pick_tiles(row_scale.reshape(ROW_GROUPS, -1)[row_group], row_slot, ROW_TILES)
            col_part = pick_tiles(col_scale.reshape(COL_GROUPS, -1)[col_group], col_slot, COL_TILES)
            scaled = jnp.abs(values.astype(jnp.float32)) * row_part[:, :, None] * col_part[:, None, :]
            return (tile_peaks(lax.optimization_barrier(jnp.max(scaled, axis=2)), row_slot, ROW_TILES), tile_peaks(lax.optimization_barrier(jnp.max(scaled, axis=1)), col_slot, COL_TILES))
        row_parts, col_parts = lax.map(device_peaks, device_items)
        row_peak = lax.optimization_barrier(jnp.max(row_parts.reshape(ROW_GROUPS, COL_GROUPS, -1), axis=1)).reshape(-1)
        col_peak = lax.optimization_barrier(jnp.max(col_parts.reshape(ROW_GROUPS, COL_GROUPS, -1), axis=0)).reshape(-1)
        row_scale = row_scale / jnp.sqrt(row_peak + SMALL_EPS)
        col_scale = col_scale / jnp.sqrt(col_peak + SMALL_EPS)
    scaled_cost = col_scale * cost_vec
    scaled_demand = row_scale * demand
    norm_ratio = jnp.sqrt(jnp.sum(scaled_cost * scaled_cost) + SMALL_EPS) / jnp.sqrt(jnp.sum(scaled_demand * scaled_demand) + SMALL_EPS)
    primal_step = STEP_SCALE / norm_ratio
    dual_step = STEP_SCALE * norm_ratio
    primal = primal_start / col_scale
    dual_now = dual_start / row_scale
    low_side = lower / col_scale
    high_side = upper / col_scale

    def transpose_product(weights):

        def device_term(device_item):
            values, row_ids, col_ids, row_group, col_group = device_item
            row_slot, col_slot = slots_of(row_ids, col_ids)
            picked = pick_tiles(weights.reshape(ROW_GROUPS, -1)[row_group], row_slot, ROW_TILES)
            block_terms = jnp.einsum('kij,ki->kj', values.astype(jnp.float32), picked.astype(jnp.float32))
            return tile_sums(block_terms, col_slot, COL_TILES)
        partials = lax.map(device_term, device_items)
        return lax.optimization_barrier(jnp.sum(partials.reshape(ROW_GROUPS, COL_GROUPS, -1), axis=0)).reshape(-1)

    def forward_product(shifted):

        def device_term(device_item):
            values, row_ids, col_ids, row_group, col_group = device_item
            row_slot, col_slot = slots_of(row_ids, col_ids)
            picked = pick_tiles(shifted.reshape(COL_GROUPS, -1)[col_group], col_slot, COL_TILES)
            block_terms = jnp.einsum('kij,kj->ki', values.astype(jnp.float32), picked.astype(jnp.float32))
            return tile_sums(block_terms, row_slot, ROW_TILES)
        partials = lax.map(device_term, device_items)
        return lax.optimization_barrier(jnp.sum(partials.reshape(ROW_GROUPS, COL_GROUPS, -1), axis=1)).reshape(-1)
    for pass_index in range(ITERS):
        weights = (row_scale * dual_now).astype(jnp.bfloat16)
        gradient = col_scale * transpose_product(weights)
        primal_next = project_bounds(primal - primal_step * (scaled_cost - gradient), low_side, high_side, bound_kind)
        shifted = (col_scale * (2.0 * primal_next - primal)).astype(jnp.bfloat16)
        row_image = row_scale * forward_product(shifted)
        dual_now = jnp.maximum(dual_now + dual_step * (scaled_demand - row_image), 0.0)
        primal = primal_next
    return (col_scale * primal, row_scale * dual_now)
```

```python
import jax
import jax.numpy as jnp
from jax import lax
from jax.sharding import PartitionSpec as P

RUIZ_PASSES = 2
ITERS = 2


SMALL_EPS = 1e-06
STEP_SCALE = 0.3

COL_HALVINGS = 1
ROW_HALVINGS = 2


def swap_bit(vector, axis, size, bit):
    return lax.ppermute(vector, axis, [(i, i ^ bit) for i in range(size)])


def reduce_over(vector, axis, size, halvings, combine):
    kept = []
    bit = 1
    for _ in range(halvings):
        half = vector.shape[0] // 2
        got = swap_bit(vector[half:], axis, size, bit)
        vector = combine(vector[:half], got)
        kept.append(bit)
        bit *= 2
    while bit < size:
        vector = combine(vector, swap_bit(vector, axis, size, bit))
        bit *= 2
    for back in reversed(kept):
        vector = jnp.concatenate([vector, swap_bit(vector, axis, size, back)], axis=0)
    return vector


def own_order(vector, index, halvings):
    shape = vector.shape
    for level in range(halvings):
        parts = vector.reshape(2**level, 2, -1)
        flip = ((index >> level) & 1) == 1
        vector = jnp.where(flip, parts[:, ::-1], parts)
    return vector.reshape(shape)


def own_slots(slot_ids, tile_count, index, halvings):
    place = slot_ids
    for level in range(halvings):
        place = place ^ (((index >> level) & 1) * (tile_count >> (level + 1)))
    return jnp.where(slot_ids >= 0, place, tile_count)


def pick_tiles(vector, slot_ids, tile_count):
    tile_width = vector.shape[0] // tile_count
    padded = jnp.concatenate(
        [vector.reshape(tile_count, tile_width), jnp.zeros((1, tile_width), vector.dtype)], axis=0
    )
    return padded[slot_ids]


def tile_peaks(block_terms, slot_ids, tile_count):
    tile_width = block_terms.shape[1]
    return (
        jnp.zeros((tile_count + 1, tile_width), jnp.float32)
        .at[slot_ids]
        .max(block_terms)[:tile_count]
        .reshape(-1)
    )


def tile_sums(block_terms, slot_ids, tile_count):
    tile_width = block_terms.shape[1]
    return (
        jnp.zeros((tile_count + 1, tile_width), jnp.float32)
        .at[slot_ids]
        .add(block_terms)[:tile_count]
        .reshape(-1)
    )


def project_bounds(values, low_side, high_side, bound_types):
    lifted = jnp.where(
        (bound_types == 1) | (bound_types == 3), jnp.maximum(values, low_side), values
    )
    return jnp.where(
        (bound_types == 2) | (bound_types == 3), jnp.minimum(lifted, high_side), lifted
    )


def per_device(
    row_groups,
    col_groups,
    block_values,
    block_rows,
    block_cols,
    cost_vec,
    demand,
    lower,
    upper,
    bound_kind,
    primal_start,
    dual_start,
):
    values = block_values[0, 0]
    tile_width = values.shape[1]
    row_length = demand.shape[0]
    col_length = cost_vec.shape[0]
    row_count = row_length // tile_width
    col_count = col_length // tile_width
    row_index = lax.axis_index("row")
    col_index = lax.axis_index("col")
    row_slot = own_slots(block_rows[0, 0], row_count, col_index, COL_HALVINGS)
    col_slot = own_slots(block_cols[0, 0], col_count, row_index, ROW_HALVINGS)
    demand, dual_start = [own_order(v, col_index, COL_HALVINGS) for v in (demand, dual_start)]
    cost_vec, lower, upper, bound_kind, primal_start = [
        own_order(v, row_index, ROW_HALVINGS)
        for v in (cost_vec, lower, upper, bound_kind, primal_start)
    ]

    def over_col(vector, combine):
        return reduce_over(vector, "col", col_groups, COL_HALVINGS, combine)

    def over_row(vector, combine):
        return reduce_over(vector, "row", row_groups, ROW_HALVINGS, combine)

    def transpose_product(weights):
        picked = pick_tiles(weights, row_slot, row_count)
        terms = jnp.einsum("kij,ki->kj", values, picked, preferred_element_type=jnp.float32)
        return over_row(tile_sums(terms, col_slot, col_count), jnp.add)

    def forward_product(shifted):
        picked = pick_tiles(shifted, col_slot, col_count)
        terms = jnp.einsum("kij,kj->ki", values, picked, preferred_element_type=jnp.float32)
        return over_col(tile_sums(terms, row_slot, row_count), jnp.add)

    first_product = transpose_product(dual_start.astype(jnp.bfloat16))
    row_scale = jnp.ones((row_length,), jnp.float32)
    col_scale = jnp.ones((col_length,), jnp.float32)
    for pass_index in range(RUIZ_PASSES):
        row_part = pick_tiles(row_scale, row_slot, row_count)
        col_part = pick_tiles(col_scale, col_slot, col_count)
        scaled = jnp.abs(values).astype(jnp.float32) * row_part[:, :, None] * col_part[:, None, :]
        row_peak = over_col(tile_peaks(jnp.max(scaled, axis=2), row_slot, row_count), jnp.maximum)
        col_peak = over_row(tile_peaks(jnp.max(scaled, axis=1), col_slot, col_count), jnp.maximum)
        row_scale = row_scale / jnp.sqrt(row_peak + SMALL_EPS)
        col_scale = col_scale / jnp.sqrt(col_peak + SMALL_EPS)
    scaled_cost = col_scale * cost_vec
    scaled_demand = row_scale * demand
    squares = jnp.stack(
        [
            jnp.sum(scaled_cost * scaled_cost) / row_groups,
            jnp.sum(scaled_demand * scaled_demand) / col_groups,
        ]
    )
    totals = lax.psum(squares, ("row", "col"))
    norm_ratio = jnp.sqrt(totals[0] + SMALL_EPS) / jnp.sqrt(totals[1] + SMALL_EPS)
    primal_step = STEP_SCALE / norm_ratio
    dual_step = STEP_SCALE * norm_ratio
    primal = primal_start / col_scale
    dual_now = dual_start / row_scale
    low_side = lower / col_scale
    high_side = upper / col_scale
    for pass_index in range(ITERS):
        if pass_index == 0:
            product = first_product
        else:
            product = transpose_product((row_scale * dual_now).astype(jnp.bfloat16))
        gradient = col_scale * product
        primal_next = project_bounds(
            primal - primal_step * (scaled_cost - gradient), low_side, high_side, bound_kind
        )
        shifted = (col_scale * (2.0 * primal_next - primal)).astype(jnp.bfloat16)
        row_image = row_scale * forward_product(shifted)
        dual_now = jnp.maximum(dual_now + dual_step * (scaled_demand - row_image), 0.0)
        primal = primal_next
    return (
        own_order(col_scale * primal, row_index, ROW_HALVINGS),
        own_order(row_scale * dual_now, col_index, COL_HALVINGS),
    )


def solution(mesh):
    def body(*args):
        return per_device(mesh.shape["row"], mesh.shape["col"], *args)

    return jax.shard_map(
        body,
        mesh=mesh,
        in_specs=(
            P("row", "col", None, None, None),
            P("row", "col", None),
            P("row", "col", None),
            P("col"),
            P("row"),
            P("col"),
            P("col"),
            P("col"),
            P("col"),
            P("row"),
        ),
        out_specs=(P("col"), P("row")),
        check_vma=False,
    )
```

```python
import functools

import jax
import jax.numpy as jnp
from jax import lax
from jax.experimental import pallas as pl
from jax.experimental.pallas import tpu as pltpu
from jax.sharding import PartitionSpec as P

SMALL_EPS = 1e-06
STEP_SCALE = 0.3

CHUNKS = 8
SLOT_STEP = 32
UNROLL = 8

COL_HALVINGS = ((1, 2), (2, 4))
ROW_HALVING = 1


def bit_of(index, bit):
    return jnp.where((index & bit) != 0, 1, 0)


def col_masks():
    row_index = lax.axis_index("row")
    return [
        bit_of(row_index, first) * 2 + bit_of(row_index, second) for first, second in COL_HALVINGS
    ]


def row_mask():
    return bit_of(lax.axis_index("col"), ROW_HALVING) * (CHUNKS // 2)


def col_chunk(place, masks):
    return place ^ masks[place // (CHUNKS // 2)]


def col_place(tile, count, masks):
    size = count // CHUNKS
    mask = jnp.where(tile >= count // 2, masks[1], masks[0])
    return jnp.where(tile < 0, count, tile ^ (mask * size))


def row_place(tile, count, mask):
    return jnp.where(tile < 0, count, tile ^ (mask * (count // CHUNKS)))


def chunk_rows(chunk, size):
    return pl.ds(pl.multiple_of(chunk * size, size), size)


def piece_chunk(pieces, place, size):
    per_piece = CHUNKS // len(pieces)
    start = (place % per_piece) * size
    return pieces[place // per_piece], pl.ds(start, size)


def store_pieces(acc, pieces, count):
    size = count // len(pieces)
    for index, piece in enumerate(pieces):
        piece[...] = acc[pl.ds(index * size, size), :]


def add_row(acc, place, term, combine):
    acc[pl.ds(place, 1), :] = combine(acc[pl.ds(place, 1), :], term)


def one_row(ref, tile):
    return ref[pl.ds(jnp.maximum(tile, 0), 1), :]


def tree_sum(parts):
    while len(parts) > 1:
        parts = [parts[i] + parts[i + 1] for i in range(0, len(parts), 2)]
    return parts[0]


def fold_rows(values):
    return jnp.sum(values.reshape(-1, 8, values.shape[-1]), axis=0)


def for_slots(rows_ref, cols_ref, values_ref, visit, finish):
    step = pl.program_id(0)

    def group(index, carry):
        found = []
        for inner in range(UNROLL):
            local = index * UNROLL + inner
            slot = step * SLOT_STEP + local
            row, col = rows_ref[slot], cols_ref[slot]
            found.append((row, col, visit(row, col, values_ref[local])))
        for row, col, terms in found:
            finish(row, col, terms)
        return carry

    lax.fori_loop(0, SLOT_STEP // UNROLL, group, 0)


def transposed_term(weights_ref, row, block):
    weights = one_row(weights_ref, row).astype(jnp.bfloat16)
    return jnp.dot(weights, block, preferred_element_type=jnp.float32)


def forward_term(shifted_ref, col, block):
    shifted = one_row(shifted_ref, col).astype(jnp.bfloat16)
    return lax.dot_general(
        shifted, block, (((1,), (1,)), ((), ())), preferred_element_type=jnp.float32
    )


def row_max(values):
    return jnp.max(values, axis=0, keepdims=True)


def packed_max(values):
    folded = jnp.max(values.reshape(-1, 16, values.shape[-1]), axis=0)
    return row_max(folded.astype(jnp.float32))


def first_pass_kernel(count, rows_ref, cols_ref, values_ref, dual_ref, *refs):
    row_out, col_out, product_out = refs[:2], refs[2:6], refs[6:10]
    row_acc, col_acc, product_acc = refs[10:]
    step = pl.program_id(0)
    masks, across = col_masks(), row_mask()

    @pl.when(step == 0)
    def _():
        for acc in (row_acc, col_acc, product_acc):
            acc[...] = jnp.zeros_like(acc)

    def visit(row, col, block):
        size = jnp.abs(block)
        return (packed_max(size.T), packed_max(size), transposed_term(dual_ref, row, block))

    def finish(row, col, terms):
        at_row, at_col = row_place(row, count, across), col_place(col, count, masks)
        add_row(row_acc, at_row, terms[0], jnp.maximum)
        add_row(col_acc, at_col, terms[1], jnp.maximum)
        add_row(product_acc, at_col, terms[2], jnp.add)

    for_slots(rows_ref, cols_ref, values_ref, visit, finish)

    @pl.when(step == pl.num_programs(0) - 1)
    def _():
        store_pieces(row_acc, row_out, count)
        store_pieces(col_acc, col_out, count)
        store_pieces(product_acc, product_out, count)


def second_pass_kernel(count, rows_ref, cols_ref, values_ref, *refs):
    row_in, col_in, row_out, col_out = refs[:2], refs[2:6], refs[6:8], refs[8:12]
    row_scale, col_scale, row_acc, col_acc = refs[12:]
    step = pl.program_id(0)
    masks, across = col_masks(), row_mask()
    size = count // CHUNKS

    @pl.when(step == 0)
    def _():
        row_acc[...] = jnp.zeros_like(row_acc)
        col_acc[...] = jnp.zeros_like(col_acc)
        for place in range(CHUNKS):
            piece, part = piece_chunk(row_in, place, size)
            row_scale[chunk_rows(place ^ across, size), :] = 1.0 / jnp.sqrt(
                piece[part, :] + SMALL_EPS
            )
            piece, part = piece_chunk(col_in, place, size)
            col_scale[chunk_rows(col_chunk(place, masks), size), :] = 1.0 / jnp.sqrt(
                piece[part, :] + SMALL_EPS
            )

    def visit(row, col, block):
        sizes = jnp.abs(block).astype(jnp.float32)
        by_col = sizes * one_row(col_scale, col)
        by_row = sizes * jnp.broadcast_to(one_row(row_scale, row), sizes.shape).T
        return row_max(by_col.T), row_max(by_row)

    def finish(row, col, terms):
        add_row(row_acc, row_place(row, count, across), terms[0], jnp.maximum)
        add_row(col_acc, col_place(col, count, masks), terms[1], jnp.maximum)

    for_slots(rows_ref, cols_ref, values_ref, visit, finish)

    @pl.when(step == pl.num_programs(0) - 1)
    def _():
        for place in range(CHUNKS):
            piece, part = piece_chunk(row_out, place, size)
            scale = row_scale[chunk_rows(place ^ across, size), :]
            piece[part, :] = row_acc[pl.ds(place * size, size), :] * scale
            piece, part = piece_chunk(col_out, place, size)
            scale = col_scale[chunk_rows(col_chunk(place, masks), size), :]
            piece[part, :] = col_acc[pl.ds(place * size, size), :] * scale


def scale_kernel(count, over_rows, pieces, *refs):
    peaks, (scale_ref, vector_ref, new_scale, squares) = refs[:pieces], refs[pieces:]
    masks, across = col_masks(), row_mask()
    size = count // CHUNKS
    sums = []
    for place in range(CHUNKS):
        chunk = place ^ across if over_rows else col_chunk(place, masks)
        part = chunk_rows(chunk, size)
        piece, inside = piece_chunk(peaks, place, size)
        scale = scale_ref[part, :] / jnp.sqrt(piece[inside, :] + SMALL_EPS)
        new_scale[part, :] = scale
        scaled = scale * vector_ref[part, :]
        sums.append(fold_rows(scaled * scaled))
    if over_rows:
        half = CHUNKS // 2
        squares[...] = tree_sum(sums[:half]) + tree_sum(sums[half:])
    else:
        squares[...] = tree_sum(sums)


def norm_ratio(cost_squares, demand_squares):
    cost_total = jnp.sum(cost_squares[...], keepdims=True)
    demand_total = jnp.sum(demand_squares[...], keepdims=True)
    return jnp.sqrt(cost_total + SMALL_EPS) / jnp.sqrt(demand_total + SMALL_EPS)


def forward_kernel(count, first, last, rows_ref, cols_ref, values_ref, *refs):
    product, refs = refs[:4], refs[4:]
    scale_ref, cost_ref, low_ref, high_ref, kind_ref, primal_ref = refs[:6]
    cost_squares, demand_squares, primal_out = refs[6:9]
    row_out, (shifted, row_acc) = refs[9:11], refs[11:]
    step = pl.program_id(0)
    masks, across = col_masks(), row_mask()
    size = count // CHUNKS

    @pl.when(step == 0)
    def _():
        row_acc[...] = jnp.zeros_like(row_acc)
        primal_step = STEP_SCALE / norm_ratio(cost_squares, demand_squares)
        for place in range(CHUNKS):
            part = chunk_rows(col_chunk(place, masks), size)
            piece, inside = piece_chunk(product, place, size)
            scale = scale_ref[part, :]
            primal = primal_ref[part, :]
            if first:
                primal = primal / scale
            gradient = scale * piece[inside, :]
            moved = primal - primal_step * (scale * cost_ref[part, :] - gradient)
            kind = kind_ref[part, :]
            moved = jnp.where(
                (kind == 1) | (kind == 3), jnp.maximum(moved, low_ref[part, :] / scale), moved
            )
            moved = jnp.where(
                (kind == 2) | (kind == 3), jnp.minimum(moved, high_ref[part, :] / scale), moved
            )
            shifted[part, :] = scale * (2.0 * moved - primal)
            primal_out[part, :] = scale * moved if last else moved

    def visit(row, col, block):
        return forward_term(shifted, col, block)

    def finish(row, col, term):
        add_row(row_acc, row_place(row, count, across), term, jnp.add)

    for_slots(rows_ref, cols_ref, values_ref, visit, finish)

    @pl.when(step == pl.num_programs(0) - 1)
    def _():
        store_pieces(row_acc, row_out, count)


def next_dual(first, image, inside, scale, demand, dual, dual_step):
    if first:
        dual = dual / scale
    row_image = scale * image[inside, :]
    return jnp.maximum(dual + dual_step * (scale * demand - row_image), 0.0)


def transposed_kernel(count, first, rows_ref, cols_ref, values_ref, *refs):
    image, refs = refs[:2], refs[2:]
    scale_ref, demand_ref, dual_ref, cost_squares, demand_squares, dual_out = refs[:6]
    product_out, (weights, product_acc) = refs[6:10], refs[10:]
    step = pl.program_id(0)
    masks, across = col_masks(), row_mask()
    size = count // CHUNKS

    @pl.when(step == 0)
    def _():
        product_acc[...] = jnp.zeros_like(product_acc)
        dual_step = STEP_SCALE * norm_ratio(cost_squares, demand_squares)
        for place in range(CHUNKS):
            part = chunk_rows(place ^ across, size)
            piece, inside = piece_chunk(image, place, size)
            scale = scale_ref[part, :]
            dual = next_dual(
                first, piece, inside, scale, demand_ref[part, :], dual_ref[part, :], dual_step
            )
            dual_out[part, :] = dual
            weights[part, :] = scale * dual

    def visit(row, col, block):
        return transposed_term(weights, row, block)

    def finish(row, col, term):
        add_row(product_acc, col_place(col, count, masks), term, jnp.add)

    for_slots(rows_ref, cols_ref, values_ref, visit, finish)

    @pl.when(step == pl.num_programs(0) - 1)
    def _():
        store_pieces(product_acc, product_out, count)


def last_dual_kernel(count, first, *refs):
    image, refs = refs[:2], refs[2:]
    scale_ref, demand_ref, dual_ref, cost_squares, demand_squares, dual_out = refs
    across = row_mask()
    size = count // CHUNKS
    dual_step = STEP_SCALE * norm_ratio(cost_squares, demand_squares)
    for place in range(CHUNKS):
        part = chunk_rows(place ^ across, size)
        piece, inside = piece_chunk(image, place, size)
        scale = scale_ref[part, :]
        dual = next_dual(
            first, piece, inside, scale, demand_ref[part, :], dual_ref[part, :], dual_step
        )
        dual_out[part, :] = scale * dual


def vectors(*row_counts):
    return [jax.ShapeDtypeStruct((rows, 128), jnp.float32) for rows in row_counts]


def call_plain(kernel, operands, out_shape):
    return pl.pallas_call(
        kernel,
        out_shape=out_shape,
        in_specs=[pl.BlockSpec(memory_space=pltpu.VMEM)] * len(operands),
        out_specs=[pl.BlockSpec(memory_space=pltpu.VMEM)] * len(out_shape),
    )(*operands)


def call_blocks(kernel, slots, operands, out_shape, scratch):
    row_ids, col_ids, values = slots
    width = values.shape[1]
    whole = lambda step, *_: (0, 0)
    return pl.pallas_call(
        kernel,
        out_shape=out_shape,
        grid_spec=pltpu.PrefetchScalarGridSpec(
            num_scalar_prefetch=2,
            grid=(values.shape[0] // SLOT_STEP,),
            in_specs=[pl.BlockSpec((SLOT_STEP, width, width), lambda step, *_: (step, 0, 0))]
            + [pl.BlockSpec(operand.shape, whole) for operand in operands],
            out_specs=[pl.BlockSpec(result.shape, whole) for result in out_shape],
            scratch_shapes=[pltpu.VMEM((rows, width), jnp.float32) for rows in scratch],
        ),
        compiler_params=pltpu.CompilerParams(vmem_limit_bytes=32 * 1024 * 1024),
        cost_estimate=pl.CostEstimate(
            flops=2 * values.size, bytes_accessed=2 * values.size, transcendentals=0
        ),
    )(row_ids, col_ids, values, *operands)


def swap(vector, axis, size, bit):
    return lax.ppermute(vector, axis, [(i, i ^ bit) for i in range(size)])


def reduce_rows(pieces, groups, combine):
    near, far = pieces
    near = combine(near, swap(far, "col", groups, ROW_HALVING))
    bit = 1
    while bit < groups:
        if bit != ROW_HALVING:
            near = combine(near, swap(near, "col", groups, bit))
        bit *= 2
    return [near, swap(near, "col", groups, ROW_HALVING)]


def reduce_cols(pieces, groups, combine):
    halves = [list(pieces[:2]), list(pieces[2:])]
    exchange = lambda vector, bit: swap(vector, "row", groups, bit)
    held = [
        combine(near, exchange(far, first))
        for (near, far), (first, _) in zip(halves, COL_HALVINGS)
    ]
    half = held[0].shape[0] // 2
    held = [
        combine(vector[:half], exchange(vector[half:], second))
        for vector, (_, second) in zip(held, COL_HALVINGS)
    ]
    bits = [1 << k for k in range(groups.bit_length() - 1)]
    orders = [[bit for bit in bits if bit not in halvings] for halvings in COL_HALVINGS]
    for step in range(len(orders[0])):
        held = [
            combine(vector, exchange(vector, order[step])) for vector, order in zip(held, orders)
        ]
    held = [
        jnp.concatenate([vector, exchange(vector, second)], axis=0)
        for vector, (_, second) in zip(held, COL_HALVINGS)
    ]
    return [
        part
        for vector, (first, _) in zip(held, COL_HALVINGS)
        for part in (vector, exchange(vector, first))
    ]


def sum_all(vector, axis, groups):
    parts = [vector] + [swap(vector, axis, groups, bits) for bits in range(1, groups)]
    return tree_sum(parts)


def per_device(
    row_groups,
    col_groups,
    block_values,
    block_rows,
    block_cols,
    cost_vec,
    demand,
    lower,
    upper,
    bound_kind,
    primal_start,
    dual_start,
):
    values = block_values[0, 0]
    width = values.shape[1]
    slots = (block_rows[0, 0], block_cols[0, 0], values)
    row_length, col_length = demand.shape[0], cost_vec.shape[0]
    cost_vec, demand, lower, upper, bound_kind, primal_start, dual_start = [
        v.reshape(-1, width)
        for v in (cost_vec, demand, lower, upper, bound_kind, primal_start, dual_start)
    ]
    count = demand.shape[0]
    half, quarter, spare = count // 2, count // 4, count + 8
    row_pieces, col_pieces = vectors(half, half), vectors(*[quarter] * 4)
    whole = vectors(count)
    squares = vectors(8)

    def over_col(pieces, combine):
        return reduce_rows(pieces, col_groups, combine)

    def over_row(pieces, combine):
        return reduce_cols(pieces, row_groups, combine)

    out = call_blocks(
        functools.partial(first_pass_kernel, count),
        slots,
        [dual_start],
        row_pieces + col_pieces + col_pieces,
        [spare] * 3,
    )
    row_peaks = over_col(out[:2], jnp.maximum)
    col_peaks = over_row(out[2:6], jnp.maximum)
    product = over_row(out[6:], jnp.add)
    out = call_blocks(
        functools.partial(second_pass_kernel, count),
        slots,
        row_peaks + col_peaks,
        row_pieces + col_pieces + whole + whole,
        [spare] * 2,
    )
    row_scale, col_scale = out[6:]
    row_peaks = over_col(out[:2], jnp.maximum)
    row_scale, demand_squares = call_plain(
        functools.partial(scale_kernel, count, True, 2),
        row_peaks + [row_scale, demand],
        whole + squares,
    )
    demand_squares = sum_all(demand_squares, "row", row_groups)
    col_peaks = over_row(out[2:6], jnp.maximum)
    col_scale, cost_squares = call_plain(
        functools.partial(scale_kernel, count, False, 4),
        col_peaks + [col_scale, cost_vec],
        whole + squares,
    )
    cost_squares = sum_all(cost_squares, "col", col_groups)
    norms = [cost_squares, demand_squares]

    def forward(first, last, product, primal):
        out = call_blocks(
            functools.partial(forward_kernel, count, first, last),
            slots,
            product + [col_scale, cost_vec, lower, upper, bound_kind, primal] + norms,
            whole + row_pieces,
            [count, spare],
        )
        return out[0], over_col(out[1:], jnp.add)

    primal, image = forward(True, False, product, primal_start)
    out = call_blocks(
        functools.partial(transposed_kernel, count, True),
        slots,
        image + [row_scale, demand, dual_start] + norms,
        whole + col_pieces,
        [count, spare],
    )
    dual, product = out[0], over_row(out[1:], jnp.add)
    primal, image = forward(False, True, product, primal)
    (dual,) = call_plain(
        functools.partial(last_dual_kernel, count, False),
        image + [row_scale, demand, dual] + norms,
        whole,
    )
    return primal.reshape(col_length), dual.reshape(row_length)


def solution(mesh):
    def body(*args):
        return per_device(mesh.shape["row"], mesh.shape["col"], *args)

    return jax.shard_map(
        body,
        mesh=mesh,
        in_specs=(
            P("row", "col", None, None, None),
            P("row", "col", None),
            P("row", "col", None),
            P("col"),
            P("row"),
            P("col"),
            P("col"),
            P("col"),
            P("col"),
            P("row"),
        ),
        out_specs=(P("col"), P("row")),
        check_vma=False,
    )
```

```python
import functools

import jax
import jax.numpy as jnp
from jax import lax
from jax.experimental import pallas as pl
from jax.experimental.pallas import tpu as pltpu
from jax.sharding import PartitionSpec as P

SMALL_EPS = 1e-06
STEP_SCALE = 0.3

CHUNKS = 8
PRODUCT_GROUP = 32
PEAK_GROUP = 16

COL_HALVINGS = ((1, 2), (2, 4))
ROW_HALVING = 1


def bit_of(index, bit):
    return jnp.where((index & bit) != 0, 1, 0)


def col_masks():
    row_index = lax.axis_index("row")
    return [
        bit_of(row_index, first) * 2 + bit_of(row_index, second) for first, second in COL_HALVINGS
    ]


def row_mask():
    return bit_of(lax.axis_index("col"), ROW_HALVING) * (CHUNKS // 2)


def col_chunk(place, masks):
    return place ^ masks[place // (CHUNKS // 2)]


def col_place(tile, count, masks):
    size = count // CHUNKS
    mask = jnp.where(tile >= count // 2, masks[1], masks[0])
    return jnp.where(tile < 0, count, tile ^ (mask * size))


def row_place(tile, count, mask):
    return jnp.where(tile < 0, count, tile ^ (mask * (count // CHUNKS)))


def chunk_rows(chunk, size):
    return pl.ds(pl.multiple_of(chunk * size, size), size)


def piece_chunk(pieces, place, size):
    per_piece = CHUNKS // len(pieces)
    start = (place % per_piece) * size
    return pieces[place // per_piece], pl.ds(start, size)


def store_pieces(acc, pieces, count):
    size = count // len(pieces)
    for index, piece in enumerate(pieces):
        piece[...] = acc[pl.ds(index * size, size), :]


def add_row(acc, place, term, combine):
    acc[pl.ds(place, 1), :] = combine(acc[pl.ds(place, 1), :], term)


def one_row(ref, tile):
    return ref[pl.ds(jnp.maximum(tile, 0), 1), :]


def tree_sum(parts):
    while len(parts) > 1:
        parts = [parts[i] + parts[i + 1] for i in range(0, len(parts), 2)]
    return parts[0]


def fold_rows(values):
    return jnp.sum(values.reshape(-1, 8, values.shape[-1]), axis=0)


def block_copy(group, index, values_ref, blocks, arrived):
    part = pl.ds(pl.multiple_of(index * group, group), group)
    return pltpu.make_async_copy(values_ref.at[part], blocks.at[part], arrived.at[index])


def start_blocks(group, values_ref, blocks, arrived):
    for index in range(values_ref.shape[0] // group):
        block_copy(group, index, values_ref, blocks, arrived).start()


def for_slots(group, slot_refs, visit, finish):
    rows_ref, cols_ref, values_ref, blocks, arrived = slot_refs

    def step(index, carry):
        block_copy(group, index, values_ref, blocks, arrived).wait()
        found = []
        for inner in range(group):
            slot = index * group + inner
            row, col = rows_ref[slot], cols_ref[slot]
            found.append((row, col, visit(row, col, blocks.at[slot])))
        for row, col, terms in found:
            finish(row, col, terms)
        return carry

    lax.fori_loop(0, values_ref.shape[0] // group, step, 0)


def transposed_term(weights_ref, row, block_ref):
    weights = one_row(weights_ref, row).astype(jnp.bfloat16)
    return jnp.dot(weights, block_ref[...], preferred_element_type=jnp.float32)


def forward_term(shifted_ref, col, block_ref):
    shifted = one_row(shifted_ref, col).astype(jnp.bfloat16)
    return lax.dot_general(
        shifted, block_ref[...], (((1,), (1,)), ((), ())), preferred_element_type=jnp.float32
    )


def row_max(values):
    return jnp.max(values, axis=0, keepdims=True)


def packed_max(values):
    folded = jnp.max(values.reshape(-1, 16, values.shape[-1]), axis=0)
    return row_max(folded.astype(jnp.float32))


def first_pass_kernel(count, rows_ref, cols_ref, values_ref, dual_ref, *refs):
    row_out, col_out, product_out = refs[:2], refs[2:6], refs[6:10]
    blocks, arrived, row_acc, col_acc, product_acc = refs[10:]
    masks, across = col_masks(), row_mask()
    start_blocks(PEAK_GROUP, values_ref, blocks, arrived)
    for acc in (row_acc, col_acc, product_acc):
        acc[...] = jnp.zeros_like(acc)

    def visit(row, col, block_ref):
        size = jnp.abs(block_ref[...])
        return (packed_max(size.T), packed_max(size), transposed_term(dual_ref, row, block_ref))

    def finish(row, col, terms):
        at_row, at_col = row_place(row, count, across), col_place(col, count, masks)
        add_row(row_acc, at_row, terms[0], jnp.maximum)
        add_row(col_acc, at_col, terms[1], jnp.maximum)
        add_row(product_acc, at_col, terms[2], jnp.add)

    for_slots(PEAK_GROUP, (rows_ref, cols_ref, values_ref, blocks, arrived), visit, finish)
    store_pieces(row_acc, row_out, count)
    store_pieces(col_acc, col_out, count)
    store_pieces(product_acc, product_out, count)


def second_pass_kernel(count, rows_ref, cols_ref, values_ref, *refs):
    row_in, col_in, row_out, col_out = refs[:2], refs[2:6], refs[6:8], refs[8:12]
    row_scale, col_scale, blocks, arrived, row_acc, col_acc = refs[12:]
    masks, across = col_masks(), row_mask()
    size = count // CHUNKS
    start_blocks(PEAK_GROUP, values_ref, blocks, arrived)
    row_acc[...] = jnp.zeros_like(row_acc)
    col_acc[...] = jnp.zeros_like(col_acc)
    for place in range(CHUNKS):
        piece, part = piece_chunk(row_in, place, size)
        row_scale[chunk_rows(place ^ across, size), :] = lax.rsqrt(piece[part, :] + SMALL_EPS)
        piece, part = piece_chunk(col_in, place, size)
        col_scale[chunk_rows(col_chunk(place, masks), size), :] = lax.rsqrt(
            piece[part, :] + SMALL_EPS
        )
    width = values_ref.shape[-1]
    square = (width, width)
    diagonal = lax.broadcasted_iota(jnp.int32, square, 0) == lax.broadcasted_iota(
        jnp.int32, square, 1
    )
    diagonal = diagonal.astype(jnp.float32).astype(jnp.bfloat16)

    def visit(row, col, block_ref):
        sizes = jnp.abs(block_ref[...])
        by_col = sizes.astype(jnp.float32) * one_row(col_scale, col)
        scale = one_row(row_scale, row)
        high = scale.astype(jnp.bfloat16)
        low = (scale - high.astype(jnp.float32)).astype(jnp.bfloat16)
        by_row = jnp.dot(
            jnp.concatenate([diagonal * high, diagonal * low], axis=1),
            jnp.concatenate([sizes, sizes], axis=0),
            preferred_element_type=jnp.float32,
        )
        return row_max(by_col.T), row_max(by_row)

    def finish(row, col, terms):
        add_row(row_acc, row_place(row, count, across), terms[0], jnp.maximum)
        add_row(col_acc, col_place(col, count, masks), terms[1], jnp.maximum)

    for_slots(PEAK_GROUP, (rows_ref, cols_ref, values_ref, blocks, arrived), visit, finish)
    for place in range(CHUNKS):
        piece, part = piece_chunk(row_out, place, size)
        scale = row_scale[chunk_rows(place ^ across, size), :]
        piece[part, :] = row_acc[pl.ds(place * size, size), :] * scale
        piece, part = piece_chunk(col_out, place, size)
        scale = col_scale[chunk_rows(col_chunk(place, masks), size), :]
        piece[part, :] = col_acc[pl.ds(place * size, size), :] * scale


def scale_kernel(count, over_rows, pieces, *refs):
    peaks, (scale_ref, vector_ref, new_scale, squares) = refs[:pieces], refs[pieces:]
    masks, across = col_masks(), row_mask()
    size = count // CHUNKS
    sums = []
    for place in range(CHUNKS):
        chunk = place ^ across if over_rows else col_chunk(place, masks)
        part = chunk_rows(chunk, size)
        piece, inside = piece_chunk(peaks, place, size)
        scale = scale_ref[part, :] * lax.rsqrt(piece[inside, :] + SMALL_EPS)
        new_scale[part, :] = scale
        scaled = scale * vector_ref[part, :]
        sums.append(fold_rows(scaled * scaled))
    if over_rows:
        half = CHUNKS // 2
        squares[...] = tree_sum(sums[:half]) + tree_sum(sums[half:])
    else:
        squares[...] = tree_sum(sums)


def norm_ratio(cost_squares, demand_squares):
    cost_total = jnp.sum(cost_squares[...], keepdims=True)
    demand_total = jnp.sum(demand_squares[...], keepdims=True)
    return jnp.sqrt(cost_total + SMALL_EPS) / jnp.sqrt(demand_total + SMALL_EPS)


def forward_kernel(count, first, last, rows_ref, cols_ref, values_ref, *refs):
    product, refs = refs[:4], refs[4:]
    scale_ref, cost_ref, low_ref, high_ref, kind_ref, primal_ref = refs[:6]
    cost_squares, demand_squares, primal_out = refs[6:9]
    row_out, (blocks, arrived, shifted, row_acc) = refs[9:11], refs[11:]
    masks, across = col_masks(), row_mask()
    size = count // CHUNKS
    start_blocks(PRODUCT_GROUP, values_ref, blocks, arrived)
    row_acc[...] = jnp.zeros_like(row_acc)
    primal_step = STEP_SCALE / norm_ratio(cost_squares, demand_squares)
    for place in range(CHUNKS):
        part = chunk_rows(col_chunk(place, masks), size)
        piece, inside = piece_chunk(product, place, size)
        scale = scale_ref[part, :]
        inverse = 1.0 / scale
        primal = primal_ref[part, :]
        if first:
            primal = primal * inverse
        gradient = scale * piece[inside, :]
        moved = primal - primal_step * (scale * cost_ref[part, :] - gradient)
        kind = kind_ref[part, :]
        moved = jnp.where(
            (kind == 1) | (kind == 3), jnp.maximum(moved, low_ref[part, :] * inverse), moved
        )
        moved = jnp.where(
            (kind == 2) | (kind == 3), jnp.minimum(moved, high_ref[part, :] * inverse), moved
        )
        shifted[part, :] = scale * (2.0 * moved - primal)
        primal_out[part, :] = scale * moved if last else moved

    def visit(row, col, block_ref):
        return forward_term(shifted, col, block_ref)

    def finish(row, col, term):
        add_row(row_acc, row_place(row, count, across), term, jnp.add)

    for_slots(PRODUCT_GROUP, (rows_ref, cols_ref, values_ref, blocks, arrived), visit, finish)
    store_pieces(row_acc, row_out, count)


def next_dual(first, image, inside, scale, demand, dual, dual_step):
    if first:
        dual = dual / scale
    row_image = scale * image[inside, :]
    return jnp.maximum(dual + dual_step * (scale * demand - row_image), 0.0)


def transposed_kernel(count, first, rows_ref, cols_ref, values_ref, *refs):
    image, refs = refs[:2], refs[2:]
    scale_ref, demand_ref, dual_ref, cost_squares, demand_squares, dual_out = refs[:6]
    product_out, (blocks, arrived, weights, product_acc) = refs[6:10], refs[10:]
    masks, across = col_masks(), row_mask()
    size = count // CHUNKS
    start_blocks(PRODUCT_GROUP, values_ref, blocks, arrived)
    product_acc[...] = jnp.zeros_like(product_acc)
    dual_step = STEP_SCALE * norm_ratio(cost_squares, demand_squares)
    for place in range(CHUNKS):
        part = chunk_rows(place ^ across, size)
        piece, inside = piece_chunk(image, place, size)
        scale = scale_ref[part, :]
        dual = next_dual(
            first, piece, inside, scale, demand_ref[part, :], dual_ref[part, :], dual_step
        )
        dual_out[part, :] = dual
        weights[part, :] = scale * dual

    def visit(row, col, block_ref):
        return transposed_term(weights, row, block_ref)

    def finish(row, col, term):
        add_row(product_acc, col_place(col, count, masks), term, jnp.add)

    for_slots(PRODUCT_GROUP, (rows_ref, cols_ref, values_ref, blocks, arrived), visit, finish)
    store_pieces(product_acc, product_out, count)


def last_dual_kernel(count, first, *refs):
    image, refs = refs[:2], refs[2:]
    scale_ref, demand_ref, dual_ref, cost_squares, demand_squares, dual_out = refs
    across = row_mask()
    size = count // CHUNKS
    dual_step = STEP_SCALE * norm_ratio(cost_squares, demand_squares)
    for place in range(CHUNKS):
        part = chunk_rows(place ^ across, size)
        piece, inside = piece_chunk(image, place, size)
        scale = scale_ref[part, :]
        dual = next_dual(
            first, piece, inside, scale, demand_ref[part, :], dual_ref[part, :], dual_step
        )
        dual_out[part, :] = scale * dual


def vectors(*row_counts):
    return [jax.ShapeDtypeStruct((rows, 128), jnp.float32) for rows in row_counts]


def call_plain(kernel, operands, out_shape):
    return pl.pallas_call(
        kernel,
        out_shape=out_shape,
        in_specs=[pl.BlockSpec(memory_space=pltpu.VMEM)] * len(operands),
        out_specs=[pl.BlockSpec(memory_space=pltpu.VMEM)] * len(out_shape),
    )(*operands)


def call_blocks(kernel, group, slots, operands, out_shape, scratch):
    row_ids, col_ids, values = slots
    count, width = values.shape[0], values.shape[1]
    return pl.pallas_call(
        kernel,
        out_shape=out_shape,
        in_specs=[pl.BlockSpec(memory_space=pltpu.SMEM)] * 2
        + [pl.BlockSpec(memory_space=pltpu.HBM)]
        + [pl.BlockSpec(memory_space=pltpu.VMEM)] * len(operands),
        out_specs=[pl.BlockSpec(memory_space=pltpu.VMEM)] * len(out_shape),
        scratch_shapes=[
            pltpu.VMEM(values.shape, values.dtype),
            pltpu.SemaphoreType.DMA((count // group,)),
        ]
        + [pltpu.VMEM((rows, width), jnp.float32) for rows in scratch],
        compiler_params=pltpu.CompilerParams(vmem_limit_bytes=32 * 1024 * 1024),
        cost_estimate=pl.CostEstimate(
            flops=2 * values.size, bytes_accessed=2 * values.size, transcendentals=0
        ),
    )(row_ids, col_ids, values, *operands)


def swap(vector, axis, size, bit):
    return lax.ppermute(vector, axis, [(i, i ^ bit) for i in range(size)])


def reduce_rows(pieces, groups, combine):
    near, far = pieces
    near = combine(near, swap(far, "col", groups, ROW_HALVING))
    bit = 1
    while bit < groups:
        if bit != ROW_HALVING:
            near = combine(near, swap(near, "col", groups, bit))
        bit *= 2
    return [near, swap(near, "col", groups, ROW_HALVING)]


def reduce_cols(pieces, groups, combine):
    halves = [list(pieces[:2]), list(pieces[2:])]
    exchange = lambda vector, bit: swap(vector, "row", groups, bit)
    held = [
        combine(near, exchange(far, first))
        for (near, far), (first, _) in zip(halves, COL_HALVINGS)
    ]
    half = held[0].shape[0] // 2
    held = [
        combine(vector[:half], exchange(vector[half:], second))
        for vector, (_, second) in zip(held, COL_HALVINGS)
    ]
    bits = [1 << k for k in range(groups.bit_length() - 1)]
    orders = [[bit for bit in bits if bit not in halvings] for halvings in COL_HALVINGS]
    for step in range(len(orders[0])):
        held = [
            combine(vector, exchange(vector, order[step])) for vector, order in zip(held, orders)
        ]
    held = [
        jnp.concatenate([vector, exchange(vector, second)], axis=0)
        for vector, (_, second) in zip(held, COL_HALVINGS)
    ]
    return [
        part
        for vector, (first, _) in zip(held, COL_HALVINGS)
        for part in (vector, exchange(vector, first))
    ]


def sum_all(vector, axis, groups):
    parts = [vector] + [swap(vector, axis, groups, bits) for bits in range(1, groups)]
    return tree_sum(parts)


def per_device(
    row_groups,
    col_groups,
    block_values,
    block_rows,
    block_cols,
    cost_vec,
    demand,
    lower,
    upper,
    bound_kind,
    primal_start,
    dual_start,
):
    values = block_values[0, 0]
    width = values.shape[1]
    slots = (block_rows[0, 0], block_cols[0, 0], values)
    row_length, col_length = demand.shape[0], cost_vec.shape[0]
    cost_vec, demand, lower, upper, bound_kind, primal_start, dual_start = [
        v.reshape(-1, width)
        for v in (cost_vec, demand, lower, upper, bound_kind, primal_start, dual_start)
    ]
    count = demand.shape[0]
    half, quarter, spare = count // 2, count // 4, count + 8
    row_pieces, col_pieces = vectors(half, half), vectors(*[quarter] * 4)
    whole = vectors(count)
    squares = vectors(8)

    def over_col(pieces, combine):
        return reduce_rows(pieces, col_groups, combine)

    def over_row(pieces, combine):
        return reduce_cols(pieces, row_groups, combine)

    out = call_blocks(
        functools.partial(first_pass_kernel, count),
        PEAK_GROUP,
        slots,
        [dual_start],
        row_pieces + col_pieces + col_pieces,
        [spare] * 3,
    )
    row_peaks = over_col(out[:2], jnp.maximum)
    col_peaks = over_row(out[2:6], jnp.maximum)
    product = over_row(out[6:], jnp.add)
    out = call_blocks(
        functools.partial(second_pass_kernel, count),
        PEAK_GROUP,
        slots,
        row_peaks + col_peaks,
        row_pieces + col_pieces + whole + whole,
        [spare] * 2,
    )
    row_scale, col_scale = out[6:]
    row_peaks = over_col(out[:2], jnp.maximum)
    row_scale, demand_squares = call_plain(
        functools.partial(scale_kernel, count, True, 2),
        row_peaks + [row_scale, demand],
        whole + squares,
    )
    demand_squares = sum_all(demand_squares, "row", row_groups)
    col_peaks = over_row(out[2:6], jnp.maximum)
    col_scale, cost_squares = call_plain(
        functools.partial(scale_kernel, count, False, 4),
        col_peaks + [col_scale, cost_vec],
        whole + squares,
    )
    cost_squares = sum_all(cost_squares, "col", col_groups)
    norms = [cost_squares, demand_squares]

    def forward(first, last, product, primal):
        out = call_blocks(
            functools.partial(forward_kernel, count, first, last),
            PRODUCT_GROUP,
            slots,
            product + [col_scale, cost_vec, lower, upper, bound_kind, primal] + norms,
            whole + row_pieces,
            [count, spare],
        )
        return out[0], over_col(out[1:], jnp.add)

    primal, image = forward(True, False, product, primal_start)
    out = call_blocks(
        functools.partial(transposed_kernel, count, True),
        PRODUCT_GROUP,
        slots,
        image + [row_scale, demand, dual_start] + norms,
        whole + col_pieces,
        [count, spare],
    )
    dual, product = out[0], over_row(out[1:], jnp.add)
    primal, image = forward(False, True, product, primal)
    (dual,) = call_plain(
        functools.partial(last_dual_kernel, count, False),
        image + [row_scale, demand, dual] + norms,
        whole,
    )
    return primal.reshape(col_length), dual.reshape(row_length)


def solution(mesh):
    def body(*args):
        return per_device(mesh.shape["row"], mesh.shape["col"], *args)

    return jax.shard_map(
        body,
        mesh=mesh,
        in_specs=(
            P("row", "col", None, None, None),
            P("row", "col", None),
            P("row", "col", None),
            P("col"),
            P("row"),
            P("col"),
            P("col"),
            P("col"),
            P("col"),
            P("row"),
        ),
        out_specs=(P("col"), P("row")),
        check_vma=False,
    )
```

```python
import functools

import jax
import jax.numpy as jnp
from jax import lax
from jax.experimental import pallas as pl
from jax.experimental.pallas import tpu as pltpu
from jax.sharding import PartitionSpec as P

SMALL_EPS = 1e-06
STEP_SCALE = 0.3

CHUNKS = 8
PRODUCT_GROUP = 32
PEAK_GROUP = 16
ROW_HALVING = 1
STREAM_VMEM = 57 * 1024 * 1024
RESIDENT_VMEM = 16 * 1024 * 1024
SMALL_VMEM = 8 * 1024 * 1024


def bit_of(index, bit):
    return jnp.where((index & bit) != 0, 1, 0)


def row_mask():
    return bit_of(lax.axis_index("col"), ROW_HALVING) * (CHUNKS // 2)


def col_place(tile, count):
    return jnp.where(tile < 0, count, tile)


def row_place(tile, count, mask):
    return jnp.where(tile < 0, count, tile ^ (mask * (count // CHUNKS)))


def chunk_rows(chunk, size):
    return pl.ds(pl.multiple_of(chunk * size, size), size)


def piece_chunk(pieces, place, size):
    per_piece = CHUNKS // len(pieces)
    start = (place % per_piece) * size
    return pieces[place // per_piece], pl.ds(start, size)


def store_pieces(acc, pieces, count):
    size = count // len(pieces)
    for index, piece in enumerate(pieces):
        piece[...] = acc[pl.ds(index * size, size), :]


def add_row(acc, place, term, combine):
    acc[pl.ds(place, 1), :] = combine(acc[pl.ds(place, 1), :], term)


def one_row(ref, tile):
    return ref[pl.ds(jnp.maximum(tile, 0), 1), :]


def tree_sum(parts):
    while len(parts) > 1:
        parts = [parts[i] + parts[i + 1] for i in range(0, len(parts), 2)]
    return parts[0]


def fold_rows(values):
    return jnp.sum(values.reshape(-1, 8, values.shape[-1]), axis=0)


def block_copy(group, index, values_ref, blocks, arrived):
    part = pl.ds(pl.multiple_of(index * group, group), group)
    return pltpu.make_async_copy(values_ref.at[part], blocks.at[part], arrived.at[index])


def start_blocks(group, values_ref, blocks, arrived):
    for index in range(values_ref.shape[0] // group):
        block_copy(group, index, values_ref, blocks, arrived).start()


def for_slots(group, rows_ref, cols_ref, blocks, visit, finish, ready=None):
    def step(index, carry):
        if ready is not None:
            ready(index)
        found = []
        for inner in range(group):
            slot = index * group + inner
            row, col = rows_ref[slot], cols_ref[slot]
            found.append((row, col, visit(row, col, blocks.at[slot])))
        for row, col, terms in found:
            finish(row, col, terms)
        return carry

    lax.fori_loop(0, blocks.shape[0] // group, step, 0)


def transposed_term(weights_ref, row, block_ref):
    weights = one_row(weights_ref, row).astype(jnp.bfloat16)
    return jnp.dot(weights, block_ref[...], preferred_element_type=jnp.float32)


def forward_term(shifted_ref, col, block_ref):
    shifted = one_row(shifted_ref, col).astype(jnp.bfloat16)
    return lax.dot_general(
        shifted, block_ref[...], (((1,), (1,)), ((), ())), preferred_element_type=jnp.float32
    )


def row_max(values):
    return jnp.max(values, axis=0, keepdims=True)


def packed_max(values):
    folded = jnp.max(values.reshape(-1, 16, values.shape[-1]), axis=0)
    return row_max(folded.astype(jnp.float32))


def first_pass_kernel(count, rows_ref, cols_ref, values_ref, dual_ref, *refs):
    near, far, col_out, blocks, arrived, row_acc, col_acc, product_acc = refs
    across = row_mask()
    start_blocks(PEAK_GROUP, values_ref, blocks, arrived)
    for acc in (row_acc, col_acc, product_acc):
        acc[...] = jnp.zeros_like(acc)

    def ready(index):
        block_copy(PEAK_GROUP, index, values_ref, blocks, arrived).wait()

    def visit(row, col, block_ref):
        size = jnp.abs(block_ref[...])
        return (packed_max(size.T), packed_max(size), transposed_term(dual_ref, row, block_ref))

    def finish(row, col, terms):
        at_row, at_col = row_place(row, count, across), col_place(col, count)
        add_row(row_acc, at_row, terms[0], jnp.maximum)
        add_row(col_acc, at_col, terms[1], jnp.maximum)
        add_row(product_acc, at_col, terms[2], jnp.add)

    for_slots(PEAK_GROUP, rows_ref, cols_ref, blocks, visit, finish, ready)
    store_pieces(row_acc, (near, far), count)
    share = col_out.shape[1] // 2
    for owner in range(col_out.shape[0]):
        part = pl.ds(owner * share, share)
        col_out[owner, pl.ds(0, share), :] = col_acc[part, :]
        col_out[owner, pl.ds(share, share), :] = product_acc[part, :]


def second_pass_kernel(count, rows_ref, cols_ref, blocks, *refs):
    row_in, col_in, row_out, col_out = refs[:2], refs[2], refs[3:5], refs[5]
    row_scale, col_scale, row_acc, col_acc = refs[6:]
    across = row_mask()
    size = count // CHUNKS
    row_acc[...] = jnp.zeros_like(row_acc)
    col_acc[...] = jnp.zeros_like(col_acc)
    for place in range(CHUNKS):
        piece, part = piece_chunk(row_in, place, size)
        row_scale[chunk_rows(place ^ across, size), :] = lax.rsqrt(piece[part, :] + SMALL_EPS)
        part = pl.ds(place * size, size)
        col_scale[part, :] = lax.rsqrt(col_in[part, :] + SMALL_EPS)
    width = blocks.shape[-1]
    square = (width, width)
    diagonal = lax.broadcasted_iota(jnp.int32, square, 0) == lax.broadcasted_iota(
        jnp.int32, square, 1
    )
    diagonal = diagonal.astype(jnp.float32).astype(jnp.bfloat16)

    def visit(row, col, block_ref):
        sizes = jnp.abs(block_ref[...])
        by_col = sizes.astype(jnp.float32) * one_row(col_scale, col)
        scale = one_row(row_scale, row)
        high = scale.astype(jnp.bfloat16)
        low = (scale - high.astype(jnp.float32)).astype(jnp.bfloat16)
        by_row = jnp.dot(
            jnp.concatenate([diagonal * high, diagonal * low], axis=1),
            jnp.concatenate([sizes, sizes], axis=0),
            preferred_element_type=jnp.float32,
        )
        return row_max(by_col.T), row_max(by_row)

    def finish(row, col, terms):
        add_row(row_acc, row_place(row, count, across), terms[0], jnp.maximum)
        add_row(col_acc, col_place(col, count), terms[1], jnp.maximum)

    for_slots(PEAK_GROUP, rows_ref, cols_ref, blocks, visit, finish)
    for place in range(CHUNKS):
        piece, part = piece_chunk(row_out, place, size)
        scale = row_scale[chunk_rows(place ^ across, size), :]
        piece[part, :] = row_acc[pl.ds(place * size, size), :] * scale
        part = pl.ds(place * size, size)
        col_out[part, :] = col_acc[part, :] * col_scale[part, :]


def row_scale_kernel(count, near, far, scale_ref, vector_ref, new_scale, squares):
    across = row_mask()
    size = count // CHUNKS
    sums = []
    for place in range(CHUNKS):
        part = chunk_rows(place ^ across, size)
        piece, inside = piece_chunk((near, far), place, size)
        scale = scale_ref[part, :] * lax.rsqrt(piece[inside, :] + SMALL_EPS)
        new_scale[part, :] = scale
        scaled = scale * vector_ref[part, :]
        sums.append(fold_rows(scaled * scaled))
    half = CHUNKS // 2
    squares[...] = tree_sum(sums[:half]) + tree_sum(sums[half:])


def col_scale_kernel(count, gathered, scale_ref, vector_ref, new_scale, squares, demand_squares):
    groups, rows = gathered.shape[0], gathered.shape[1]
    size = count // groups
    sums, demand_sums = [], []
    for owner in range(groups):
        part = pl.ds(owner * size, size)
        scale = scale_ref[part, :] * lax.rsqrt(gathered[owner, pl.ds(0, size), :] + SMALL_EPS)
        new_scale[part, :] = scale
        scaled = scale * vector_ref[part, :]
        sums.append(fold_rows(scaled * scaled))
        demand_sums.append(gathered[owner, pl.ds(rows - 8, 8), :])
    squares[...] = tree_sum(sums)
    demand_squares[...] = tree_sum(demand_sums)


def norm_ratio(cost_squares, demand_squares):
    cost_total = jnp.sum(cost_squares[...], keepdims=True)
    demand_total = jnp.sum(demand_squares[...], keepdims=True)
    return jnp.sqrt(cost_total + SMALL_EPS) / jnp.sqrt(demand_total + SMALL_EPS)


def forward_kernel(count, first, last, rows_ref, cols_ref, blocks, product_ref, *refs):
    scale_ref, cost_ref, low_ref, high_ref, kind_ref, primal_ref = refs[:6]
    cost_squares, demand_squares, primal_out = refs[6:9]
    row_out, (shifted, row_acc) = refs[9:11], refs[11:]
    across = row_mask()
    groups = product_ref.shape[0]
    size = count // groups
    row_acc[...] = jnp.zeros_like(row_acc)
    primal_step = STEP_SCALE / norm_ratio(cost_squares, demand_squares)
    for owner in range(groups):
        part = pl.ds(owner * size, size)
        product = product_ref[owner, pl.ds(size if first else 0, size), :]
        scale = scale_ref[part, :]
        inverse = 1.0 / scale
        primal = primal_ref[part, :]
        if first:
            primal = primal * inverse
        gradient = scale * product
        moved = primal - primal_step * (scale * cost_ref[part, :] - gradient)
        kind = kind_ref[part, :]
        moved = jnp.where(
            (kind == 1) | (kind == 3), jnp.maximum(moved, low_ref[part, :] * inverse), moved
        )
        moved = jnp.where(
            (kind == 2) | (kind == 3), jnp.minimum(moved, high_ref[part, :] * inverse), moved
        )
        shifted[part, :] = scale * (2.0 * moved - primal)
        primal_out[part, :] = scale * moved if last else moved

    def visit(row, col, block_ref):
        return forward_term(shifted, col, block_ref)

    def finish(row, col, term):
        add_row(row_acc, row_place(row, count, across), term, jnp.add)

    for_slots(PRODUCT_GROUP, rows_ref, cols_ref, blocks, visit, finish)
    store_pieces(row_acc, row_out, count)


def next_dual(first, image, inside, scale, demand, dual, dual_step):
    if first:
        dual = dual / scale
    row_image = scale * image[inside, :]
    return jnp.maximum(dual + dual_step * (scale * demand - row_image), 0.0)


def transposed_kernel(count, first, rows_ref, cols_ref, blocks, *refs):
    image, refs = refs[:2], refs[2:]
    scale_ref, demand_ref, dual_ref, cost_squares, demand_squares, dual_out = refs[:6]
    product_out, weights, product_acc = refs[6:]
    across = row_mask()
    size = count // CHUNKS
    product_acc[...] = jnp.zeros_like(product_acc)
    dual_step = STEP_SCALE * norm_ratio(cost_squares, demand_squares)
    for place in range(CHUNKS):
        part = chunk_rows(place ^ across, size)
        piece, inside = piece_chunk(image, place, size)
        scale = scale_ref[part, :]
        dual = next_dual(
            first, piece, inside, scale, demand_ref[part, :], dual_ref[part, :], dual_step
        )
        dual_out[part, :] = dual
        weights[part, :] = scale * dual

    def visit(row, col, block_ref):
        return transposed_term(weights, row, block_ref)

    def finish(row, col, term):
        add_row(product_acc, col_place(col, count), term, jnp.add)

    for_slots(PRODUCT_GROUP, rows_ref, cols_ref, blocks, visit, finish)
    store_pieces(product_acc, (product_out,), count)


def last_dual_kernel(count, first, *refs):
    image, refs = refs[:2], refs[2:]
    scale_ref, demand_ref, dual_ref, cost_squares, demand_squares, dual_out = refs
    across = row_mask()
    size = count // CHUNKS
    dual_step = STEP_SCALE * norm_ratio(cost_squares, demand_squares)
    for place in range(CHUNKS):
        part = chunk_rows(place ^ across, size)
        piece, inside = piece_chunk(image, place, size)
        scale = scale_ref[part, :]
        dual = next_dual(
            first, piece, inside, scale, demand_ref[part, :], dual_ref[part, :], dual_step
        )
        dual_out[part, :] = scale * dual


def vectors(*row_counts):
    return [jax.ShapeDtypeStruct((rows, 128), jnp.float32) for rows in row_counts]


def call_plain(kernel, operands, out_shape):
    return pl.pallas_call(
        kernel,
        out_shape=out_shape,
        in_specs=[pl.BlockSpec(memory_space=pltpu.VMEM)] * len(operands),
        out_specs=[pl.BlockSpec(memory_space=pltpu.VMEM)] * len(out_shape),
        compiler_params=pltpu.CompilerParams(vmem_limit_bytes=SMALL_VMEM),
    )(*operands)


def call_blocks(kernel, slots, operands, out_shape, scratch, stream_group=None):
    row_ids, col_ids, values = slots
    count, width = values.shape[0], values.shape[1]
    scratch_shapes = [pltpu.VMEM((rows, width), jnp.float32) for rows in scratch]
    if stream_group:
        scratch_shapes = [
            pltpu.VMEM(values.shape, values.dtype),
            pltpu.SemaphoreType.DMA((count // stream_group,)),
        ] + scratch_shapes
    return pl.pallas_call(
        kernel,
        out_shape=out_shape,
        in_specs=[pl.BlockSpec(memory_space=pltpu.SMEM)] * 2
        + [pl.BlockSpec(memory_space=pl.ANY if stream_group else pltpu.VMEM)]
        + [pl.BlockSpec(memory_space=pltpu.VMEM)] * len(operands),
        out_specs=[pl.BlockSpec(memory_space=pltpu.VMEM)] * len(out_shape),
        scratch_shapes=scratch_shapes,
        compiler_params=pltpu.CompilerParams(
            vmem_limit_bytes=STREAM_VMEM if stream_group else RESIDENT_VMEM
        ),
        cost_estimate=pl.CostEstimate(
            flops=2 * values.size, bytes_accessed=2 * values.size, transcendentals=0
        ),
    )(row_ids, col_ids, values, *operands)


def swap(vector, axis, size, bit):
    return lax.ppermute(vector, axis, [(i, i ^ bit) for i in range(size)])


def reduce_rows(pieces, groups, combine):
    near, far = pieces
    near = combine(near, swap(far, "col", groups, ROW_HALVING))
    bit = 1
    while bit < groups:
        if bit != ROW_HALVING:
            near = combine(near, swap(near, "col", groups, bit))
        bit *= 2
    return [near, swap(near, "col", groups, ROW_HALVING)]


def scatter_cols(vector, combine):
    parts = lax.all_to_all(vector, "row", 0, 0)
    shares = [parts[source] for source in range(parts.shape[0])]
    while len(shares) > 1:
        shares = [combine(shares[i], shares[i + 1]) for i in range(0, len(shares), 2)]
    return shares[0]


def gather_cols(share, groups):
    return lax.all_to_all(jnp.broadcast_to(share, (groups,) + share.shape), "row", 0, 0)


def sum_cols(vector, groups):
    bit = 1
    while bit < groups:
        vector = vector + swap(vector, "col", groups, bit)
        bit *= 2
    return vector


def per_device(
    row_groups,
    col_groups,
    block_values,
    block_rows,
    block_cols,
    cost_vec,
    demand,
    lower,
    upper,
    bound_kind,
    primal_start,
    dual_start,
):
    values = block_values[0, 0]
    width = values.shape[1]
    slots = (block_rows[0, 0], block_cols[0, 0], values)
    row_length, col_length = demand.shape[0], cost_vec.shape[0]
    cost_vec, demand, lower, upper, bound_kind, primal_start, dual_start = [
        v.reshape(-1, width)
        for v in (cost_vec, demand, lower, upper, bound_kind, primal_start, dual_start)
    ]
    count = demand.shape[0]
    half, share, spare = count // 2, count // row_groups, count + 8
    row_pieces = vectors(half, half)
    whole = vectors(count)
    squares = vectors(8)
    shares = (row_groups, share, width)

    def over_col(pieces, combine):
        return reduce_rows(pieces, col_groups, combine)

    near, far, col_terms = call_blocks(
        functools.partial(first_pass_kernel, count),
        slots,
        [dual_start],
        row_pieces + [jax.ShapeDtypeStruct((row_groups, 2 * share, width), jnp.float32)],
        [spare] * 3,
        PEAK_GROUP,
    )
    row_peaks = over_col([near, far], jnp.maximum)
    is_peak = lax.broadcasted_iota(jnp.int32, (2 * share, width), 0) < share
    col_terms = scatter_cols(col_terms, lambda a, b: jnp.where(is_peak, jnp.maximum(a, b), a + b))
    product = col_terms[share:]
    col_peaks = gather_cols(col_terms[:share], row_groups).reshape(count, width)
    near, far, col_peaks, row_scale, col_scale = call_blocks(
        functools.partial(second_pass_kernel, count),
        slots,
        row_peaks + [col_peaks],
        row_pieces + whole * 3,
        [spare] * 2,
    )
    row_peaks = over_col([near, far], jnp.maximum)
    row_scale, demand_squares = call_plain(
        functools.partial(row_scale_kernel, count),
        row_peaks + [row_scale, demand],
        whole + squares,
    )
    col_peaks = scatter_cols(col_peaks.reshape(shares), jnp.maximum)
    gathered = gather_cols(
        jnp.concatenate([col_peaks, product, demand_squares], axis=0), row_groups
    )
    col_scale, cost_squares, demand_squares = call_plain(
        functools.partial(col_scale_kernel, count),
        [gathered, col_scale, cost_vec],
        whole + squares + squares,
    )
    norms = [sum_cols(cost_squares, col_groups), demand_squares]

    def forward(first, last, product, primal):
        out = call_blocks(
            functools.partial(forward_kernel, count, first, last),
            slots,
            [product, col_scale, cost_vec, lower, upper, bound_kind, primal] + norms,
            whole + row_pieces,
            [count, spare],
        )
        return out[0], over_col(out[1:], jnp.add)

    primal, image = forward(True, False, gathered, primal_start)
    dual, product = call_blocks(
        functools.partial(transposed_kernel, count, True),
        slots,
        image + [row_scale, demand, dual_start] + norms,
        whole + whole,
        [count, spare],
    )
    product = gather_cols(scatter_cols(product.reshape(shares), jnp.add), row_groups)
    primal, image = forward(False, True, product, primal)
    (dual,) = call_plain(
        functools.partial(last_dual_kernel, count, False),
        image + [row_scale, demand, dual] + norms,
        whole,
    )
    return primal.reshape(col_length), dual.reshape(row_length)


def solution(mesh):
    def body(*args):
        return per_device(mesh.shape["row"], mesh.shape["col"], *args)

    return jax.shard_map(
        body,
        mesh=mesh,
        in_specs=(
            P("row", "col", None, None, None),
            P("row", "col", None),
            P("row", "col", None),
            P("col"),
            P("row"),
            P("col"),
            P("col"),
            P("col"),
            P("col"),
            P("row"),
        ),
        out_specs=(P("col"), P("row")),
        check_vma=False,
    )
```

```python
import functools

import jax
import jax.numpy as jnp
from jax import lax
from jax.experimental import pallas as pl
from jax.experimental.pallas import tpu as pltpu
from jax.sharding import PartitionSpec as P

SMALL_EPS = 1e-06
STEP_SCALE = 0.3

CHUNKS = 8
PRODUCT_GROUP = 32
PEAK_GROUP = 16
ROW_HALVING = 1
QUARTERS = 4
BLOCK_VMEM = 57 * 1024 * 1024
SMALL_VMEM = 8 * 1024 * 1024


def bit_of(index, bit):
    return jnp.where((index & bit) != 0, 1, 0)


def row_mask():
    return bit_of(lax.axis_index("col"), ROW_HALVING) * (CHUNKS // 2)


def col_mask():
    return (lax.axis_index("row") & (QUARTERS - 1)) * (CHUNKS // QUARTERS)


def col_place(tile, count, mask):
    return jnp.where(tile < 0, count, tile ^ (mask * (count // CHUNKS)))


def row_place(tile, count, mask):
    return jnp.where(tile < 0, count, tile ^ (mask * (count // CHUNKS)))


def chunk_rows(chunk, size):
    return pl.ds(pl.multiple_of(chunk * size, size), size)


def piece_chunk(pieces, place, size):
    per_piece = CHUNKS // len(pieces)
    start = (place % per_piece) * size
    return pieces[place // per_piece], pl.ds(start, size)


def store_pieces(acc, pieces, count):
    size = count // len(pieces)
    for index, piece in enumerate(pieces):
        piece[...] = acc[pl.ds(index * size, size), :]


def add_row(acc, place, term, combine):
    acc[pl.ds(place, 1), :] = combine(acc[pl.ds(place, 1), :], term)


def one_row(ref, tile):
    return ref[pl.ds(jnp.maximum(tile, 0), 1), :]


def tree_sum(parts):
    while len(parts) > 1:
        parts = [parts[i] + parts[i + 1] for i in range(0, len(parts), 2)]
    return parts[0]


def fold_rows(values):
    return jnp.sum(values.reshape(-1, 8, values.shape[-1]), axis=0)


def block_copy(group, index, values_ref, blocks, arrived):
    part = pl.ds(pl.multiple_of(index * group, group), group)
    return pltpu.make_async_copy(values_ref.at[part], blocks.at[part], arrived.at[index])


def start_blocks(group, values_ref, blocks, arrived):
    for index in range(values_ref.shape[0] // group):
        block_copy(group, index, values_ref, blocks, arrived).start()


def for_slots(group, rows_ref, cols_ref, values_ref, blocks, arrived, visit, finish, after=None):
    def step(index, carry):
        block_copy(group, index, values_ref, blocks, arrived).wait()
        found = []
        for inner in range(group):
            slot = index * group + inner
            row, col = rows_ref[slot], cols_ref[slot]
            found.append((row, col, visit(row, col, slot)))
        for row, col, terms in found:
            finish(row, col, terms)
        if after is not None:
            after(index)
        return carry

    lax.fori_loop(0, blocks.shape[0] // group, step, 0)


def product_term(vector_ref, tile, block):
    vector = one_row(vector_ref, tile).astype(jnp.bfloat16)
    return jnp.dot(vector, block, preferred_element_type=jnp.float32)


def row_max(values):
    return jnp.max(values, axis=0, keepdims=True)


def packed_max(values):
    folded = jnp.max(values.reshape(-1, 16, values.shape[-1]), axis=0)
    return row_max(folded.astype(jnp.float32))


def first_pass_kernel(count, rows_ref, cols_ref, values_ref, dual_ref, *refs):
    row_out, col_out, product_out, turned_out = refs[:2], refs[2:6], refs[6:10], refs[10]
    blocks, arrived, turned, written, row_acc, col_acc, product_acc = refs[11:]
    mask, across = col_mask(), row_mask()
    start_blocks(PEAK_GROUP, values_ref, blocks, arrived)
    for acc in (row_acc, col_acc, product_acc):
        acc[...] = jnp.zeros_like(acc)

    def visit(row, col, slot):
        block = blocks[slot]
        flipped = block.T
        turned[slot] = flipped
        return (
            packed_max(jnp.abs(flipped)),
            packed_max(jnp.abs(block)),
            product_term(dual_ref, row, block),
        )

    def finish(row, col, terms):
        at_row, at_col = row_place(row, count, across), col_place(col, count, mask)
        add_row(row_acc, at_row, terms[0], jnp.maximum)
        add_row(col_acc, at_col, terms[1], jnp.maximum)
        add_row(product_acc, at_col, terms[2], jnp.add)

    def after(index):
        block_copy(PEAK_GROUP, index, turned, turned_out, written).start()

    for_slots(
        PEAK_GROUP, rows_ref, cols_ref, values_ref, blocks, arrived, visit, finish, after
    )
    store_pieces(row_acc, row_out, count)
    store_pieces(col_acc, col_out, count)
    store_pieces(product_acc, product_out, count)
    for index in range(values_ref.shape[0] // PEAK_GROUP):
        block_copy(PEAK_GROUP, index, turned, turned_out, written).wait()


def second_pass_kernel(count, rows_ref, cols_ref, values_ref, *refs):
    row_in, col_in, row_out, col_out = refs[:2], refs[2:6], refs[6:8], refs[8:12]
    row_scale, col_scale, blocks, arrived, row_acc, col_acc = refs[12:]
    mask, across = col_mask(), row_mask()
    size = count // CHUNKS
    start_blocks(PEAK_GROUP, values_ref, blocks, arrived)
    row_acc[...] = jnp.zeros_like(row_acc)
    col_acc[...] = jnp.zeros_like(col_acc)
    for place in range(CHUNKS):
        piece, part = piece_chunk(row_in, place, size)
        row_scale[chunk_rows(place ^ across, size), :] = lax.rsqrt(piece[part, :] + SMALL_EPS)
        piece, part = piece_chunk(col_in, place, size)
        col_scale[chunk_rows(place ^ mask, size), :] = lax.rsqrt(piece[part, :] + SMALL_EPS)
    width = blocks.shape[-1]
    square = (width, width)
    diagonal = lax.broadcasted_iota(jnp.int32, square, 0) == lax.broadcasted_iota(
        jnp.int32, square, 1
    )
    diagonal = diagonal.astype(jnp.float32).astype(jnp.bfloat16)

    def visit(row, col, slot):
        sizes = jnp.abs(blocks[slot])
        by_col = sizes * one_row(col_scale, col).astype(jnp.bfloat16)
        scale = one_row(row_scale, row)
        high = scale.astype(jnp.bfloat16)
        low = (scale - high.astype(jnp.float32)).astype(jnp.bfloat16)
        by_row = jnp.dot(
            jnp.concatenate([diagonal * high, diagonal * low], axis=1),
            jnp.concatenate([sizes, sizes], axis=0),
            preferred_element_type=jnp.float32,
        )
        return packed_max(by_col.T), row_max(by_row)

    def finish(row, col, terms):
        add_row(row_acc, row_place(row, count, across), terms[0], jnp.maximum)
        add_row(col_acc, col_place(col, count, mask), terms[1], jnp.maximum)

    for_slots(PEAK_GROUP, rows_ref, cols_ref, values_ref, blocks, arrived, visit, finish)
    for place in range(CHUNKS):
        part = pl.ds(place * size, size)
        piece, inside = piece_chunk(row_out, place, size)
        piece[inside, :] = row_acc[part, :] * row_scale[chunk_rows(place ^ across, size), :]
        piece, inside = piece_chunk(col_out, place, size)
        piece[inside, :] = col_acc[part, :] * col_scale[chunk_rows(place ^ mask, size), :]


def row_scale_kernel(count, near, far, scale_ref, vector_ref, new_scale, squares):
    across = row_mask()
    size = count // CHUNKS
    sums = []
    for place in range(CHUNKS):
        part = chunk_rows(place ^ across, size)
        piece, inside = piece_chunk((near, far), place, size)
        scale = scale_ref[part, :] * lax.rsqrt(piece[inside, :] + SMALL_EPS)
        new_scale[part, :] = scale
        scaled = scale * vector_ref[part, :]
        sums.append(fold_rows(scaled * scaled))
    half = CHUNKS // 2
    squares[...] = tree_sum(sums[:half]) + tree_sum(sums[half:])


def col_scale_kernel(count, *refs):
    pieces, (scale_ref, vector_ref, new_scale, squares, demand_squares) = refs[:4], refs[4:]
    mask = col_mask()
    size = count // CHUNKS
    sums = []
    for place in range(CHUNKS):
        part = chunk_rows(place ^ mask, size)
        piece, inside = piece_chunk(pieces, place, size)
        scale = scale_ref[part, :] * lax.rsqrt(piece[inside, :] + SMALL_EPS)
        new_scale[part, :] = scale
        scaled = scale * vector_ref[part, :]
        sums.append(fold_rows(scaled * scaled))
    squares[...] = tree_sum(sums)
    tail = pl.ds(count // QUARTERS, 8)
    demand_squares[...] = tree_sum([piece[tail, :] for piece in pieces])


def norm_ratio(cost_squares, demand_squares):
    cost_total = jnp.sum(cost_squares[...], keepdims=True)
    demand_total = jnp.sum(demand_squares[...], keepdims=True)
    return jnp.sqrt(cost_total + SMALL_EPS) / jnp.sqrt(demand_total + SMALL_EPS)


def forward_kernel(count, first, last, rows_ref, cols_ref, turned_ref, *refs):
    product, refs = refs[:4], refs[4:]
    scale_ref, cost_ref, low_ref, high_ref, kind_ref, primal_ref = refs[:6]
    cost_squares, demand_squares, primal_out = refs[6:9]
    row_out, (blocks, arrived, shifted, row_acc) = refs[9:11], refs[11:]
    mask, across = col_mask(), row_mask()
    size = count // CHUNKS
    start_blocks(PRODUCT_GROUP, turned_ref, blocks, arrived)
    row_acc[...] = jnp.zeros_like(row_acc)
    primal_step = STEP_SCALE / norm_ratio(cost_squares, demand_squares)
    for place in range(CHUNKS):
        part = chunk_rows(place ^ mask, size)
        piece, inside = piece_chunk(product, place, size)
        scale = scale_ref[part, :]
        inverse = 1.0 / scale
        primal = primal_ref[part, :]
        if first:
            primal = primal * inverse
        gradient = scale * piece[inside, :]
        moved = primal - primal_step * (scale * cost_ref[part, :] - gradient)
        kind = kind_ref[part, :]
        moved = jnp.where(
            (kind == 1) | (kind == 3), jnp.maximum(moved, low_ref[part, :] * inverse), moved
        )
        moved = jnp.where(
            (kind == 2) | (kind == 3), jnp.minimum(moved, high_ref[part, :] * inverse), moved
        )
        shifted[part, :] = scale * (2.0 * moved - primal)
        primal_out[part, :] = scale * moved if last else moved

    def visit(row, col, slot):
        return product_term(shifted, col, blocks[slot])

    def finish(row, col, term):
        add_row(row_acc, row_place(row, count, across), term, jnp.add)

    for_slots(PRODUCT_GROUP, rows_ref, cols_ref, turned_ref, blocks, arrived, visit, finish)
    store_pieces(row_acc, row_out, count)


def next_dual(first, image, inside, scale, demand, dual, dual_step):
    if first:
        dual = dual / scale
    row_image = scale * image[inside, :]
    return jnp.maximum(dual + dual_step * (scale * demand - row_image), 0.0)


def transposed_kernel(count, first, rows_ref, cols_ref, values_ref, *refs):
    image, refs = refs[:2], refs[2:]
    scale_ref, demand_ref, dual_ref, cost_squares, demand_squares, dual_out = refs[:6]
    product_out, (blocks, arrived, weights, product_acc) = refs[6:10], refs[10:]
    mask, across = col_mask(), row_mask()
    size = count // CHUNKS
    start_blocks(PRODUCT_GROUP, values_ref, blocks, arrived)
    product_acc[...] = jnp.zeros_like(product_acc)
    dual_step = STEP_SCALE * norm_ratio(cost_squares, demand_squares)
    for place in range(CHUNKS):
        part = chunk_rows(place ^ across, size)
        piece, inside = piece_chunk(image, place, size)
        scale = scale_ref[part, :]
        dual = next_dual(
            first, piece, inside, scale, demand_ref[part, :], dual_ref[part, :], dual_step
        )
        dual_out[part, :] = dual
        weights[part, :] = scale * dual

    def visit(row, col, slot):
        return product_term(weights, row, blocks[slot])

    def finish(row, col, term):
        add_row(product_acc, col_place(col, count, mask), term, jnp.add)

    for_slots(PRODUCT_GROUP, rows_ref, cols_ref, values_ref, blocks, arrived, visit, finish)
    store_pieces(product_acc, product_out, count)


def last_dual_kernel(count, first, *refs):
    image, refs = refs[:2], refs[2:]
    scale_ref, demand_ref, dual_ref, cost_squares, demand_squares, dual_out = refs
    across = row_mask()
    size = count // CHUNKS
    dual_step = STEP_SCALE * norm_ratio(cost_squares, demand_squares)
    for place in range(CHUNKS):
        part = chunk_rows(place ^ across, size)
        piece, inside = piece_chunk(image, place, size)
        scale = scale_ref[part, :]
        dual = next_dual(
            first, piece, inside, scale, demand_ref[part, :], dual_ref[part, :], dual_step
        )
        dual_out[part, :] = scale * dual


def vectors(*row_counts):
    return [jax.ShapeDtypeStruct((rows, 128), jnp.float32) for rows in row_counts]


def call_plain(kernel, operands, out_shape):
    return pl.pallas_call(
        kernel,
        out_shape=out_shape,
        in_specs=[pl.BlockSpec(memory_space=pltpu.VMEM)] * len(operands),
        out_specs=[pl.BlockSpec(memory_space=pltpu.VMEM)] * len(out_shape),
        compiler_params=pltpu.CompilerParams(vmem_limit_bytes=SMALL_VMEM),
    )(*operands)


def call_blocks(kernel, group, slots, operands, out_shape, scratch, turned=False):
    row_ids, col_ids, values = slots
    count, width = values.shape[0], values.shape[1]
    scratch_shapes = [
        pltpu.VMEM(values.shape, values.dtype),
        pltpu.SemaphoreType.DMA((count // group,)),
    ]
    out_specs = [pl.BlockSpec(memory_space=pltpu.VMEM)] * len(out_shape)
    if turned:
        out_shape = out_shape + [jax.ShapeDtypeStruct(values.shape, values.dtype)]
        out_specs = out_specs + [pl.BlockSpec(memory_space=pl.ANY)]
        scratch_shapes = scratch_shapes * 2
    return pl.pallas_call(
        kernel,
        out_shape=out_shape,
        in_specs=[pl.BlockSpec(memory_space=pltpu.SMEM)] * 2
        + [pl.BlockSpec(memory_space=pl.ANY)]
        + [pl.BlockSpec(memory_space=pltpu.VMEM)] * len(operands),
        out_specs=out_specs,
        scratch_shapes=scratch_shapes
        + [pltpu.VMEM((rows, width), jnp.float32) for rows in scratch],
        compiler_params=pltpu.CompilerParams(vmem_limit_bytes=BLOCK_VMEM),
        cost_estimate=pl.CostEstimate(
            flops=2 * values.size, bytes_accessed=2 * values.size, transcendentals=0
        ),
    )(row_ids, col_ids, values, *operands)


def swap(vector, axis, size, bit):
    return lax.ppermute(vector, axis, [(i, i ^ bit) for i in range(size)])


def reduce_rows(pieces, groups, combine):
    near, far = pieces
    near = combine(near, swap(far, "col", groups, ROW_HALVING))
    bit = 1
    while bit < groups:
        if bit != ROW_HALVING:
            near = combine(near, swap(near, "col", groups, bit))
        bit *= 2
    return [near, swap(near, "col", groups, ROW_HALVING)]


def scatter_cols(pieces, groups, combine):
    got = {
        mask: swap(pieces[mask], "row", groups, mask) for mask in (QUARTERS - 1, 1, 2)
    }
    return combine(combine(pieces[0], got[1]), combine(got[2], got[3]))


def exchange_cols(piece, groups, combine):
    bit = QUARTERS
    while bit < groups:
        piece = combine(piece, swap(piece, "row", groups, bit))
        bit *= 2
    return piece


def gather_cols(piece, groups):
    got = {mask: swap(piece, "row", groups, mask) for mask in (QUARTERS - 1, 1, 2)}
    return [piece] + [got[mask] for mask in range(1, QUARTERS)]


def sum_cols(vector, groups):
    bit = 1
    while bit < groups:
        vector = vector + swap(vector, "col", groups, bit)
        bit *= 2
    return vector


def per_device(
    row_groups,
    col_groups,
    block_values,
    block_rows,
    block_cols,
    cost_vec,
    demand,
    lower,
    upper,
    bound_kind,
    primal_start,
    dual_start,
):
    values = block_values[0, 0]
    width = values.shape[1]
    slots = (block_rows[0, 0], block_cols[0, 0], values)
    row_length, col_length = demand.shape[0], cost_vec.shape[0]
    cost_vec, demand, lower, upper, bound_kind, primal_start, dual_start = [
        v.reshape(-1, width)
        for v in (cost_vec, demand, lower, upper, bound_kind, primal_start, dual_start)
    ]
    count = demand.shape[0]
    half, quarter, spare = count // 2, count // QUARTERS, count + 8
    row_pieces, col_pieces = vectors(half, half), vectors(*[quarter] * QUARTERS)
    whole = vectors(count)
    squares = vectors(8)

    def over_col(pieces, combine):
        return reduce_rows(pieces, col_groups, combine)

    def over_row(pieces, combine):
        share = scatter_cols(pieces, row_groups, combine)
        return gather_cols(exchange_cols(share, row_groups, combine), row_groups)

    out = call_blocks(
        functools.partial(first_pass_kernel, count),
        PEAK_GROUP,
        slots,
        [dual_start],
        row_pieces + col_pieces + col_pieces,
        [spare] * 3,
        turned=True,
    )
    turned_slots = slots[:2] + (out[10],)
    row_peaks = over_col(out[:2], jnp.maximum)
    col_peaks = over_row(out[2:6], jnp.maximum)
    product = over_row(out[6:10], jnp.add)
    out = call_blocks(
        functools.partial(second_pass_kernel, count),
        PEAK_GROUP,
        slots,
        row_peaks + col_peaks,
        row_pieces + col_pieces + whole + whole,
        [spare] * 2,
    )
    row_scale, col_scale = out[6:]
    row_peaks = over_col(out[:2], jnp.maximum)
    row_scale, demand_squares = call_plain(
        functools.partial(row_scale_kernel, count),
        row_peaks + [row_scale, demand],
        whole + squares,
    )
    col_peaks = scatter_cols(out[2:6], row_groups, jnp.maximum)
    is_peak = lax.broadcasted_iota(jnp.int32, (quarter + 8, width), 0) < quarter
    col_peaks = exchange_cols(
        jnp.concatenate([col_peaks, demand_squares], axis=0),
        row_groups,
        lambda a, b: jnp.where(is_peak, jnp.maximum(a, b), a + b),
    )
    col_scale, cost_squares, demand_squares = call_plain(
        functools.partial(col_scale_kernel, count),
        gather_cols(col_peaks, row_groups) + [col_scale, cost_vec],
        whole + squares + squares,
    )
    norms = [sum_cols(cost_squares, col_groups), demand_squares]

    def forward(first, last, product, primal):
        out = call_blocks(
            functools.partial(forward_kernel, count, first, last),
            PRODUCT_GROUP,
            turned_slots,
            product + [col_scale, cost_vec, lower, upper, bound_kind, primal] + norms,
            whole + row_pieces,
            [count, spare],
        )
        return out[0], over_col(out[1:], jnp.add)

    primal, image = forward(True, False, product, primal_start)
    out = call_blocks(
        functools.partial(transposed_kernel, count, True),
        PRODUCT_GROUP,
        slots,
        image + [row_scale, demand, dual_start] + norms,
        whole + col_pieces,
        [count, spare],
    )
    dual, product = out[0], over_row(out[1:], jnp.add)
    primal, image = forward(False, True, product, primal)
    (dual,) = call_plain(
        functools.partial(last_dual_kernel, count, False),
        image + [row_scale, demand, dual] + norms,
        whole,
    )
    return primal.reshape(col_length), dual.reshape(row_length)


def solution(mesh):
    def body(*args):
        return per_device(mesh.shape["row"], mesh.shape["col"], *args)

    return jax.shard_map(
        body,
        mesh=mesh,
        in_specs=(
            P("row", "col", None, None, None),
            P("row", "col", None),
            P("row", "col", None),
            P("col"),
            P("row"),
            P("col"),
            P("col"),
            P("col"),
            P("col"),
            P("row"),
        ),
        out_specs=(P("col"), P("row")),
        check_vma=False,
    )
```

```python
import functools

import jax
import jax.numpy as jnp
from jax import lax
from jax.experimental import pallas as pl
from jax.experimental.pallas import tpu as pltpu
from jax.sharding import PartitionSpec as P

SMALL_EPS = 1e-06
STEP_SCALE = 0.3

CHUNKS = 8
GROUP = 32
ROW_HALVING = 1
QUARTERS = 4
FIRST_VMEM = 44 * 1024 * 1024
BLOCK_VMEM = 16 * 1024 * 1024
SMALL_VMEM = 8 * 1024 * 1024


def bit_of(index, bit):
    return jnp.where((index & bit) != 0, 1, 0)


def row_mask():
    return bit_of(lax.axis_index("col"), ROW_HALVING) * (CHUNKS // 2)


def col_mask():
    return (lax.axis_index("row") & (QUARTERS - 1)) * (CHUNKS // QUARTERS)


def col_place(tile, count, mask):
    return jnp.where(tile < 0, count, tile ^ (mask * (count // CHUNKS)))


def row_place(tile, count, mask):
    return jnp.where(tile < 0, count, tile ^ (mask * (count // CHUNKS)))


def chunk_rows(chunk, size):
    return pl.ds(pl.multiple_of(chunk * size, size), size)


def piece_chunk(pieces, place, size, offset=0):
    per_piece = CHUNKS // len(pieces)
    start = offset + (place % per_piece) * size
    return pieces[place // per_piece], pl.ds(start, size)


def store_pieces(acc, pieces, count):
    size = count // len(pieces)
    for index, piece in enumerate(pieces):
        piece[...] = acc[pl.ds(index * size, size), :]


def add_row(acc, place, term, combine):
    acc[pl.ds(place, 1), :] = combine(acc[pl.ds(place, 1), :], term)


def one_row(ref, tile):
    return ref[pl.ds(jnp.maximum(tile, 0), 1), :]


def tree_sum(parts):
    while len(parts) > 1:
        parts = [parts[i] + parts[i + 1] for i in range(0, len(parts), 2)]
    return parts[0]


def fold_rows(values):
    return jnp.sum(values.reshape(-1, 8, values.shape[-1]), axis=0)


def block_copy(index, values_ref, blocks, arrived):
    part = pl.ds(pl.multiple_of(index * GROUP, GROUP), GROUP)
    return pltpu.make_async_copy(values_ref.at[part], blocks.at[part], arrived.at[index])


def for_slots(rows_ref, cols_ref, visit, finish, before=None, after=None):
    def step(index, carry):
        if before is not None:
            before(index)
        found = []
        for inner in range(GROUP):
            slot = index * GROUP + inner
            row, col = rows_ref[slot], cols_ref[slot]
            found.append((row, col, visit(row, col, slot)))
        for row, col, terms in found:
            finish(row, col, terms)
        if after is not None:
            after(index)
        return carry

    lax.fori_loop(0, rows_ref.shape[0] // GROUP, step, 0)


def product_term(vector_ref, tile, block):
    vector = one_row(vector_ref, tile).astype(jnp.bfloat16)
    return jnp.dot(vector, block, preferred_element_type=jnp.float32)


def row_max(values):
    return jnp.max(values, axis=0, keepdims=True)


def packed_max(values):
    folded = jnp.max(values.reshape(-1, 16, values.shape[-1]), axis=0)
    return row_max(folded.astype(jnp.float32))


def first_pass_kernel(count, rows_ref, cols_ref, values_ref, dual_ref, *refs):
    row_out, col_out, blocks, turned_out = refs[:2], refs[2:6], refs[6], refs[7]
    arrived, turned, written, row_acc, col_acc, product_acc = refs[8:]
    mask, across = col_mask(), row_mask()
    for index in range(values_ref.shape[0] // GROUP):
        block_copy(index, values_ref, blocks, arrived).start()
    for acc in (row_acc, col_acc, product_acc):
        acc[...] = jnp.zeros_like(acc)

    def visit(row, col, slot):
        block = blocks[slot]
        flipped = block.T
        turned[slot] = flipped
        return (
            packed_max(jnp.abs(flipped)),
            packed_max(jnp.abs(block)),
            product_term(dual_ref, row, block),
        )

    def finish(row, col, terms):
        at_row, at_col = row_place(row, count, across), col_place(col, count, mask)
        add_row(row_acc, at_row, terms[0], jnp.maximum)
        add_row(col_acc, at_col, terms[1], jnp.maximum)
        add_row(product_acc, at_col, terms[2], jnp.add)

    def before(index):
        block_copy(index, values_ref, blocks, arrived).wait()

    def after(index):
        block_copy(index, turned, turned_out, written).start()

    for_slots(rows_ref, cols_ref, visit, finish, before, after)
    store_pieces(row_acc, row_out, count)
    quarter = count // QUARTERS
    for index, piece in enumerate(col_out):
        part = pl.ds(index * quarter, quarter)
        piece[pl.ds(0, quarter), :] = col_acc[part, :]
        piece[pl.ds(quarter, quarter), :] = product_acc[part, :]
    for index in range(values_ref.shape[0] // GROUP):
        block_copy(index, turned, turned_out, written).wait()


def second_pass_kernel(count, rows_ref, cols_ref, blocks, *refs):
    row_in, col_in, row_out, col_out = refs[:2], refs[2:6], refs[6:8], refs[8:12]
    row_scale, col_scale, row_acc, col_acc = refs[12:]
    mask, across = col_mask(), row_mask()
    size = count // CHUNKS
    row_acc[...] = jnp.zeros_like(row_acc)
    col_acc[...] = jnp.zeros_like(col_acc)
    for place in range(CHUNKS):
        piece, part = piece_chunk(row_in, place, size)
        row_scale[chunk_rows(place ^ across, size), :] = lax.rsqrt(piece[part, :] + SMALL_EPS)
        piece, part = piece_chunk(col_in, place, size)
        col_scale[chunk_rows(place ^ mask, size), :] = lax.rsqrt(piece[part, :] + SMALL_EPS)
    width = blocks.shape[-1]
    square = (width, width)
    diagonal = lax.broadcasted_iota(jnp.int32, square, 0) == lax.broadcasted_iota(
        jnp.int32, square, 1
    )
    diagonal = diagonal.astype(jnp.float32).astype(jnp.bfloat16)

    def visit(row, col, slot):
        sizes = jnp.abs(blocks[slot])
        by_col = sizes.astype(jnp.float32) * one_row(col_scale, col)
        scale = one_row(row_scale, row)
        high = scale.astype(jnp.bfloat16)
        low = (scale - high.astype(jnp.float32)).astype(jnp.bfloat16)
        by_row = jnp.dot(
            jnp.concatenate([diagonal * high, diagonal * low], axis=1),
            jnp.concatenate([sizes, sizes], axis=0),
            preferred_element_type=jnp.float32,
        )
        return row_max(by_col.T), row_max(by_row)

    def finish(row, col, terms):
        add_row(row_acc, row_place(row, count, across), terms[0], jnp.maximum)
        add_row(col_acc, col_place(col, count, mask), terms[1], jnp.maximum)

    for_slots(rows_ref, cols_ref, visit, finish)
    for place in range(CHUNKS):
        part = pl.ds(place * size, size)
        piece, inside = piece_chunk(row_out, place, size)
        piece[inside, :] = row_acc[part, :] * row_scale[chunk_rows(place ^ across, size), :]
        piece, inside = piece_chunk(col_out, place, size)
        piece[inside, :] = col_acc[part, :] * col_scale[chunk_rows(place ^ mask, size), :]


def row_scale_kernel(count, near, far, scale_ref, vector_ref, new_scale, squares):
    across = row_mask()
    size = count // CHUNKS
    sums = []
    for place in range(CHUNKS):
        part = chunk_rows(place ^ across, size)
        piece, inside = piece_chunk((near, far), place, size)
        scale = scale_ref[part, :] * lax.rsqrt(piece[inside, :] + SMALL_EPS)
        new_scale[part, :] = scale
        scaled = scale * vector_ref[part, :]
        sums.append(fold_rows(scaled * scaled))
    half = CHUNKS // 2
    squares[...] = tree_sum(sums[:half]) + tree_sum(sums[half:])


def col_scale_kernel(count, *refs):
    pieces, (scale_ref, vector_ref, new_scale, squares, demand_squares) = refs[:4], refs[4:]
    mask = col_mask()
    size = count // CHUNKS
    sums = []
    for place in range(CHUNKS):
        part = chunk_rows(place ^ mask, size)
        piece, inside = piece_chunk(pieces, place, size)
        scale = scale_ref[part, :] * lax.rsqrt(piece[inside, :] + SMALL_EPS)
        new_scale[part, :] = scale
        scaled = scale * vector_ref[part, :]
        sums.append(fold_rows(scaled * scaled))
    squares[...] = tree_sum(sums)
    tail = pl.ds(pieces[0].shape[0] - 8, 8)
    demand_squares[...] = tree_sum([piece[tail, :] for piece in pieces])


def norm_ratio(cost_squares, demand_squares):
    cost_total = jnp.sum(cost_squares[...], keepdims=True)
    demand_total = jnp.sum(demand_squares[...], keepdims=True)
    return jnp.sqrt(cost_total + SMALL_EPS) / jnp.sqrt(demand_total + SMALL_EPS)


def forward_kernel(count, first, last, rows_ref, cols_ref, turned, *refs):
    product, refs = refs[:4], refs[4:]
    scale_ref, cost_ref, low_ref, high_ref, kind_ref, primal_ref = refs[:6]
    cost_squares, demand_squares, primal_out = refs[6:9]
    row_out, (shifted, row_acc) = refs[9:11], refs[11:]
    mask, across = col_mask(), row_mask()
    size = count // CHUNKS
    row_acc[...] = jnp.zeros_like(row_acc)
    primal_step = STEP_SCALE / norm_ratio(cost_squares, demand_squares)
    for place in range(CHUNKS):
        part = chunk_rows(place ^ mask, size)
        piece, inside = piece_chunk(product, place, size, count // QUARTERS if first else 0)
        scale = scale_ref[part, :]
        inverse = 1.0 / scale
        primal = primal_ref[part, :]
        if first:
            primal = primal * inverse
        gradient = scale * piece[inside, :]
        moved = primal - primal_step * (scale * cost_ref[part, :] - gradient)
        kind = kind_ref[part, :]
        moved = jnp.where(
            (kind == 1) | (kind == 3), jnp.maximum(moved, low_ref[part, :] * inverse), moved
        )
        moved = jnp.where(
            (kind == 2) | (kind == 3), jnp.minimum(moved, high_ref[part, :] * inverse), moved
        )
        shifted[part, :] = scale * (2.0 * moved - primal)
        primal_out[part, :] = scale * moved if last else moved

    def visit(row, col, slot):
        return product_term(shifted, col, turned[slot])

    def finish(row, col, term):
        add_row(row_acc, row_place(row, count, across), term, jnp.add)

    for_slots(rows_ref, cols_ref, visit, finish)
    store_pieces(row_acc, row_out, count)


def next_dual(first, image, inside, scale, demand, dual, dual_step):
    if first:
        dual = dual / scale
    row_image = scale * image[inside, :]
    return jnp.maximum(dual + dual_step * (scale * demand - row_image), 0.0)


def transposed_kernel(count, first, rows_ref, cols_ref, blocks, *refs):
    image, refs = refs[:2], refs[2:]
    scale_ref, demand_ref, dual_ref, cost_squares, demand_squares, dual_out = refs[:6]
    product_out, (weights, product_acc) = refs[6:10], refs[10:]
    mask, across = col_mask(), row_mask()
    size = count // CHUNKS
    product_acc[...] = jnp.zeros_like(product_acc)
    dual_step = STEP_SCALE * norm_ratio(cost_squares, demand_squares)
    for place in range(CHUNKS):
        part = chunk_rows(place ^ across, size)
        piece, inside = piece_chunk(image, place, size)
        scale = scale_ref[part, :]
        dual = next_dual(
            first, piece, inside, scale, demand_ref[part, :], dual_ref[part, :], dual_step
        )
        dual_out[part, :] = dual
        weights[part, :] = scale * dual

    def visit(row, col, slot):
        return product_term(weights, row, blocks[slot])

    def finish(row, col, term):
        add_row(product_acc, col_place(col, count, mask), term, jnp.add)

    for_slots(rows_ref, cols_ref, visit, finish)
    store_pieces(product_acc, product_out, count)


def last_dual_kernel(count, first, *refs):
    image, refs = refs[:2], refs[2:]
    scale_ref, demand_ref, dual_ref, cost_squares, demand_squares, dual_out = refs
    across = row_mask()
    size = count // CHUNKS
    dual_step = STEP_SCALE * norm_ratio(cost_squares, demand_squares)
    for place in range(CHUNKS):
        part = chunk_rows(place ^ across, size)
        piece, inside = piece_chunk(image, place, size)
        scale = scale_ref[part, :]
        dual = next_dual(
            first, piece, inside, scale, demand_ref[part, :], dual_ref[part, :], dual_step
        )
        dual_out[part, :] = scale * dual


def vectors(*row_counts):
    return [jax.ShapeDtypeStruct((rows, 128), jnp.float32) for rows in row_counts]


def call_plain(kernel, operands, out_shape):
    return pl.pallas_call(
        kernel,
        out_shape=out_shape,
        in_specs=[pl.BlockSpec(memory_space=pltpu.VMEM)] * len(operands),
        out_specs=[pl.BlockSpec(memory_space=pltpu.VMEM)] * len(out_shape),
        compiler_params=pltpu.CompilerParams(vmem_limit_bytes=SMALL_VMEM),
    )(*operands)


def call_blocks(kernel, row_ids, col_ids, values, operands, out_shape, scratch, first=False):
    width = values.shape[1]
    scratch_shapes = [pltpu.VMEM((rows, width), jnp.float32) for rows in scratch]
    out_specs = [pl.BlockSpec(memory_space=pltpu.VMEM)] * len(out_shape)
    if first:
        arrivals = pltpu.SemaphoreType.DMA((values.shape[0] // GROUP,))
        turned = pltpu.VMEM(values.shape, values.dtype)
        scratch_shapes = [arrivals, turned, arrivals] + scratch_shapes
        out_specs[-1] = pl.BlockSpec(memory_space=pl.ANY)
    return pl.pallas_call(
        kernel,
        out_shape=out_shape,
        in_specs=[pl.BlockSpec(memory_space=pltpu.SMEM)] * 2
        + [pl.BlockSpec(memory_space=pl.ANY if first else pltpu.VMEM)]
        + [pl.BlockSpec(memory_space=pltpu.VMEM)] * len(operands),
        out_specs=out_specs,
        scratch_shapes=scratch_shapes,
        compiler_params=pltpu.CompilerParams(
            vmem_limit_bytes=FIRST_VMEM if first else BLOCK_VMEM
        ),
        cost_estimate=pl.CostEstimate(
            flops=2 * values.size, bytes_accessed=2 * values.size, transcendentals=0
        ),
    )(row_ids, col_ids, values, *operands)


def swap(vector, axis, size, bit):
    return lax.ppermute(vector, axis, [(i, i ^ bit) for i in range(size)])


def reduce_rows(pieces, groups, combine):
    near, far = pieces
    near = combine(near, swap(far, "col", groups, ROW_HALVING))
    bit = 1
    while bit < groups:
        if bit != ROW_HALVING:
            near = combine(near, swap(near, "col", groups, bit))
        bit *= 2
    return [near, swap(near, "col", groups, ROW_HALVING)]


def scatter_cols(pieces, groups, combine):
    got = {
        mask: swap(pieces[mask], "row", groups, mask) for mask in (QUARTERS - 1, 1, 2)
    }
    return combine(combine(pieces[0], got[1]), combine(got[2], got[3]))


def exchange_cols(piece, groups, combine):
    bit = QUARTERS
    while bit < groups:
        piece = combine(piece, swap(piece, "row", groups, bit))
        bit *= 2
    return piece


def gather_cols(piece, groups):
    got = {mask: swap(piece, "row", groups, mask) for mask in (QUARTERS - 1, 1, 2)}
    return [piece] + [got[mask] for mask in range(1, QUARTERS)]


def sum_cols(vector, groups):
    bit = 1
    while bit < groups:
        vector = vector + swap(vector, "col", groups, bit)
        bit *= 2
    return vector


def per_device(
    row_groups,
    col_groups,
    block_values,
    block_rows,
    block_cols,
    cost_vec,
    demand,
    lower,
    upper,
    bound_kind,
    primal_start,
    dual_start,
):
    values = block_values[0, 0]
    width = values.shape[1]
    row_ids, col_ids = block_rows[0, 0], block_cols[0, 0]
    row_length, col_length = demand.shape[0], cost_vec.shape[0]
    cost_vec, demand, lower, upper, bound_kind, primal_start, dual_start = [
        v.reshape(-1, width)
        for v in (cost_vec, demand, lower, upper, bound_kind, primal_start, dual_start)
    ]
    count = demand.shape[0]
    half, quarter, spare = count // 2, count // QUARTERS, count + 8
    row_pieces, col_pieces = vectors(half, half), vectors(*[quarter] * QUARTERS)
    whole = vectors(count)
    squares = vectors(8)

    def over_col(pieces, combine):
        return reduce_rows(pieces, col_groups, combine)

    def over_row(pieces, combine):
        share = scatter_cols(pieces, row_groups, combine)
        return gather_cols(exchange_cols(share, row_groups, combine), row_groups)

    tile = lax.broadcasted_iota(jnp.int32, (2 * quarter, width), 0)

    def mixed(a, b):
        return jnp.where(tile[: a.shape[0]] < quarter, jnp.maximum(a, b), a + b)

    out = call_blocks(
        functools.partial(first_pass_kernel, count),
        row_ids,
        col_ids,
        values,
        [dual_start],
        row_pieces
        + vectors(*[2 * quarter] * QUARTERS)
        + [jax.ShapeDtypeStruct(values.shape, values.dtype)] * 2,
        [spare] * 3,
        first=True,
    )
    blocks, turned = out[6:]
    row_peaks = over_col(out[:2], jnp.maximum)
    share = exchange_cols(scatter_cols(out[2:6], row_groups, mixed), row_groups, mixed)
    product = share[quarter:]
    col_peaks = gather_cols(share[:quarter], row_groups)
    out = call_blocks(
        functools.partial(second_pass_kernel, count),
        row_ids,
        col_ids,
        blocks,
        row_peaks + col_peaks,
        row_pieces + col_pieces + whole + whole,
        [spare] * 2,
    )
    row_scale, col_scale = out[6:]
    row_peaks = over_col(out[:2], jnp.maximum)
    row_scale, demand_squares = call_plain(
        functools.partial(row_scale_kernel, count),
        row_peaks + [row_scale, demand],
        whole + squares,
    )
    col_peaks = scatter_cols(out[2:6], row_groups, jnp.maximum)
    share = exchange_cols(
        jnp.concatenate([col_peaks, demand_squares], axis=0), row_groups, mixed
    )
    gathered = gather_cols(
        jnp.concatenate([share[:quarter], product, share[quarter:]], axis=0), row_groups
    )
    col_scale, cost_squares, demand_squares = call_plain(
        functools.partial(col_scale_kernel, count),
        gathered + [col_scale, cost_vec],
        whole + squares + squares,
    )
    norms = [sum_cols(cost_squares, col_groups), demand_squares]

    def forward(first, last, product, primal):
        out = call_blocks(
            functools.partial(forward_kernel, count, first, last),
            row_ids,
            col_ids,
            turned,
            product + [col_scale, cost_vec, lower, upper, bound_kind, primal] + norms,
            whole + row_pieces,
            [count, spare],
        )
        return out[0], over_col(out[1:], jnp.add)

    primal, image = forward(True, False, gathered, primal_start)
    out = call_blocks(
        functools.partial(transposed_kernel, count, True),
        row_ids,
        col_ids,
        blocks,
        image + [row_scale, demand, dual_start] + norms,
        whole + col_pieces,
        [count, spare],
    )
    dual, product = out[0], over_row(out[1:], jnp.add)
    primal, image = forward(False, True, product, primal)
    (dual,) = call_plain(
        functools.partial(last_dual_kernel, count, False),
        image + [row_scale, demand, dual] + norms,
        whole,
    )
    return primal.reshape(col_length), dual.reshape(row_length)


def solution(mesh):
    def body(*args):
        return per_device(mesh.shape["row"], mesh.shape["col"], *args)

    return jax.shard_map(
        body,
        mesh=mesh,
        in_specs=(
            P("row", "col", None, None, None),
            P("row", "col", None),
            P("row", "col", None),
            P("col"),
            P("row"),
            P("col"),
            P("col"),
            P("col"),
            P("col"),
            P("row"),
        ),
        out_specs=(P("col"), P("row")),
        check_vma=False,
    )
```

```python
import functools

import jax
import jax.numpy as jnp
from jax import lax
from jax.experimental import pallas as pl
from jax.experimental.pallas import tpu as pltpu
from jax.sharding import PartitionSpec as P

SMALL_EPS = 1e-06
STEP_SCALE = 0.3

CHUNKS = 8
GROUP = 32
ROW_HALVING = 1
QUARTERS = 4
FIRST_VMEM = 44 * 1024 * 1024
BLOCK_VMEM = 16 * 1024 * 1024
SMALL_VMEM = 8 * 1024 * 1024


def bit_of(index, bit):
    return jnp.where((index & bit) != 0, 1, 0)


def row_mask():
    return bit_of(lax.axis_index("col"), ROW_HALVING) * (CHUNKS // 2)


def col_mask():
    return (lax.axis_index("row") & (QUARTERS - 1)) * (CHUNKS // QUARTERS)


def col_place(tile, count, mask):
    return jnp.where(tile < 0, count, tile ^ (mask * (count // CHUNKS)))


def row_place(tile, count, mask):
    return jnp.where(tile < 0, count, tile ^ (mask * (count // CHUNKS)))


def chunk_rows(chunk, size):
    return pl.ds(pl.multiple_of(chunk * size, size), size)


def piece_chunk(pieces, place, size, offset=0):
    per_piece = CHUNKS // len(pieces)
    start = offset + (place % per_piece) * size
    return pieces[place // per_piece], pl.ds(start, size)


def store_pieces(acc, pieces, count):
    size = count // len(pieces)
    for index, piece in enumerate(pieces):
        piece[...] = acc[pl.ds(index * size, size), :]


def add_row(acc, place, term, combine):
    acc[pl.ds(place, 1), :] = combine(acc[pl.ds(place, 1), :], term)


def one_row(ref, tile):
    return ref[pl.ds(jnp.maximum(tile, 0), 1), :]


def tree_sum(parts):
    while len(parts) > 1:
        parts = [parts[i] + parts[i + 1] for i in range(0, len(parts), 2)]
    return parts[0]


def fold_rows(values):
    return jnp.sum(values.reshape(-1, 8, values.shape[-1]), axis=0)


def block_copy(index, values_ref, blocks, arrived):
    part = pl.ds(pl.multiple_of(index * GROUP, GROUP), GROUP)
    return pltpu.make_async_copy(values_ref.at[part], blocks.at[part], arrived.at[index])


def for_slots(ids_ref, visit, finish, before=None):
    count = ids_ref.shape[0] // 2

    def step(index, carry):
        if before is not None:
            before(index)
        slots = [index * GROUP + inner for inner in range(GROUP)]
        ids = [(ids_ref[slot], ids_ref[count + slot]) for slot in slots]
        terms = visit(slots, ids)
        for (row, col), term in zip(ids, terms):
            finish(row, col, term)
        return carry

    lax.fori_loop(0, count // GROUP, step, 0)


def product_terms(vector_ref, tiles, blocks):
    width = vector_ref.shape[1]
    place = lax.broadcasted_iota(jnp.int32, (8, width), 0)
    terms = []
    for start in range(0, len(tiles), 4):
        rows = [one_row(vector_ref, tile) for tile in tiles[start : start + 4]]
        left = jnp.where(place == 0, rows[0], jnp.where(place == 1, rows[1], 0.0))
        right = jnp.where(place == 2, rows[2], jnp.where(place == 3, rows[3], 0.0))
        quad = blocks[start : start + 4]
        found = jnp.dot(
            jnp.concatenate([left, right], axis=1).astype(jnp.bfloat16),
            jnp.concatenate(
                [jnp.concatenate(quad[:2], axis=1), jnp.concatenate(quad[2:], axis=1)], axis=0
            ),
            preferred_element_type=jnp.float32,
        )
        for index in range(4):
            side = (index % 2) * width
            terms.append(found[index : index + 1, side : side + width])
    return terms


def row_max(values):
    return jnp.max(values, axis=0, keepdims=True)


def packed_max(values):
    folded = jnp.max(values.reshape(-1, 16, values.shape[-1]), axis=0)
    return row_max(folded.astype(jnp.float32))


def first_pass_kernel(count, ids_ref, values_ref, *refs):
    row_out, col_out, blocks = refs[:2], refs[2:6], refs[6]
    arrived, row_acc, col_acc = refs[7:]
    mask, across = col_mask(), row_mask()
    for index in range(values_ref.shape[0] // GROUP):
        block_copy(index, values_ref, blocks, arrived).start()
    for acc in (row_acc, col_acc):
        acc[...] = jnp.zeros_like(acc)

    def before(index):
        block_copy(index, values_ref, blocks, arrived).wait()

    def visit(slots, ids):
        sizes = [jnp.abs(blocks[slot]) for slot in slots]
        return [(packed_max(size.T), packed_max(size)) for size in sizes]

    def finish(row, col, terms):
        add_row(row_acc, row_place(row, count, across), terms[0], jnp.maximum)
        add_row(col_acc, col_place(col, count, mask), terms[1], jnp.maximum)

    for_slots(ids_ref, visit, finish, before)
    store_pieces(row_acc, row_out, count)
    store_pieces(col_acc, col_out, count)


def first_product_kernel(count, ids_ref, blocks, dual_ref, *refs):
    product_out, turned, product_acc = refs[:4], refs[4], refs[5]
    mask = col_mask()
    product_acc[...] = jnp.zeros_like(product_acc)

    def visit(slots, ids):
        found = [blocks[slot] for slot in slots]
        for slot, block in zip(slots, found):
            turned[slot] = block.T
        return product_terms(dual_ref, [row for row, _ in ids], found)

    def finish(row, col, term):
        add_row(product_acc, col_place(col, count, mask), term, jnp.add)

    for_slots(ids_ref, visit, finish)
    store_pieces(product_acc, product_out, count)


def second_pass_kernel(count, ids_ref, blocks, *refs):
    row_in, col_in, product_in = refs[:2], refs[2:6], refs[6:10]
    row_out, col_out, refs = refs[10:12], refs[12:16], refs[16:]
    row_scale, col_scale, row_acc, col_acc = refs
    mask, across = col_mask(), row_mask()
    size = count // CHUNKS
    row_acc[...] = jnp.zeros_like(row_acc)
    col_acc[...] = jnp.zeros_like(col_acc)
    for place in range(CHUNKS):
        piece, part = piece_chunk(row_in, place, size)
        row_scale[chunk_rows(place ^ across, size), :] = lax.rsqrt(piece[part, :] + SMALL_EPS)
        piece, part = piece_chunk(col_in, place, size)
        col_scale[chunk_rows(place ^ mask, size), :] = lax.rsqrt(piece[part, :] + SMALL_EPS)
    width = blocks.shape[-1]
    square = (width, width)
    diagonal = lax.broadcasted_iota(jnp.int32, square, 0) == lax.broadcasted_iota(
        jnp.int32, square, 1
    )
    diagonal = diagonal.astype(jnp.float32).astype(jnp.bfloat16)

    def peaks(row, col, slot):
        sizes = jnp.abs(blocks[slot])
        by_col = sizes.astype(jnp.float32) * one_row(col_scale, col)
        scale = one_row(row_scale, row)
        high = scale.astype(jnp.bfloat16)
        low = (scale - high.astype(jnp.float32)).astype(jnp.bfloat16)
        by_row = jnp.dot(
            jnp.concatenate([diagonal * high, diagonal * low], axis=1),
            jnp.concatenate([sizes, sizes], axis=0),
            preferred_element_type=jnp.float32,
        )
        return row_max(by_col.T), row_max(by_row)

    def visit(slots, ids):
        return [peaks(row, col, slot) for slot, (row, col) in zip(slots, ids)]

    def finish(row, col, terms):
        add_row(row_acc, row_place(row, count, across), terms[0], jnp.maximum)
        add_row(col_acc, col_place(col, count, mask), terms[1], jnp.maximum)

    for_slots(ids_ref, visit, finish)
    for place in range(CHUNKS):
        part = pl.ds(place * size, size)
        piece, inside = piece_chunk(row_out, place, size)
        piece[inside, :] = row_acc[part, :] * row_scale[chunk_rows(place ^ across, size), :]
        piece, inside = piece_chunk(col_out, place, size)
        piece[inside, :] = col_acc[part, :] * col_scale[chunk_rows(place ^ mask, size), :]
    quarter = count // QUARTERS
    for piece, product in zip(col_out, product_in):
        piece[pl.ds(quarter, quarter), :] = product[...]


def row_scale_kernel(count, near, far, scale_ref, vector_ref, new_scale, squares):
    across = row_mask()
    size = count // CHUNKS
    sums = []
    for place in range(CHUNKS):
        part = chunk_rows(place ^ across, size)
        piece, inside = piece_chunk((near, far), place, size)
        scale = scale_ref[part, :] * lax.rsqrt(piece[inside, :] + SMALL_EPS)
        new_scale[part, :] = scale
        scaled = scale * vector_ref[part, :]
        sums.append(fold_rows(scaled * scaled))
    half = CHUNKS // 2
    squares[...] = tree_sum(sums[:half]) + tree_sum(sums[half:])


def col_scale_kernel(count, *refs):
    pieces, (scale_ref, vector_ref, new_scale, squares, demand_squares) = refs[:4], refs[4:]
    mask = col_mask()
    size = count // CHUNKS
    sums = []
    for place in range(CHUNKS):
        part = chunk_rows(place ^ mask, size)
        piece, inside = piece_chunk(pieces, place, size)
        scale = scale_ref[part, :] * lax.rsqrt(piece[inside, :] + SMALL_EPS)
        new_scale[part, :] = scale
        scaled = scale * vector_ref[part, :]
        sums.append(fold_rows(scaled * scaled))
    squares[...] = tree_sum(sums)
    tail = pl.ds(pieces[0].shape[0] - 8, 8)
    demand_squares[...] = tree_sum([piece[tail, :] for piece in pieces])


def norm_ratio(cost_squares, demand_squares):
    cost_total = jnp.sum(cost_squares[...], keepdims=True)
    demand_total = jnp.sum(demand_squares[...], keepdims=True)
    return jnp.sqrt(cost_total + SMALL_EPS) / jnp.sqrt(demand_total + SMALL_EPS)


def forward_kernel(count, first, last, ids_ref, turned, *refs):
    product, refs = refs[:4], refs[4:]
    scale_ref, cost_ref, low_ref, high_ref, kind_ref, primal_ref = refs[:6]
    cost_squares, demand_squares, primal_out = refs[6:9]
    row_out, (shifted, row_acc) = refs[9:11], refs[11:]
    mask, across = col_mask(), row_mask()
    size = count // CHUNKS
    row_acc[...] = jnp.zeros_like(row_acc)
    primal_step = STEP_SCALE / norm_ratio(cost_squares, demand_squares)
    for place in range(CHUNKS):
        part = chunk_rows(place ^ mask, size)
        piece, inside = piece_chunk(product, place, size, count // QUARTERS if first else 0)
        scale = scale_ref[part, :]
        inverse = 1.0 / scale
        primal = primal_ref[part, :]
        if first:
            primal = primal * inverse
        gradient = scale * piece[inside, :]
        moved = primal - primal_step * (scale * cost_ref[part, :] - gradient)
        kind = kind_ref[part, :]
        moved = jnp.where(
            (kind == 1) | (kind == 3), jnp.maximum(moved, low_ref[part, :] * inverse), moved
        )
        moved = jnp.where(
            (kind == 2) | (kind == 3), jnp.minimum(moved, high_ref[part, :] * inverse), moved
        )
        shifted[part, :] = scale * (2.0 * moved - primal)
        primal_out[part, :] = scale * moved if last else moved

    def visit(slots, ids):
        return product_terms(shifted, [col for _, col in ids], [turned[slot] for slot in slots])

    def finish(row, col, term):
        add_row(row_acc, row_place(row, count, across), term, jnp.add)

    for_slots(ids_ref, visit, finish)
    store_pieces(row_acc, row_out, count)


def next_dual(first, image, inside, scale, demand, dual, dual_step):
    if first:
        dual = dual / scale
    row_image = scale * image[inside, :]
    return jnp.maximum(dual + dual_step * (scale * demand - row_image), 0.0)


def transposed_kernel(count, first, ids_ref, blocks, *refs):
    image, refs = refs[:2], refs[2:]
    scale_ref, demand_ref, dual_ref, cost_squares, demand_squares, dual_out = refs[:6]
    product_out, (weights, product_acc) = refs[6:10], refs[10:]
    mask, across = col_mask(), row_mask()
    size = count // CHUNKS
    product_acc[...] = jnp.zeros_like(product_acc)
    dual_step = STEP_SCALE * norm_ratio(cost_squares, demand_squares)
    for place in range(CHUNKS):
        part = chunk_rows(place ^ across, size)
        piece, inside = piece_chunk(image, place, size)
        scale = scale_ref[part, :]
        dual = next_dual(
            first, piece, inside, scale, demand_ref[part, :], dual_ref[part, :], dual_step
        )
        dual_out[part, :] = dual
        weights[part, :] = scale * dual

    def visit(slots, ids):
        return product_terms(weights, [row for row, _ in ids], [blocks[slot] for slot in slots])

    def finish(row, col, term):
        add_row(product_acc, col_place(col, count, mask), term, jnp.add)

    for_slots(ids_ref, visit, finish)
    store_pieces(product_acc, product_out, count)


def last_dual_kernel(count, first, *refs):
    image, refs = refs[:2], refs[2:]
    scale_ref, demand_ref, dual_ref, cost_squares, demand_squares, dual_out = refs
    across = row_mask()
    size = count // CHUNKS
    dual_step = STEP_SCALE * norm_ratio(cost_squares, demand_squares)
    for place in range(CHUNKS):
        part = chunk_rows(place ^ across, size)
        piece, inside = piece_chunk(image, place, size)
        scale = scale_ref[part, :]
        dual = next_dual(
            first, piece, inside, scale, demand_ref[part, :], dual_ref[part, :], dual_step
        )
        dual_out[part, :] = scale * dual


def vectors(*row_counts):
    return [jax.ShapeDtypeStruct((rows, 128), jnp.float32) for rows in row_counts]


def call_plain(kernel, operands, out_shape):
    return pl.pallas_call(
        kernel,
        out_shape=out_shape,
        in_specs=[pl.BlockSpec(memory_space=pltpu.VMEM)] * len(operands),
        out_specs=[pl.BlockSpec(memory_space=pltpu.VMEM)] * len(out_shape),
        compiler_params=pltpu.CompilerParams(vmem_limit_bytes=SMALL_VMEM),
    )(*operands)


def call_blocks(kernel, ids, values, operands, out_shape, scratch, first=False):
    width = values.shape[1]
    scratch_shapes = [pltpu.VMEM((rows, width), jnp.float32) for rows in scratch]
    if first:
        arrivals = pltpu.SemaphoreType.DMA((values.shape[0] // GROUP,))
        scratch_shapes = [arrivals] + scratch_shapes
    return pl.pallas_call(
        kernel,
        out_shape=out_shape,
        in_specs=[pl.BlockSpec(memory_space=pltpu.SMEM)]
        + [pl.BlockSpec(memory_space=pl.ANY if first else pltpu.VMEM)]
        + [pl.BlockSpec(memory_space=pltpu.VMEM)] * len(operands),
        out_specs=[pl.BlockSpec(memory_space=pltpu.VMEM)] * len(out_shape),
        scratch_shapes=scratch_shapes,
        compiler_params=pltpu.CompilerParams(
            vmem_limit_bytes=FIRST_VMEM if first else BLOCK_VMEM
        ),
        cost_estimate=pl.CostEstimate(
            flops=2 * values.size, bytes_accessed=2 * values.size, transcendentals=0
        ),
    )(ids, values, *operands)


def swap(vector, axis, size, bit):
    return lax.ppermute(vector, axis, [(i, i ^ bit) for i in range(size)])


def reduce_rows(pieces, groups, combine):
    near, far = pieces
    near = combine(near, swap(far, "col", groups, ROW_HALVING))
    bit = 1
    while bit < groups:
        if bit != ROW_HALVING:
            near = combine(near, swap(near, "col", groups, bit))
        bit *= 2
    return [near, swap(near, "col", groups, ROW_HALVING)]


def scatter_cols(pieces, groups, combine):
    got = {
        mask: swap(pieces[mask], "row", groups, mask) for mask in (QUARTERS - 1, 1, 2)
    }
    return combine(combine(pieces[0], got[1]), combine(got[2], got[3]))


def exchange_cols(piece, groups, combine):
    bit = QUARTERS
    while bit < groups:
        piece = combine(piece, swap(piece, "row", groups, bit))
        bit *= 2
    return piece


def gather_cols(piece, groups):
    got = {mask: swap(piece, "row", groups, mask) for mask in (QUARTERS - 1, 1, 2)}
    return [piece] + [got[mask] for mask in range(1, QUARTERS)]


def sum_cols(vector, groups):
    bit = 1
    while bit < groups:
        vector = vector + swap(vector, "col", groups, bit)
        bit *= 2
    return vector


def per_device(
    row_groups,
    col_groups,
    block_values,
    block_rows,
    block_cols,
    cost_vec,
    demand,
    lower,
    upper,
    bound_kind,
    primal_start,
    dual_start,
):
    values = block_values[0, 0]
    width = values.shape[1]
    ids = jnp.concatenate([block_rows[0, 0], block_cols[0, 0]])
    row_length, col_length = demand.shape[0], cost_vec.shape[0]
    cost_vec, demand, lower, upper, bound_kind, primal_start, dual_start = [
        v.reshape(-1, width)
        for v in (cost_vec, demand, lower, upper, bound_kind, primal_start, dual_start)
    ]
    count = demand.shape[0]
    half, quarter, spare = count // 2, count // QUARTERS, count + 8
    row_pieces, col_pieces = vectors(half, half), vectors(*[quarter] * QUARTERS)
    whole = vectors(count)
    squares = vectors(8)

    def over_col(pieces, combine):
        return reduce_rows(pieces, col_groups, combine)

    def over_row(pieces, combine):
        share = scatter_cols(pieces, row_groups, combine)
        return gather_cols(exchange_cols(share, row_groups, combine), row_groups)

    tile = lax.broadcasted_iota(jnp.int32, (2 * quarter + 8, width), 0)

    def mixed(a, b):
        return jnp.where(tile[: a.shape[0]] < quarter, jnp.maximum(a, b), a + b)

    block_shape = jax.ShapeDtypeStruct(values.shape, values.dtype)
    out = call_blocks(
        functools.partial(first_pass_kernel, count),
        ids,
        values,
        [],
        row_pieces + col_pieces + [block_shape],
        [spare] * 2,
        first=True,
    )
    blocks = out[6]
    row_peaks = over_col(out[:2], jnp.maximum)
    share = scatter_cols(out[2:6], row_groups, jnp.maximum)
    share, dual_first = lax.optimization_barrier((share, dual_start))
    *first_product, turned = call_blocks(
        functools.partial(first_product_kernel, count),
        ids,
        blocks,
        [dual_first],
        col_pieces + [block_shape],
        [spare],
    )
    col_peaks = gather_cols(exchange_cols(share, row_groups, jnp.maximum), row_groups)
    out = call_blocks(
        functools.partial(second_pass_kernel, count),
        ids,
        blocks,
        row_peaks + col_peaks + first_product,
        row_pieces + vectors(*[2 * quarter] * QUARTERS) + whole + whole,
        [spare] * 2,
    )
    row_scale, col_scale = out[6:]
    row_peaks = over_col(out[:2], jnp.maximum)
    row_scale, demand_squares = call_plain(
        functools.partial(row_scale_kernel, count),
        row_peaks + [row_scale, demand],
        whole + squares,
    )
    share = scatter_cols(out[2:6], row_groups, mixed)
    share = exchange_cols(
        jnp.concatenate([share, demand_squares], axis=0), row_groups, mixed
    )
    gathered = gather_cols(share, row_groups)
    col_scale, cost_squares, demand_squares = call_plain(
        functools.partial(col_scale_kernel, count),
        gathered + [col_scale, cost_vec],
        whole + squares + squares,
    )
    norms = [sum_cols(cost_squares, col_groups), demand_squares]

    def forward(first, last, product, primal):
        out = call_blocks(
            functools.partial(forward_kernel, count, first, last),
            ids,
            turned,
            product + [col_scale, cost_vec, lower, upper, bound_kind, primal] + norms,
            whole + row_pieces,
            [count, spare],
        )
        return out[0], over_col(out[1:], jnp.add)

    primal, image = forward(True, False, gathered, primal_start)
    out = call_blocks(
        functools.partial(transposed_kernel, count, True),
        ids,
        blocks,
        image + [row_scale, demand, dual_start] + norms,
        whole + col_pieces,
        [count, spare],
    )
    dual, product = out[0], over_row(out[1:], jnp.add)
    primal, image = forward(False, True, product, primal)
    (dual,) = call_plain(
        functools.partial(last_dual_kernel, count, False),
        image + [row_scale, demand, dual] + norms,
        whole,
    )
    return primal.reshape(col_length), dual.reshape(row_length)


def solution(mesh):
    def body(*args):
        return per_device(mesh.shape["row"], mesh.shape["col"], *args)

    return jax.shard_map(
        body,
        mesh=mesh,
        in_specs=(
            P("row", "col", None, None, None),
            P("row", "col", None),
            P("row", "col", None),
            P("col"),
            P("row"),
            P("col"),
            P("col"),
            P("col"),
            P("col"),
            P("row"),
        ),
        out_specs=(P("col"), P("row")),
        check_vma=False,
    )
```

```python
import functools

import jax
import jax.numpy as jnp
from jax import lax
from jax.experimental import pallas as pl
from jax.experimental.pallas import tpu as pltpu
from jax.sharding import PartitionSpec as P

SMALL_EPS = 1e-06
STEP_SCALE = 0.3

CHUNKS = 8
GROUP = 32
AHEAD = 3
ROW_HALVING = 1
QUARTERS = 4
FIRST_VMEM = 44 * 1024 * 1024
BLOCK_VMEM = 16 * 1024 * 1024
SMALL_VMEM = 8 * 1024 * 1024


def bit_of(index, bit):
    return jnp.where((index & bit) != 0, 1, 0)


def row_mask():
    return bit_of(lax.axis_index("col"), ROW_HALVING) * (CHUNKS // 2)


def col_mask():
    return (lax.axis_index("row") & (QUARTERS - 1)) * (CHUNKS // QUARTERS)


def col_place(tile, count, mask):
    return jnp.where(tile < 0, count, tile ^ (mask * (count // CHUNKS)))


def row_place(tile, count, mask):
    return jnp.where(tile < 0, count, tile ^ (mask * (count // CHUNKS)))


def chunk_rows(chunk, size):
    return pl.ds(pl.multiple_of(chunk * size, size), size)


def piece_chunk(pieces, place, size):
    per_piece = CHUNKS // len(pieces)
    start = (place % per_piece) * size
    return pieces[place // per_piece], pl.ds(start, size)


def store_pieces(acc, pieces, count):
    size = count // len(pieces)
    for index, piece in enumerate(pieces):
        piece[...] = acc[pl.ds(index * size, size), :]


def add_row(acc, place, term, combine):
    acc[pl.ds(place, 1), :] = combine(acc[pl.ds(place, 1), :], term)


def one_row(ref, tile):
    return ref[pl.ds(jnp.maximum(tile, 0), 1), :]


def tree_sum(parts):
    while len(parts) > 1:
        parts = [parts[i] + parts[i + 1] for i in range(0, len(parts), 2)]
    return parts[0]


def fold_rows(values):
    return jnp.sum(values.reshape(-1, 8, values.shape[-1]), axis=0)


def block_copy(index, values_ref, blocks, arrived):
    part = pl.ds(pl.multiple_of(index * GROUP, GROUP), GROUP)
    return pltpu.make_async_copy(values_ref.at[part], blocks.at[part], arrived.at[index])


def for_slots(ids_ref, visit, finish, before=None):
    count = ids_ref.shape[0] // 2

    def step(index, carry):
        if before is not None:
            before(index)
        slots = [index * GROUP + inner for inner in range(GROUP)]
        ids = [(ids_ref[slot], ids_ref[count + slot]) for slot in slots]
        terms = visit(slots, ids)
        for (row, col), term in zip(ids, terms):
            finish(row, col, term)
        return carry

    lax.fori_loop(0, count // GROUP, step, 0)


def product_terms(vector_ref, tiles, blocks):
    width = vector_ref.shape[1]
    place = lax.broadcasted_iota(jnp.int32, (8, width), 0)
    terms = []
    for start in range(0, len(tiles), 4):
        rows = [one_row(vector_ref, tile) for tile in tiles[start : start + 4]]
        left = jnp.where(place == 0, rows[0], jnp.where(place == 1, rows[1], 0.0))
        right = jnp.where(place == 2, rows[2], jnp.where(place == 3, rows[3], 0.0))
        quad = blocks[start : start + 4]
        found = jnp.dot(
            jnp.concatenate([left, right], axis=1).astype(jnp.bfloat16),
            jnp.concatenate(
                [jnp.concatenate(quad[:2], axis=1), jnp.concatenate(quad[2:], axis=1)], axis=0
            ),
            preferred_element_type=jnp.float32,
        )
        for index in range(4):
            side = (index % 2) * width
            terms.append(found[index : index + 1, side : side + width])
    return terms


def row_max(values):
    return jnp.max(values, axis=0, keepdims=True)


def packed_max(values):
    folded = jnp.max(values.reshape(-1, 16, values.shape[-1]), axis=0)
    return row_max(folded.astype(jnp.float32))


def first_pass_kernel(count, ids_ref, values_ref, *refs):
    row_out, col_out, blocks = refs[:2], refs[2:6], refs[6]
    arrived, row_acc, col_acc = refs[7:]
    mask, across = col_mask(), row_mask()
    groups = values_ref.shape[0] // GROUP
    for index in range(min(AHEAD, groups)):
        block_copy(index, values_ref, blocks, arrived).start()
    for acc in (row_acc, col_acc):
        acc[...] = jnp.zeros_like(acc)

    def before(index):
        block_copy(index, values_ref, blocks, arrived).wait()

        @pl.when(index + AHEAD < groups)
        def _():
            block_copy(index + AHEAD, values_ref, blocks, arrived).start()

    def visit(slots, ids):
        sizes = [jnp.abs(blocks[slot]) for slot in slots]
        return [(packed_max(size.T), packed_max(size)) for size in sizes]

    def finish(row, col, terms):
        add_row(row_acc, row_place(row, count, across), terms[0], jnp.maximum)
        add_row(col_acc, col_place(col, count, mask), terms[1], jnp.maximum)

    for_slots(ids_ref, visit, finish, before)
    store_pieces(row_acc, row_out, count)
    store_pieces(col_acc, col_out, count)


def first_product_kernel(count, ids_ref, blocks, dual_ref, *refs):
    product_out, turned, product_acc = refs[:4], refs[4], refs[5]
    mask = col_mask()
    product_acc[...] = jnp.zeros_like(product_acc)

    def visit(slots, ids):
        found = [blocks[slot] for slot in slots]
        for slot, block in zip(slots, found):
            turned[slot] = block.T
        return product_terms(dual_ref, [row for row, _ in ids], found)

    def finish(row, col, term):
        add_row(product_acc, col_place(col, count, mask), term, jnp.add)

    for_slots(ids_ref, visit, finish)
    store_pieces(product_acc, product_out, count)


def second_pass_kernel(count, ids_ref, blocks, *refs):
    row_in, col_in, row_out, col_out = refs[:2], refs[2:6], refs[6:8], refs[8:12]
    row_scale, col_scale, row_acc, col_acc = refs[12:]
    mask, across = col_mask(), row_mask()
    size = count // CHUNKS
    row_acc[...] = jnp.zeros_like(row_acc)
    col_acc[...] = jnp.zeros_like(col_acc)
    for place in range(CHUNKS):
        piece, part = piece_chunk(row_in, place, size)
        row_scale[chunk_rows(place ^ across, size), :] = lax.rsqrt(piece[part, :] + SMALL_EPS)
        piece, part = piece_chunk(col_in, place, size)
        col_scale[chunk_rows(place ^ mask, size), :] = lax.rsqrt(piece[part, :] + SMALL_EPS)
    width = blocks.shape[-1]
    square = (width, width)
    diagonal = lax.broadcasted_iota(jnp.int32, square, 0) == lax.broadcasted_iota(
        jnp.int32, square, 1
    )
    diagonal = diagonal.astype(jnp.float32).astype(jnp.bfloat16)

    def peaks(row, col, slot):
        sizes = jnp.abs(blocks[slot])
        by_col = sizes.astype(jnp.float32) * one_row(col_scale, col)
        scale = one_row(row_scale, row)
        high = scale.astype(jnp.bfloat16)
        low = (scale - high.astype(jnp.float32)).astype(jnp.bfloat16)
        by_row = jnp.dot(
            jnp.concatenate([diagonal * high, diagonal * low], axis=1),
            jnp.concatenate([sizes, sizes], axis=0),
            preferred_element_type=jnp.float32,
        )
        return row_max(by_col.T), row_max(by_row)

    def visit(slots, ids):
        return [peaks(row, col, slot) for slot, (row, col) in zip(slots, ids)]

    def finish(row, col, terms):
        add_row(row_acc, row_place(row, count, across), terms[0], jnp.maximum)
        add_row(col_acc, col_place(col, count, mask), terms[1], jnp.maximum)

    for_slots(ids_ref, visit, finish)
    for place in range(CHUNKS):
        part = pl.ds(place * size, size)
        piece, inside = piece_chunk(row_out, place, size)
        piece[inside, :] = row_acc[part, :] * row_scale[chunk_rows(place ^ across, size), :]
        piece, inside = piece_chunk(col_out, place, size)
        piece[inside, :] = col_acc[part, :] * col_scale[chunk_rows(place ^ mask, size), :]


def row_scale_kernel(count, near, far, scale_ref, vector_ref, new_scale, squares):
    across = row_mask()
    size = count // CHUNKS
    sums = []
    for place in range(CHUNKS):
        part = chunk_rows(place ^ across, size)
        piece, inside = piece_chunk((near, far), place, size)
        scale = scale_ref[part, :] * lax.rsqrt(piece[inside, :] + SMALL_EPS)
        new_scale[part, :] = scale
        scaled = scale * vector_ref[part, :]
        sums.append(fold_rows(scaled * scaled))
    half = CHUNKS // 2
    squares[...] = tree_sum(sums[:half]) + tree_sum(sums[half:])


def col_scale_kernel(count, *refs):
    pieces, (scale_ref, vector_ref, new_scale, squares, demand_squares) = refs[:4], refs[4:]
    mask = col_mask()
    size = count // CHUNKS
    sums = []
    for place in range(CHUNKS):
        part = chunk_rows(place ^ mask, size)
        piece, inside = piece_chunk(pieces, place, size)
        scale = scale_ref[part, :] * lax.rsqrt(piece[inside, :] + SMALL_EPS)
        new_scale[part, :] = scale
        scaled = scale * vector_ref[part, :]
        sums.append(fold_rows(scaled * scaled))
    squares[...] = tree_sum(sums)
    tail = pl.ds(pieces[0].shape[0] - 8, 8)
    demand_squares[...] = tree_sum([piece[tail, :] for piece in pieces])


def norm_ratio(cost_squares, demand_squares):
    cost_total = jnp.sum(cost_squares[...], keepdims=True)
    demand_total = jnp.sum(demand_squares[...], keepdims=True)
    return jnp.sqrt(cost_total + SMALL_EPS) / jnp.sqrt(demand_total + SMALL_EPS)


def forward_kernel(count, first, last, ids_ref, turned, *refs):
    product, refs = refs[:4], refs[4:]
    scale_ref, cost_ref, low_ref, high_ref, kind_ref, primal_ref = refs[:6]
    cost_squares, demand_squares, primal_out = refs[6:9]
    row_out, (shifted, row_acc) = refs[9:11], refs[11:]
    mask, across = col_mask(), row_mask()
    size = count // CHUNKS
    row_acc[...] = jnp.zeros_like(row_acc)
    primal_step = STEP_SCALE / norm_ratio(cost_squares, demand_squares)
    for place in range(CHUNKS):
        part = chunk_rows(place ^ mask, size)
        piece, inside = piece_chunk(product, place, size)
        scale = scale_ref[part, :]
        inverse = 1.0 / scale
        primal = primal_ref[part, :]
        if first:
            primal = primal * inverse
        gradient = scale * piece[inside, :]
        moved = primal - primal_step * (scale * cost_ref[part, :] - gradient)
        kind = kind_ref[part, :]
        moved = jnp.where(
            (kind == 1) | (kind == 3), jnp.maximum(moved, low_ref[part, :] * inverse), moved
        )
        moved = jnp.where(
            (kind == 2) | (kind == 3), jnp.minimum(moved, high_ref[part, :] * inverse), moved
        )
        shifted[part, :] = scale * (2.0 * moved - primal)
        primal_out[part, :] = scale * moved if last else moved

    def visit(slots, ids):
        return product_terms(shifted, [col for _, col in ids], [turned[slot] for slot in slots])

    def finish(row, col, term):
        add_row(row_acc, row_place(row, count, across), term, jnp.add)

    for_slots(ids_ref, visit, finish)
    store_pieces(row_acc, row_out, count)


def next_dual(first, image, inside, scale, demand, dual, dual_step):
    if first:
        dual = dual / scale
    row_image = scale * image[inside, :]
    return jnp.maximum(dual + dual_step * (scale * demand - row_image), 0.0)


def transposed_kernel(count, first, ids_ref, blocks, *refs):
    image, refs = refs[:2], refs[2:]
    scale_ref, demand_ref, dual_ref, cost_squares, demand_squares, dual_out = refs[:6]
    product_out, (weights, product_acc) = refs[6:10], refs[10:]
    mask, across = col_mask(), row_mask()
    size = count // CHUNKS
    product_acc[...] = jnp.zeros_like(product_acc)
    dual_step = STEP_SCALE * norm_ratio(cost_squares, demand_squares)
    for place in range(CHUNKS):
        part = chunk_rows(place ^ across, size)
        piece, inside = piece_chunk(image, place, size)
        scale = scale_ref[part, :]
        dual = next_dual(
            first, piece, inside, scale, demand_ref[part, :], dual_ref[part, :], dual_step
        )
        dual_out[part, :] = dual
        weights[part, :] = scale * dual

    def visit(slots, ids):
        return product_terms(weights, [row for row, _ in ids], [blocks[slot] for slot in slots])

    def finish(row, col, term):
        add_row(product_acc, col_place(col, count, mask), term, jnp.add)

    for_slots(ids_ref, visit, finish)
    store_pieces(product_acc, product_out, count)


def last_dual_kernel(count, first, *refs):
    image, refs = refs[:2], refs[2:]
    scale_ref, demand_ref, dual_ref, cost_squares, demand_squares, dual_out = refs
    across = row_mask()
    size = count // CHUNKS
    dual_step = STEP_SCALE * norm_ratio(cost_squares, demand_squares)
    for place in range(CHUNKS):
        part = chunk_rows(place ^ across, size)
        piece, inside = piece_chunk(image, place, size)
        scale = scale_ref[part, :]
        dual = next_dual(
            first, piece, inside, scale, demand_ref[part, :], dual_ref[part, :], dual_step
        )
        dual_out[part, :] = scale * dual


def vectors(*row_counts):
    return [jax.ShapeDtypeStruct((rows, 128), jnp.float32) for rows in row_counts]


def call_plain(kernel, operands, out_shape):
    return pl.pallas_call(
        kernel,
        out_shape=out_shape,
        in_specs=[pl.BlockSpec(memory_space=pltpu.VMEM)] * len(operands),
        out_specs=[pl.BlockSpec(memory_space=pltpu.VMEM)] * len(out_shape),
        compiler_params=pltpu.CompilerParams(vmem_limit_bytes=SMALL_VMEM),
    )(*operands)


def call_blocks(kernel, ids, values, operands, out_shape, scratch, first=False):
    width = values.shape[1]
    scratch_shapes = [pltpu.VMEM((rows, width), jnp.float32) for rows in scratch]
    if first:
        arrivals = pltpu.SemaphoreType.DMA((values.shape[0] // GROUP,))
        scratch_shapes = [arrivals] + scratch_shapes
    return pl.pallas_call(
        kernel,
        out_shape=out_shape,
        in_specs=[pl.BlockSpec(memory_space=pltpu.SMEM)]
        + [pl.BlockSpec(memory_space=pl.ANY if first else pltpu.VMEM)]
        + [pl.BlockSpec(memory_space=pltpu.VMEM)] * len(operands),
        out_specs=[pl.BlockSpec(memory_space=pltpu.VMEM)] * len(out_shape),
        scratch_shapes=scratch_shapes,
        compiler_params=pltpu.CompilerParams(
            vmem_limit_bytes=FIRST_VMEM if first else BLOCK_VMEM
        ),
        cost_estimate=pl.CostEstimate(
            flops=2 * values.size, bytes_accessed=2 * values.size, transcendentals=0
        ),
    )(ids, values, *operands)


def swap(vector, axis, size, bit):
    return lax.ppermute(vector, axis, [(i, i ^ bit) for i in range(size)])


def after(values, *earlier):
    return lax.optimization_barrier((values, earlier))[0]


def halve_rows(pieces, groups, combine):
    near, far = pieces
    return combine(near, swap(far, "col", groups, ROW_HALVING))


def exchange_rows(near, groups, combine):
    bit = 1
    while bit < groups:
        if bit != ROW_HALVING:
            near = combine(near, swap(near, "col", groups, bit))
        bit *= 2
    return near


def join_rows(near, groups):
    return [near, swap(near, "col", groups, ROW_HALVING)]


def scatter_cols(pieces, groups, combine, tie=()):
    diagonal = swap(pieces[3], "row", groups, 3)
    first, second = after((pieces[1], pieces[2]), *tie) if tie else pieces[1:3]
    first, second = swap(first, "row", groups, 1), swap(second, "row", groups, 2)
    return combine(combine(pieces[0], first), combine(second, diagonal))


def exchange_cols(piece, groups, combine):
    bit = QUARTERS
    while bit < groups:
        piece = combine(piece, swap(piece, "row", groups, bit))
        bit *= 2
    return piece


def gather_cols(piece, groups):
    diagonal = swap(piece, "row", groups, 3)
    return [piece, swap(piece, "row", groups, 1), swap(piece, "row", groups, 2), diagonal]


def sum_cols(vector, groups):
    bit = 1
    while bit < groups:
        vector = vector + swap(vector, "col", groups, bit)
        bit *= 2
    return vector


def per_device(
    row_groups,
    col_groups,
    block_values,
    block_rows,
    block_cols,
    cost_vec,
    demand,
    lower,
    upper,
    bound_kind,
    primal_start,
    dual_start,
):
    values = block_values[0, 0]
    width = values.shape[1]
    ids = jnp.concatenate([block_rows[0, 0], block_cols[0, 0]])
    row_length, col_length = demand.shape[0], cost_vec.shape[0]
    cost_vec, demand, lower, upper, bound_kind, primal_start, dual_start = [
        v.reshape(-1, width)
        for v in (cost_vec, demand, lower, upper, bound_kind, primal_start, dual_start)
    ]
    count = demand.shape[0]
    half, quarter, spare = count // 2, count // QUARTERS, count + 8
    row_pieces, col_pieces = vectors(half, half), vectors(*[quarter] * QUARTERS)
    whole = vectors(count)
    squares = vectors(8)

    def over_col(pieces, combine):
        near = exchange_rows(halve_rows(pieces, col_groups, combine), col_groups, combine)
        return join_rows(near, col_groups)

    def over_row(pieces, combine):
        share = scatter_cols(pieces, row_groups, combine)
        return gather_cols(exchange_cols(share, row_groups, combine), row_groups)

    tile = lax.broadcasted_iota(jnp.int32, (quarter + 8, width), 0)

    def mixed(a, b):
        return jnp.where(tile < quarter, jnp.maximum(a, b), a + b)

    block_shape = jax.ShapeDtypeStruct(values.shape, values.dtype)
    out = call_blocks(
        functools.partial(first_pass_kernel, count),
        ids,
        values,
        [],
        row_pieces + col_pieces + [block_shape],
        [spare] * 2,
        first=True,
    )
    blocks = out[6]
    near = halve_rows(out[:2], col_groups, jnp.maximum)
    *product_pieces, turned = call_blocks(
        functools.partial(first_product_kernel, count),
        ids,
        blocks,
        [after(dual_start, near)],
        col_pieces + [block_shape],
        [spare],
    )
    share = scatter_cols(out[2:6], row_groups, jnp.maximum, (near,))
    near = exchange_rows(near, col_groups, jnp.maximum)
    row_peaks = join_rows(near, col_groups)
    product = scatter_cols(after(product_pieces, near), row_groups, jnp.add)
    share = after(exchange_cols(share, row_groups, jnp.maximum), product_pieces)
    row_peaks, col_peaks = after((row_peaks, gather_cols(share, row_groups)), product)
    product = exchange_cols(product, row_groups, jnp.add)
    out = call_blocks(
        functools.partial(second_pass_kernel, count),
        ids,
        blocks,
        row_peaks + col_peaks,
        row_pieces + col_pieces + whole + whole,
        [spare] * 2,
    )
    row_scale, col_scale = out[6:]
    near = halve_rows(out[:2], col_groups, jnp.maximum)
    share = scatter_cols(out[2:6], row_groups, jnp.maximum, (near,))
    row_peaks = join_rows(exchange_rows(near, col_groups, jnp.maximum), col_groups)
    row_scale, demand_squares = call_plain(
        functools.partial(row_scale_kernel, count),
        row_peaks + [row_scale, demand],
        whole + squares,
    )
    share = after(jnp.concatenate([share, demand_squares], axis=0), product)
    product = gather_cols(after(product, share), row_groups)
    gathered = gather_cols(exchange_cols(share, row_groups, mixed), row_groups)
    col_scale, cost_squares, demand_squares = call_plain(
        functools.partial(col_scale_kernel, count),
        gathered + [col_scale, cost_vec],
        whole + squares + squares,
    )
    norms = [sum_cols(after(cost_squares, product), col_groups), demand_squares]

    def forward(first, last, product, primal):
        out = call_blocks(
            functools.partial(forward_kernel, count, first, last),
            ids,
            turned,
            product + [col_scale, cost_vec, lower, upper, bound_kind, primal] + norms,
            whole + row_pieces,
            [count, spare],
        )
        return out[0], over_col(out[1:], jnp.add)

    primal, image = forward(True, False, product, primal_start)
    out = call_blocks(
        functools.partial(transposed_kernel, count, True),
        ids,
        blocks,
        image + [row_scale, demand, dual_start] + norms,
        whole + col_pieces,
        [count, spare],
    )
    dual, product = out[0], over_row(out[1:], jnp.add)
    primal, image = forward(False, True, product, primal)
    (dual,) = call_plain(
        functools.partial(last_dual_kernel, count, False),
        image + [row_scale, demand, dual] + norms,
        whole,
    )
    return primal.reshape(col_length), dual.reshape(row_length)


def solution(mesh):
    def body(*args):
        return per_device(mesh.shape["row"], mesh.shape["col"], *args)

    return jax.shard_map(
        body,
        mesh=mesh,
        in_specs=(
            P("row", "col", None, None, None),
            P("row", "col", None),
            P("row", "col", None),
            P("col"),
            P("row"),
            P("col"),
            P("col"),
            P("col"),
            P("col"),
            P("row"),
        ),
        out_specs=(P("col"), P("row")),
        check_vma=False,
    )
```

```python
import functools

import jax
import jax.numpy as jnp
from jax import lax
from jax.experimental import pallas as pl
from jax.experimental.pallas import tpu as pltpu
from jax.sharding import PartitionSpec as P

SMALL_EPS = 1e-06
STEP_SCALE = 0.3

CHUNKS = 8
FIRST_GROUP = 32
GROUP = 64
AHEAD = 3
ROW_HALVING = 1
QUARTERS = 4
FIRST_VMEM = 44 * 1024 * 1024
BLOCK_VMEM = 16 * 1024 * 1024
SMALL_VMEM = 8 * 1024 * 1024


def bit_of(index, bit):
    return jnp.where((index & bit) != 0, 1, 0)


def row_mask():
    return bit_of(lax.axis_index("col"), ROW_HALVING) * (CHUNKS // 2)


def col_mask():
    return (lax.axis_index("row") & (QUARTERS - 1)) * (CHUNKS // QUARTERS)


def col_place(tile, count, mask):
    return jnp.where(tile < 0, count, tile ^ (mask * (count // CHUNKS)))


def row_place(tile, count, mask):
    return jnp.where(tile < 0, count, tile ^ (mask * (count // CHUNKS)))


def chunk_rows(chunk, size):
    return pl.ds(pl.multiple_of(chunk * size, size), size)


def piece_chunk(pieces, place, size, offset=0):
    per_piece = CHUNKS // len(pieces)
    start = offset + (place % per_piece) * size
    return pieces[place // per_piece], pl.ds(start, size)


def store_pieces(acc, pieces, count):
    size = count // len(pieces)
    for index, piece in enumerate(pieces):
        piece[...] = acc[pl.ds(index * size, size), :]


def add_row(acc, place, term, combine):
    acc[pl.ds(place, 1), :] = combine(acc[pl.ds(place, 1), :], term)


def one_row(ref, tile):
    return ref[pl.ds(jnp.maximum(tile, 0), 1), :]


def tree_sum(parts):
    while len(parts) > 1:
        parts = [parts[i] + parts[i + 1] for i in range(0, len(parts), 2)]
    return parts[0]


def fold_rows(values):
    return jnp.sum(values.reshape(-1, 8, values.shape[-1]), axis=0)


def block_copy(index, values_ref, blocks, arrived):
    part = pl.ds(pl.multiple_of(index * FIRST_GROUP, FIRST_GROUP), FIRST_GROUP)
    return pltpu.make_async_copy(values_ref.at[part], blocks.at[part], arrived.at[index])


def for_slots(ids_ref, visit, finish, group=GROUP, before=None):
    count = ids_ref.shape[0] // 2

    def step(index, carry):
        if before is not None:
            before(index)
        slots = [index * group + inner for inner in range(group)]
        ids = [(ids_ref[slot], ids_ref[count + slot]) for slot in slots]
        terms = visit(slots, ids)
        for (row, col), term in zip(ids, terms):
            finish(row, col, term)
        return carry

    lax.fori_loop(0, count // group, step, 0)


def product_terms(vector_ref, tiles, blocks):
    width = vector_ref.shape[1]
    place = lax.broadcasted_iota(jnp.int32, (8, width), 0)
    terms = []
    for start in range(0, len(tiles), 4):
        rows = [one_row(vector_ref, tile) for tile in tiles[start : start + 4]]
        left = jnp.where(place == 0, rows[0], jnp.where(place == 1, rows[1], 0.0))
        right = jnp.where(place == 2, rows[2], jnp.where(place == 3, rows[3], 0.0))
        quad = blocks[start : start + 4]
        found = jnp.dot(
            jnp.concatenate([left, right], axis=1).astype(jnp.bfloat16),
            jnp.concatenate(
                [jnp.concatenate(quad[:2], axis=1), jnp.concatenate(quad[2:], axis=1)], axis=0
            ),
            preferred_element_type=jnp.float32,
        )
        for index in range(4):
            side = (index % 2) * width
            terms.append(found[index : index + 1, side : side + width])
    return terms


def row_max(values):
    return jnp.max(values, axis=0, keepdims=True)


def packed_max(values):
    folded = jnp.max(values.reshape(-1, 16, values.shape[-1]), axis=0)
    return row_max(folded.astype(jnp.float32))


def first_pass_kernel(count, ids_ref, values_ref, *refs):
    row_out, col_out, blocks = refs[:2], refs[2:6], refs[6]
    arrived, row_acc, col_acc = refs[7:]
    mask, across = col_mask(), row_mask()
    groups = values_ref.shape[0] // FIRST_GROUP
    for index in range(min(AHEAD, groups)):
        block_copy(index, values_ref, blocks, arrived).start()
    for acc in (row_acc, col_acc):
        acc[...] = jnp.zeros_like(acc)

    def before(index):
        block_copy(index, values_ref, blocks, arrived).wait()

        @pl.when(index + AHEAD < groups)
        def _():
            block_copy(index + AHEAD, values_ref, blocks, arrived).start()

    def visit(slots, ids):
        sizes = [jnp.abs(blocks[slot]) for slot in slots]
        return [(packed_max(size.T), packed_max(size)) for size in sizes]

    def finish(row, col, terms):
        add_row(row_acc, row_place(row, count, across), terms[0], jnp.maximum)
        add_row(col_acc, col_place(col, count, mask), terms[1], jnp.maximum)

    for_slots(ids_ref, visit, finish, FIRST_GROUP, before)
    store_pieces(row_acc, row_out, count)
    store_pieces(col_acc, col_out, count)


def first_product_kernel(count, ids_ref, blocks, dual_ref, *refs):
    product_out, turned, product_acc = refs[:4], refs[4], refs[5]
    mask = col_mask()
    product_acc[...] = jnp.zeros_like(product_acc)

    def visit(slots, ids):
        found = [blocks[slot] for slot in slots]
        for slot, block in zip(slots, found):
            turned[slot] = block.T
        return product_terms(dual_ref, [row for row, _ in ids], found)

    def finish(row, col, term):
        add_row(product_acc, col_place(col, count, mask), term, jnp.add)

    for_slots(ids_ref, visit, finish)
    store_pieces(product_acc, product_out, count)


def second_pass_kernel(count, ids_ref, blocks, *refs):
    row_in, col_in, row_out, col_out = refs[:2], refs[2:6], refs[6:8], refs[8:12]
    row_scale, col_scale, row_acc, col_acc = refs[12:]
    mask, across = col_mask(), row_mask()
    size = count // CHUNKS
    row_acc[...] = jnp.zeros_like(row_acc)
    col_acc[...] = jnp.zeros_like(col_acc)
    for place in range(CHUNKS):
        piece, part = piece_chunk(row_in, place, size)
        row_scale[chunk_rows(place ^ across, size), :] = lax.rsqrt(piece[part, :] + SMALL_EPS)
        piece, part = piece_chunk(col_in, place, size)
        col_scale[chunk_rows(place ^ mask, size), :] = lax.rsqrt(piece[part, :] + SMALL_EPS)
    width = blocks.shape[-1]
    square = (width, width)
    diagonal = lax.broadcasted_iota(jnp.int32, square, 0) == lax.broadcasted_iota(
        jnp.int32, square, 1
    )
    diagonal = diagonal.astype(jnp.float32).astype(jnp.bfloat16)

    def peaks(row, col, slot):
        sizes = jnp.abs(blocks[slot])
        by_col = sizes.astype(jnp.float32) * one_row(col_scale, col)
        scale = one_row(row_scale, row)
        high = scale.astype(jnp.bfloat16)
        low = (scale - high.astype(jnp.float32)).astype(jnp.bfloat16)
        by_row = jnp.dot(
            jnp.concatenate([diagonal * high, diagonal * low], axis=1),
            jnp.concatenate([sizes, sizes], axis=0),
            preferred_element_type=jnp.float32,
        )
        return row_max(by_col.T), row_max(by_row)

    def visit(slots, ids):
        return [peaks(row, col, slot) for slot, (row, col) in zip(slots, ids)]

    def finish(row, col, terms):
        add_row(row_acc, row_place(row, count, across), terms[0], jnp.maximum)
        add_row(col_acc, col_place(col, count, mask), terms[1], jnp.maximum)

    for_slots(ids_ref, visit, finish)
    for place in range(CHUNKS):
        part = pl.ds(place * size, size)
        piece, inside = piece_chunk(row_out, place, size)
        piece[inside, :] = row_acc[part, :] * row_scale[chunk_rows(place ^ across, size), :]
        piece, inside = piece_chunk(col_out, place, size)
        piece[inside, :] = col_acc[part, :] * col_scale[chunk_rows(place ^ mask, size), :]


def row_scale_kernel(count, near, far, scale_ref, vector_ref, new_scale, squares):
    across = row_mask()
    size = count // CHUNKS
    sums = []
    for place in range(CHUNKS):
        part = chunk_rows(place ^ across, size)
        piece, inside = piece_chunk((near, far), place, size)
        scale = scale_ref[part, :] * lax.rsqrt(piece[inside, :] + SMALL_EPS)
        new_scale[part, :] = scale
        scaled = scale * vector_ref[part, :]
        sums.append(fold_rows(scaled * scaled))
    half = CHUNKS // 2
    squares[...] = tree_sum(sums[:half]) + tree_sum(sums[half:])


def col_scale_kernel(count, *refs):
    pieces, (scale_ref, vector_ref, new_scale, squares, demand_squares) = refs[:4], refs[4:]
    mask = col_mask()
    size = count // CHUNKS
    sums = []
    for place in range(CHUNKS):
        part = chunk_rows(place ^ mask, size)
        piece, inside = piece_chunk(pieces, place, size)
        scale = scale_ref[part, :] * lax.rsqrt(piece[inside, :] + SMALL_EPS)
        new_scale[part, :] = scale
        scaled = scale * vector_ref[part, :]
        sums.append(fold_rows(scaled * scaled))
    squares[...] = tree_sum(sums)
    tail = pl.ds(count // QUARTERS, 8)
    demand_squares[...] = tree_sum([piece[tail, :] for piece in pieces])


def norm_ratio(cost_squares, demand_squares):
    cost_total = jnp.sum(cost_squares[...], keepdims=True)
    demand_total = jnp.sum(demand_squares[...], keepdims=True)
    return jnp.sqrt(cost_total + SMALL_EPS) / jnp.sqrt(demand_total + SMALL_EPS)


def forward_kernel(count, first, last, ids_ref, turned, *refs):
    product, refs = refs[:4], refs[4:]
    scale_ref, cost_ref, low_ref, high_ref, kind_ref, primal_ref = refs[:6]
    cost_squares, demand_squares, primal_out = refs[6:9]
    row_out, refs = refs[9:11], refs[11:]
    shifted, row_acc = refs[:2]
    moved_ref = primal_out
    if last:
        moved_ref, written = refs[2:]
    mask, across = col_mask(), row_mask()
    size = count // CHUNKS
    row_acc[...] = jnp.zeros_like(row_acc)
    primal_step = STEP_SCALE / norm_ratio(cost_squares, demand_squares)
    for place in range(CHUNKS):
        part = chunk_rows(place ^ mask, size)
        piece, inside = piece_chunk(product, place, size, product[0].shape[0] - count // QUARTERS)
        scale = scale_ref[part, :]
        inverse = 1.0 / scale
        primal = primal_ref[part, :]
        if first:
            primal = primal * inverse
        gradient = scale * piece[inside, :]
        moved = primal - primal_step * (scale * cost_ref[part, :] - gradient)
        kind = kind_ref[part, :]
        moved = jnp.where(
            (kind == 1) | (kind == 3), jnp.maximum(moved, low_ref[part, :] * inverse), moved
        )
        moved = jnp.where(
            (kind == 2) | (kind == 3), jnp.minimum(moved, high_ref[part, :] * inverse), moved
        )
        shifted[part, :] = scale * (2.0 * moved - primal)
        moved_ref[part, :] = scale * moved if last else moved

    if last:
        copy_out = pltpu.make_async_copy(moved_ref, primal_out, written)
        copy_out.start()

    def visit(slots, ids):
        return product_terms(shifted, [col for _, col in ids], [turned[slot] for slot in slots])

    def finish(row, col, term):
        add_row(row_acc, row_place(row, count, across), term, jnp.add)

    for_slots(ids_ref, visit, finish)
    store_pieces(row_acc, row_out, count)
    if last:
        copy_out.wait()


def next_dual(first, image, inside, scale, demand, dual, dual_step):
    if first:
        dual = dual / scale
    row_image = scale * image[inside, :]
    return jnp.maximum(dual + dual_step * (scale * demand - row_image), 0.0)


def transposed_kernel(count, first, ids_ref, blocks, *refs):
    image, refs = refs[:2], refs[2:]
    scale_ref, demand_ref, dual_ref, cost_squares, demand_squares, dual_out = refs[:6]
    product_out, (weights, product_acc) = refs[6:10], refs[10:]
    mask, across = col_mask(), row_mask()
    size = count // CHUNKS
    product_acc[...] = jnp.zeros_like(product_acc)
    dual_step = STEP_SCALE * norm_ratio(cost_squares, demand_squares)
    for place in range(CHUNKS):
        part = chunk_rows(place ^ across, size)
        piece, inside = piece_chunk(image, place, size)
        scale = scale_ref[part, :]
        dual = next_dual(
            first, piece, inside, scale, demand_ref[part, :], dual_ref[part, :], dual_step
        )
        dual_out[part, :] = dual
        weights[part, :] = scale * dual

    def visit(slots, ids):
        return product_terms(weights, [row for row, _ in ids], [blocks[slot] for slot in slots])

    def finish(row, col, term):
        add_row(product_acc, col_place(col, count, mask), term, jnp.add)

    for_slots(ids_ref, visit, finish)
    store_pieces(product_acc, product_out, count)


def last_dual_kernel(count, first, *refs):
    image, refs = refs[:2], refs[2:]
    scale_ref, demand_ref, dual_ref, cost_squares, demand_squares, dual_out = refs
    across = row_mask()
    size = count // CHUNKS
    dual_step = STEP_SCALE * norm_ratio(cost_squares, demand_squares)
    for place in range(CHUNKS):
        part = chunk_rows(place ^ across, size)
        piece, inside = piece_chunk(image, place, size)
        scale = scale_ref[part, :]
        dual = next_dual(
            first, piece, inside, scale, demand_ref[part, :], dual_ref[part, :], dual_step
        )
        dual_out[part, :] = scale * dual


def vectors(*row_counts):
    return [jax.ShapeDtypeStruct((rows, 128), jnp.float32) for rows in row_counts]


def call_plain(kernel, operands, out_shape):
    return pl.pallas_call(
        kernel,
        out_shape=out_shape,
        in_specs=[pl.BlockSpec(memory_space=pltpu.VMEM)] * len(operands),
        out_specs=[pl.BlockSpec(memory_space=pltpu.VMEM)] * len(out_shape),
        compiler_params=pltpu.CompilerParams(vmem_limit_bytes=SMALL_VMEM),
    )(*operands)


def call_blocks(kernel, ids, values, operands, out_shape, scratch, first=False, last=False):
    width = values.shape[1]
    scratch_shapes = [pltpu.VMEM((rows, width), jnp.float32) for rows in scratch]
    if first:
        arrivals = pltpu.SemaphoreType.DMA((values.shape[0] // FIRST_GROUP,))
        scratch_shapes = [arrivals] + scratch_shapes
    out_specs = [pl.BlockSpec(memory_space=pltpu.VMEM)] * len(out_shape)
    if last:
        out_specs[0] = pl.BlockSpec(memory_space=pl.ANY)
        scratch_shapes = scratch_shapes + [
            pltpu.VMEM(out_shape[0].shape, out_shape[0].dtype),
            pltpu.SemaphoreType.DMA,
        ]
    return pl.pallas_call(
        kernel,
        out_shape=out_shape,
        in_specs=[pl.BlockSpec(memory_space=pltpu.SMEM)]
        + [pl.BlockSpec(memory_space=pl.ANY if first else pltpu.VMEM)]
        + [pl.BlockSpec(memory_space=pltpu.VMEM)] * len(operands),
        out_specs=out_specs,
        scratch_shapes=scratch_shapes,
        compiler_params=pltpu.CompilerParams(
            vmem_limit_bytes=FIRST_VMEM if first else BLOCK_VMEM
        ),
        cost_estimate=pl.CostEstimate(
            flops=2 * values.size, bytes_accessed=2 * values.size, transcendentals=0
        ),
    )(ids, values, *operands)


def swap(vector, axis, size, bit):
    return lax.ppermute(vector, axis, [(i, i ^ bit) for i in range(size)])


def after(values, *earlier):
    return lax.optimization_barrier((values, earlier))[0]


def halve_rows(pieces, groups, combine):
    near, far = pieces
    return combine(near, swap(far, "col", groups, ROW_HALVING))


def exchange_rows(near, groups, combine):
    bit = 1
    while bit < groups:
        if bit != ROW_HALVING:
            near = combine(near, swap(near, "col", groups, bit))
        bit *= 2
    return near


def join_rows(near, groups):
    return [near, swap(near, "col", groups, ROW_HALVING)]


def scatter_cols(pieces, groups, combine, tie=()):
    diagonal = swap(pieces[3], "row", groups, 3)
    first, second = after((pieces[1], pieces[2]), *tie) if tie else pieces[1:3]
    first, second = swap(first, "row", groups, 1), swap(second, "row", groups, 2)
    return combine(combine(pieces[0], first), combine(second, diagonal))


def exchange_cols(piece, groups, combine):
    bit = QUARTERS
    while bit < groups:
        piece = combine(piece, swap(piece, "row", groups, bit))
        bit *= 2
    return piece


def gather_cols(piece, groups):
    diagonal = swap(piece, "row", groups, 3)
    return [piece, swap(piece, "row", groups, 1), swap(piece, "row", groups, 2), diagonal]


def sum_cols(vector, groups):
    parts = [vector] + [swap(vector, "col", groups, mask) for mask in range(1, groups)]
    return tree_sum(parts)


def per_device(
    row_groups,
    col_groups,
    block_values,
    block_rows,
    block_cols,
    cost_vec,
    demand,
    lower,
    upper,
    bound_kind,
    primal_start,
    dual_start,
):
    values = block_values[0, 0]
    width = values.shape[1]
    ids = jnp.concatenate([block_rows[0, 0], block_cols[0, 0]])
    row_length, col_length = demand.shape[0], cost_vec.shape[0]
    cost_vec, demand, lower, upper, bound_kind, primal_start, dual_start = [
        v.reshape(-1, width)
        for v in (cost_vec, demand, lower, upper, bound_kind, primal_start, dual_start)
    ]
    count = demand.shape[0]
    half, quarter, spare = count // 2, count // QUARTERS, count + 8
    row_pieces, col_pieces = vectors(half, half), vectors(*[quarter] * QUARTERS)
    whole = vectors(count)
    squares = vectors(8)

    def over_col(pieces, combine):
        near = exchange_rows(halve_rows(pieces, col_groups, combine), col_groups, combine)
        return join_rows(near, col_groups)

    def over_row(pieces, combine):
        share = scatter_cols(pieces, row_groups, combine)
        return gather_cols(exchange_cols(share, row_groups, combine), row_groups)

    tile = lax.broadcasted_iota(jnp.int32, (quarter + 8, width), 0)

    def mixed(a, b):
        return jnp.where(tile < quarter, jnp.maximum(a, b), a + b)

    block_shape = jax.ShapeDtypeStruct(values.shape, values.dtype)
    out = call_blocks(
        functools.partial(first_pass_kernel, count),
        ids,
        values,
        [],
        row_pieces + col_pieces + [block_shape],
        [spare] * 2,
        first=True,
    )
    blocks = out[6]
    near = halve_rows(out[:2], col_groups, jnp.maximum)
    *product_pieces, turned = call_blocks(
        functools.partial(first_product_kernel, count),
        ids,
        blocks,
        [after(dual_start, near)],
        col_pieces + [block_shape],
        [spare],
    )
    share = scatter_cols(out[2:6], row_groups, jnp.maximum, (near,))
    near = exchange_rows(near, col_groups, jnp.maximum)
    row_peaks = join_rows(near, col_groups)
    product = scatter_cols(after(product_pieces, near), row_groups, jnp.add)
    share = after(exchange_cols(share, row_groups, jnp.maximum), product_pieces)
    row_peaks, col_peaks = after((row_peaks, gather_cols(share, row_groups)), product)
    product = exchange_cols(product, row_groups, jnp.add)
    out = call_blocks(
        functools.partial(second_pass_kernel, count),
        ids,
        blocks,
        row_peaks + col_peaks,
        row_pieces + col_pieces + whole + whole,
        [spare] * 2,
    )
    row_scale, col_scale = out[6:]
    out, product = lax.optimization_barrier((out, product))
    near = halve_rows(out[:2], col_groups, jnp.maximum)
    share = scatter_cols(out[2:6], row_groups, jnp.maximum, (near,))
    row_peaks = join_rows(exchange_rows(near, col_groups, jnp.maximum), col_groups)
    row_scale, demand_squares = call_plain(
        functools.partial(row_scale_kernel, count),
        row_peaks + [row_scale, demand],
        whole + squares,
    )
    share = jnp.concatenate([share, demand_squares], axis=0)
    share = exchange_cols(share, row_groups, mixed)
    gathered = gather_cols(jnp.concatenate([share, product], axis=0), row_groups)
    col_scale, cost_squares, demand_squares = call_plain(
        functools.partial(col_scale_kernel, count),
        gathered + [col_scale, cost_vec],
        whole + squares + squares,
    )
    norms = [sum_cols(cost_squares, col_groups), demand_squares]

    def forward(first, last, product, primal):
        out = call_blocks(
            functools.partial(forward_kernel, count, first, last),
            ids,
            turned,
            product + [col_scale, cost_vec, lower, upper, bound_kind, primal] + norms,
            whole + row_pieces,
            [count, spare],
            last=last,
        )
        return out[0], over_col(out[1:], jnp.add)

    primal, image = forward(True, False, gathered, primal_start)
    out = call_blocks(
        functools.partial(transposed_kernel, count, True),
        ids,
        blocks,
        image + [row_scale, demand, dual_start] + norms,
        whole + col_pieces,
        [count, spare],
    )
    dual, product = out[0], over_row(out[1:], jnp.add)
    primal, image = forward(False, True, product, primal)
    (dual,) = call_plain(
        functools.partial(last_dual_kernel, count, False),
        image + [row_scale, demand, dual] + norms,
        whole,
    )
    return primal.reshape(col_length), dual.reshape(row_length)


def solution(mesh):
    def body(*args):
        return per_device(mesh.shape["row"], mesh.shape["col"], *args)

    return jax.shard_map(
        body,
        mesh=mesh,
        in_specs=(
            P("row", "col", None, None, None),
            P("row", "col", None),
            P("row", "col", None),
            P("col"),
            P("row"),
            P("col"),
            P("col"),
            P("col"),
            P("col"),
            P("row"),
        ),
        out_specs=(P("col"), P("row")),
        check_vma=False,
    )
```

```python
import functools

import jax
import jax.numpy as jnp
from jax import lax
from jax.experimental import pallas as pl
from jax.experimental.pallas import tpu as pltpu
from jax.sharding import PartitionSpec as P

SMALL_EPS = 1e-06
STEP_SCALE = 0.3

CHUNKS = 8
FIRST_GROUP = 32
GROUP = 64
AHEAD = 3
ROW_HALVING = 1
QUARTERS = 4
FIRST_VMEM = 44 * 1024 * 1024
BLOCK_VMEM = 16 * 1024 * 1024
SMALL_VMEM = 8 * 1024 * 1024


def bit_of(index, bit):
    return jnp.where((index & bit) != 0, 1, 0)


def row_mask():
    return bit_of(lax.axis_index("col"), ROW_HALVING) * (CHUNKS // 2)


def col_mask():
    return (lax.axis_index("row") & (QUARTERS - 1)) * (CHUNKS // QUARTERS)


def col_place(tile, count, mask):
    return jnp.where(tile < 0, count, tile ^ (mask * (count // CHUNKS)))


def row_place(tile, count, mask):
    return jnp.where(tile < 0, count, tile ^ (mask * (count // CHUNKS)))


def chunk_rows(chunk, size):
    return pl.ds(pl.multiple_of(chunk * size, size), size)


def piece_chunk(pieces, place, size, offset=0):
    per_piece = CHUNKS // len(pieces)
    start = offset + (place % per_piece) * size
    return pieces[place // per_piece], pl.ds(start, size)


def store_pieces(acc, pieces, count):
    size = count // len(pieces)
    for index, piece in enumerate(pieces):
        piece[...] = acc[pl.ds(index * size, size), :]


def add_row(acc, place, term, combine):
    acc[pl.ds(place, 1), :] = combine(acc[pl.ds(place, 1), :], term)


def one_row(ref, tile):
    return ref[pl.ds(jnp.maximum(tile, 0), 1), :]


def tree_sum(parts):
    while len(parts) > 1:
        parts = [parts[i] + parts[i + 1] for i in range(0, len(parts), 2)]
    return parts[0]


def fold_rows(values):
    return jnp.sum(values.reshape(-1, 8, values.shape[-1]), axis=0)


def block_copy(index, values_ref, blocks, arrived):
    part = pl.ds(pl.multiple_of(index * FIRST_GROUP, FIRST_GROUP), FIRST_GROUP)
    return pltpu.make_async_copy(values_ref.at[part], blocks.at[part], arrived.at[index])


def for_slots(ids_ref, visit, finish, group=GROUP, before=None):
    count = ids_ref.shape[0] // 2

    def step(index, carry):
        if before is not None:
            before(index)
        slots = [index * group + inner for inner in range(group)]
        ids = [(ids_ref[slot], ids_ref[count + slot]) for slot in slots]
        terms = visit(slots, ids)
        for (row, col), term in zip(ids, terms):
            finish(row, col, term)
        return carry

    lax.fori_loop(0, count // group, step, 0)


def product_terms(vector_ref, tiles, blocks):
    width = vector_ref.shape[1]
    place = lax.broadcasted_iota(jnp.int32, (8, width), 0)
    terms = []
    for start in range(0, len(tiles), 4):
        rows = [one_row(vector_ref, tile) for tile in tiles[start : start + 4]]
        left = jnp.where(place == 0, rows[0], jnp.where(place == 1, rows[1], 0.0))
        right = jnp.where(place == 2, rows[2], jnp.where(place == 3, rows[3], 0.0))
        quad = blocks[start : start + 4]
        found = jnp.dot(
            jnp.concatenate([left, right], axis=1).astype(jnp.bfloat16),
            jnp.concatenate(
                [jnp.concatenate(quad[:2], axis=1), jnp.concatenate(quad[2:], axis=1)], axis=0
            ),
            preferred_element_type=jnp.float32,
        )
        for index in range(4):
            side = (index % 2) * width
            terms.append(found[index : index + 1, side : side + width])
    return terms


def row_max(values):
    return jnp.max(values, axis=0, keepdims=True)


def packed_max(values):
    folded = jnp.max(values.reshape(-1, 16, values.shape[-1]), axis=0)
    return row_max(folded.astype(jnp.float32))


def first_pass_kernel(count, ids_ref, values_ref, *refs):
    row_out, col_out, blocks = refs[:2], refs[2:6], refs[6]
    arrived, row_acc, col_acc = refs[7:]
    mask, across = col_mask(), row_mask()
    groups = values_ref.shape[0] // FIRST_GROUP
    for index in range(min(AHEAD, groups)):
        block_copy(index, values_ref, blocks, arrived).start()
    for acc in (row_acc, col_acc):
        acc[...] = jnp.zeros_like(acc)

    def before(index):
        block_copy(index, values_ref, blocks, arrived).wait()

        @pl.when(index + AHEAD < groups)
        def _():
            block_copy(index + AHEAD, values_ref, blocks, arrived).start()

    def visit(slots, ids):
        sizes = [jnp.abs(blocks[slot]) for slot in slots]
        return [(packed_max(size.T), packed_max(size)) for size in sizes]

    def finish(row, col, terms):
        add_row(row_acc, row_place(row, count, across), terms[0], jnp.maximum)
        add_row(col_acc, col_place(col, count, mask), terms[1], jnp.maximum)

    for_slots(ids_ref, visit, finish, FIRST_GROUP, before)
    store_pieces(row_acc, row_out, count)
    store_pieces(col_acc, col_out, count)


def first_product_kernel(count, ids_ref, blocks, dual_ref, *refs):
    product_out, turned, product_acc = refs[:4], refs[4], refs[5]
    mask = col_mask()
    product_acc[...] = jnp.zeros_like(product_acc)

    def visit(slots, ids):
        found = [blocks[slot] for slot in slots]
        for slot, block in zip(slots, found):
            turned[slot] = block.T
        return product_terms(dual_ref, [row for row, _ in ids], found)

    def finish(row, col, term):
        add_row(product_acc, col_place(col, count, mask), term, jnp.add)

    for_slots(ids_ref, visit, finish)
    store_pieces(product_acc, product_out, count)


def second_cols_kernel(count, ids_ref, blocks, *refs):
    row_in, product_in, col_out, row_scale, col_acc = (
        refs[:2], refs[2:6], refs[6:10], refs[10], refs[11]
    )
    mask, across = col_mask(), row_mask()
    size = count // CHUNKS
    col_acc[...] = jnp.zeros_like(col_acc)
    for place in range(CHUNKS):
        piece, part = piece_chunk(row_in, place, size)
        row_scale[chunk_rows(place ^ across, size), :] = lax.rsqrt(piece[part, :] + SMALL_EPS)
    width = blocks.shape[-1]
    square = (width, width)
    diagonal = lax.broadcasted_iota(jnp.int32, square, 0) == lax.broadcasted_iota(
        jnp.int32, square, 1
    )
    diagonal = diagonal.astype(jnp.float32).astype(jnp.bfloat16)

    def peaks(row, slot):
        sizes = jnp.abs(blocks[slot])
        scale = one_row(row_scale, row)
        high = scale.astype(jnp.bfloat16)
        low = (scale - high.astype(jnp.float32)).astype(jnp.bfloat16)
        by_row = jnp.dot(
            jnp.concatenate([diagonal * high, diagonal * low], axis=1),
            jnp.concatenate([sizes, sizes], axis=0),
            preferred_element_type=jnp.float32,
        )
        return row_max(by_row)

    def visit(slots, ids):
        return [peaks(row, slot) for slot, (row, _) in zip(slots, ids)]

    def finish(row, col, term):
        add_row(col_acc, col_place(col, count, mask), term, jnp.maximum)

    for_slots(ids_ref, visit, finish)
    quarter = count // QUARTERS
    for index, (piece, product) in enumerate(zip(col_out, product_in)):
        piece[pl.ds(0, quarter), :] = col_acc[pl.ds(index * quarter, quarter), :]
        piece[pl.ds(quarter, quarter), :] = product[...]


def second_rows_kernel(count, ids_ref, blocks, *refs):
    col_in, row_out, col_scale, row_acc = refs[:4], refs[4:6], refs[6], refs[7]
    mask, across = col_mask(), row_mask()
    size = count // CHUNKS
    row_acc[...] = jnp.zeros_like(row_acc)
    for place in range(CHUNKS):
        piece, part = piece_chunk(col_in, place, size)
        col_scale[chunk_rows(place ^ mask, size), :] = lax.rsqrt(piece[part, :] + SMALL_EPS)

    def peaks(col, slot):
        by_col = jnp.abs(blocks[slot]).astype(jnp.float32) * one_row(col_scale, col)
        return row_max(by_col.T)

    def visit(slots, ids):
        return [peaks(col, slot) for slot, (_, col) in zip(slots, ids)]

    def finish(row, col, term):
        add_row(row_acc, row_place(row, count, across), term, jnp.maximum)

    for_slots(ids_ref, visit, finish)
    store_pieces(row_acc, row_out, count)


def next_scale(scale, piece, inside):
    return scale * lax.rsqrt(scale * piece[inside, :] + SMALL_EPS)


def row_scale_kernel(count, near, far, scale_ref, vector_ref, new_scale, squares):
    across = row_mask()
    size = count // CHUNKS
    sums = []
    for place in range(CHUNKS):
        part = chunk_rows(place ^ across, size)
        piece, inside = piece_chunk((near, far), place, size)
        scale = next_scale(scale_ref[part, :], piece, inside)
        new_scale[part, :] = scale
        scaled = scale * vector_ref[part, :]
        sums.append(fold_rows(scaled * scaled))
    half = CHUNKS // 2
    squares[...] = tree_sum(sums[:half]) + tree_sum(sums[half:])


def col_scale_kernel(count, *refs):
    pieces, (scale_ref, vector_ref, new_scale, squares) = refs[:4], refs[4:]
    mask = col_mask()
    size = count // CHUNKS
    sums = []
    for place in range(CHUNKS):
        part = chunk_rows(place ^ mask, size)
        piece, inside = piece_chunk(pieces, place, size)
        scale = next_scale(scale_ref[part, :], piece, inside)
        new_scale[part, :] = scale
        scaled = scale * vector_ref[part, :]
        sums.append(fold_rows(scaled * scaled))
    squares[...] = tree_sum(sums)


def norm_ratio(cost_squares, demand_squares):
    cost_total = jnp.sum(cost_squares[...], keepdims=True)
    demand_total = jnp.sum(demand_squares[...], keepdims=True)
    return jnp.sqrt(cost_total + SMALL_EPS) / jnp.sqrt(demand_total + SMALL_EPS)


def forward_kernel(count, first, last, ids_ref, turned, *refs):
    product, refs = refs[:4], refs[4:]
    scale_ref, cost_ref, low_ref, high_ref, kind_ref, primal_ref = refs[:6]
    cost_squares, demand_squares, primal_out = refs[6:9]
    row_out, refs = refs[9:11], refs[11:]
    shifted, row_acc = refs[:2]
    moved_ref = primal_out
    if last:
        moved_ref, written = refs[2:]
    mask, across = col_mask(), row_mask()
    size = count // CHUNKS
    row_acc[...] = jnp.zeros_like(row_acc)
    primal_step = STEP_SCALE / norm_ratio(cost_squares, demand_squares)
    for place in range(CHUNKS):
        part = chunk_rows(place ^ mask, size)
        piece, inside = piece_chunk(product, place, size, product[0].shape[0] - count // QUARTERS)
        scale = scale_ref[part, :]
        inverse = 1.0 / scale
        primal = primal_ref[part, :]
        if first:
            primal = primal * inverse
        gradient = scale * piece[inside, :]
        moved = primal - primal_step * (scale * cost_ref[part, :] - gradient)
        kind = kind_ref[part, :]
        moved = jnp.where(
            (kind == 1) | (kind == 3), jnp.maximum(moved, low_ref[part, :] * inverse), moved
        )
        moved = jnp.where(
            (kind == 2) | (kind == 3), jnp.minimum(moved, high_ref[part, :] * inverse), moved
        )
        shifted[part, :] = scale * (2.0 * moved - primal)
        moved_ref[part, :] = scale * moved if last else moved

    if last:
        copy_out = pltpu.make_async_copy(moved_ref, primal_out, written)
        copy_out.start()

    def visit(slots, ids):
        return product_terms(shifted, [col for _, col in ids], [turned[slot] for slot in slots])

    def finish(row, col, term):
        add_row(row_acc, row_place(row, count, across), term, jnp.add)

    for_slots(ids_ref, visit, finish)
    store_pieces(row_acc, row_out, count)
    if last:
        copy_out.wait()


def next_dual(first, image, inside, scale, demand, dual, dual_step):
    if first:
        dual = dual / scale
    row_image = scale * image[inside, :]
    return jnp.maximum(dual + dual_step * (scale * demand - row_image), 0.0)


def transposed_kernel(count, first, ids_ref, blocks, *refs):
    image, refs = refs[:2], refs[2:]
    scale_ref, demand_ref, dual_ref, cost_squares, demand_squares, dual_out = refs[:6]
    product_out, (weights, product_acc) = refs[6:10], refs[10:]
    mask, across = col_mask(), row_mask()
    size = count // CHUNKS
    product_acc[...] = jnp.zeros_like(product_acc)
    dual_step = STEP_SCALE * norm_ratio(cost_squares, demand_squares)
    for place in range(CHUNKS):
        part = chunk_rows(place ^ across, size)
        piece, inside = piece_chunk(image, place, size)
        scale = scale_ref[part, :]
        dual = next_dual(
            first, piece, inside, scale, demand_ref[part, :], dual_ref[part, :], dual_step
        )
        dual_out[part, :] = dual
        weights[part, :] = scale * dual

    def visit(slots, ids):
        return product_terms(weights, [row for row, _ in ids], [blocks[slot] for slot in slots])

    def finish(row, col, term):
        add_row(product_acc, col_place(col, count, mask), term, jnp.add)

    for_slots(ids_ref, visit, finish)
    store_pieces(product_acc, product_out, count)


def last_dual_kernel(count, first, *refs):
    image, refs = refs[:2], refs[2:]
    scale_ref, demand_ref, dual_ref, cost_squares, demand_squares, dual_out = refs
    across = row_mask()
    size = count // CHUNKS
    dual_step = STEP_SCALE * norm_ratio(cost_squares, demand_squares)
    for place in range(CHUNKS):
        part = chunk_rows(place ^ across, size)
        piece, inside = piece_chunk(image, place, size)
        scale = scale_ref[part, :]
        dual = next_dual(
            first, piece, inside, scale, demand_ref[part, :], dual_ref[part, :], dual_step
        )
        dual_out[part, :] = scale * dual


def vectors(*row_counts):
    return [jax.ShapeDtypeStruct((rows, 128), jnp.float32) for rows in row_counts]


def call_plain(kernel, operands, out_shape):
    return pl.pallas_call(
        kernel,
        out_shape=out_shape,
        in_specs=[pl.BlockSpec(memory_space=pltpu.VMEM)] * len(operands),
        out_specs=[pl.BlockSpec(memory_space=pltpu.VMEM)] * len(out_shape),
        compiler_params=pltpu.CompilerParams(vmem_limit_bytes=SMALL_VMEM),
    )(*operands)


def call_blocks(kernel, ids, values, operands, out_shape, scratch, first=False, last=False):
    width = values.shape[1]
    scratch_shapes = [pltpu.VMEM((rows, width), jnp.float32) for rows in scratch]
    if first:
        arrivals = pltpu.SemaphoreType.DMA((values.shape[0] // FIRST_GROUP,))
        scratch_shapes = [arrivals] + scratch_shapes
    out_specs = [pl.BlockSpec(memory_space=pltpu.VMEM)] * len(out_shape)
    if last:
        out_specs[0] = pl.BlockSpec(memory_space=pl.ANY)
        scratch_shapes = scratch_shapes + [
            pltpu.VMEM(out_shape[0].shape, out_shape[0].dtype),
            pltpu.SemaphoreType.DMA,
        ]
    return pl.pallas_call(
        kernel,
        out_shape=out_shape,
        in_specs=[pl.BlockSpec(memory_space=pltpu.SMEM)]
        + [pl.BlockSpec(memory_space=pl.ANY if first else pltpu.VMEM)]
        + [pl.BlockSpec(memory_space=pltpu.VMEM)] * len(operands),
        out_specs=out_specs,
        scratch_shapes=scratch_shapes,
        compiler_params=pltpu.CompilerParams(
            vmem_limit_bytes=FIRST_VMEM if first else BLOCK_VMEM
        ),
        cost_estimate=pl.CostEstimate(
            flops=2 * values.size, bytes_accessed=2 * values.size, transcendentals=0
        ),
    )(ids, values, *operands)


def swap(vector, axis, size, bit):
    return lax.ppermute(vector, axis, [(i, i ^ bit) for i in range(size)])


def after(values, *earlier):
    return lax.optimization_barrier((values, earlier))[0]


def halve_rows(pieces, groups, combine):
    near, far = pieces
    return combine(near, swap(far, "col", groups, ROW_HALVING))


def exchange_rows(near, groups, combine):
    bit = 1
    while bit < groups:
        if bit != ROW_HALVING:
            near = combine(near, swap(near, "col", groups, bit))
        bit *= 2
    return near


def join_rows(near, groups):
    return [near, swap(near, "col", groups, ROW_HALVING)]


def scatter_cols(pieces, groups, combine, tie=()):
    diagonal = swap(pieces[3], "row", groups, 3)
    first, second = after((pieces[1], pieces[2]), *tie) if tie else pieces[1:3]
    first, second = swap(first, "row", groups, 1), swap(second, "row", groups, 2)
    return combine(combine(pieces[0], first), combine(second, diagonal))


def exchange_cols(piece, groups, combine):
    bit = QUARTERS
    while bit < groups:
        piece = combine(piece, swap(piece, "row", groups, bit))
        bit *= 2
    return piece


def gather_cols(piece, groups):
    diagonal = swap(piece, "row", groups, 3)
    return [piece, swap(piece, "row", groups, 1), swap(piece, "row", groups, 2), diagonal]


def sum_rows(vector, groups):
    vector = exchange_cols(vector, groups, jnp.add)
    return tree_sum([vector] + [swap(vector, "row", groups, mask) for mask in (1, 2, 3)])


def sum_cols(vector, groups):
    parts = [vector] + [swap(vector, "col", groups, mask) for mask in range(1, groups)]
    return tree_sum(parts)


def per_device(
    row_groups,
    col_groups,
    block_values,
    block_rows,
    block_cols,
    cost_vec,
    demand,
    lower,
    upper,
    bound_kind,
    primal_start,
    dual_start,
):
    values = block_values[0, 0]
    width = values.shape[1]
    ids = jnp.concatenate([block_rows[0, 0], block_cols[0, 0]])
    row_length, col_length = demand.shape[0], cost_vec.shape[0]
    cost_vec, demand, lower, upper, bound_kind, primal_start, dual_start = [
        v.reshape(-1, width)
        for v in (cost_vec, demand, lower, upper, bound_kind, primal_start, dual_start)
    ]
    count = demand.shape[0]
    half, quarter, spare = count // 2, count // QUARTERS, count + 8
    row_pieces, col_pieces = vectors(half, half), vectors(*[quarter] * QUARTERS)
    whole = vectors(count)
    squares = vectors(8)

    def over_col(pieces, combine):
        near = exchange_rows(halve_rows(pieces, col_groups, combine), col_groups, combine)
        return join_rows(near, col_groups)

    def over_row(pieces, combine):
        share = scatter_cols(pieces, row_groups, combine)
        return gather_cols(exchange_cols(share, row_groups, combine), row_groups)

    tile = lax.broadcasted_iota(jnp.int32, (2 * quarter, width), 0)

    def mixed(a, b):
        return jnp.where(tile < quarter, jnp.maximum(a, b), a + b)

    block_shape = jax.ShapeDtypeStruct(values.shape, values.dtype)
    out = call_blocks(
        functools.partial(first_pass_kernel, count),
        ids,
        values,
        [],
        row_pieces + col_pieces + [block_shape],
        [spare] * 2,
        first=True,
    )
    blocks = out[6]
    near = halve_rows(out[:2], col_groups, jnp.maximum)
    share = scatter_cols(out[2:6], row_groups, jnp.maximum, (near,))
    row_peaks = join_rows(exchange_rows(near, col_groups, jnp.maximum), col_groups)
    *product_pieces, turned = call_blocks(
        functools.partial(first_product_kernel, count),
        ids,
        blocks,
        [after(dual_start, share)],
        col_pieces + [block_shape],
        [spare],
    )
    share = after(exchange_cols(share, row_groups, jnp.maximum), product_pieces)
    *col_pieces_2, row_scale = call_blocks(
        functools.partial(second_cols_kernel, count),
        ids,
        blocks,
        after(row_peaks, share) + product_pieces,
        vectors(*[2 * quarter] * QUARTERS) + whole,
        [spare],
    )
    col_peaks = gather_cols(share, row_groups)
    share = scatter_cols(after(col_pieces_2, col_peaks), row_groups, mixed)
    near, far, col_scale = call_blocks(
        functools.partial(second_rows_kernel, count),
        ids,
        blocks,
        col_peaks,
        row_pieces + whole,
        [spare],
    )
    near, far = after((near, far), share)
    share = exchange_cols(share, row_groups, mixed)
    row_scale, demand_squares = call_plain(
        functools.partial(row_scale_kernel, count),
        over_col([near, far], jnp.maximum) + [row_scale, demand],
        whole + squares,
    )
    demand_squares = sum_rows(demand_squares, row_groups)
    gathered = gather_cols(share, row_groups)
    col_scale, cost_squares = call_plain(
        functools.partial(col_scale_kernel, count),
        gathered + [col_scale, cost_vec],
        whole + squares,
    )
    norms = [sum_cols(cost_squares, col_groups), demand_squares]

    def forward(first, last, product, primal):
        out = call_blocks(
            functools.partial(forward_kernel, count, first, last),
            ids,
            turned,
            product + [col_scale, cost_vec, lower, upper, bound_kind, primal] + norms,
            whole + row_pieces,
            [count, spare],
            last=last,
        )
        return out[0], over_col(out[1:], jnp.add)

    primal, image = forward(True, False, gathered, primal_start)
    out = call_blocks(
        functools.partial(transposed_kernel, count, True),
        ids,
        blocks,
        image + [row_scale, demand, dual_start] + norms,
        whole + col_pieces,
        [count, spare],
    )
    dual, product = out[0], over_row(out[1:], jnp.add)
    primal, image = forward(False, True, product, primal)
    (dual,) = call_plain(
        functools.partial(last_dual_kernel, count, False),
        image + [row_scale, demand, dual] + norms,
        whole,
    )
    return primal.reshape(col_length), dual.reshape(row_length)


def solution(mesh):
    def body(*args):
        return per_device(mesh.shape["row"], mesh.shape["col"], *args)

    return jax.shard_map(
        body,
        mesh=mesh,
        in_specs=(
            P("row", "col", None, None, None),
            P("row", "col", None),
            P("row", "col", None),
            P("col"),
            P("row"),
            P("col"),
            P("col"),
            P("col"),
            P("col"),
            P("row"),
        ),
        out_specs=(P("col"), P("row")),
        check_vma=False,
    )
```

```python
import functools

import jax
import jax.numpy as jnp
from jax import lax
from jax.experimental import pallas as pl
from jax.experimental.pallas import tpu as pltpu
from jax.sharding import PartitionSpec as P

SMALL_EPS = 1e-06
STEP_SCALE = 0.3

CHUNKS = 8
FIRST_GROUP = 32
GROUP = 64
AHEAD = 3
ROW_HALVING = 1
QUARTERS = 4
FIRST_VMEM = 44 * 1024 * 1024
BLOCK_VMEM = 20 * 1024 * 1024
SMALL_VMEM = 8 * 1024 * 1024


def bit_of(index, bit):
    return jnp.where((index & bit) != 0, 1, 0)


def row_mask():
    return bit_of(lax.axis_index("col"), ROW_HALVING) * (CHUNKS // 2)


def col_mask():
    return (lax.axis_index("row") & (QUARTERS - 1)) * (CHUNKS // QUARTERS)


def col_place(tile, count, mask):
    return jnp.where(tile < 0, count, tile ^ (mask * (count // CHUNKS)))


def row_place(tile, count, mask):
    return jnp.where(tile < 0, count, tile ^ (mask * (count // CHUNKS)))


def chunk_rows(chunk, size):
    return pl.ds(pl.multiple_of(chunk * size, size), size)


def piece_chunk(pieces, place, size):
    per_piece = CHUNKS // len(pieces)
    start = (place % per_piece) * size
    return pieces[place // per_piece], pl.ds(start, size)


def store_pieces(acc, pieces, count):
    size = count // len(pieces)
    for index, piece in enumerate(pieces):
        piece[...] = acc[pl.ds(index * size, size), :]


def add_row(acc, place, term, combine):
    acc[pl.ds(place, 1), :] = combine(acc[pl.ds(place, 1), :], term)


def one_row(ref, tile):
    return ref[pl.ds(jnp.maximum(tile, 0), 1), :]


def tree_of(parts, combine):
    while len(parts) > 1:
        parts = [combine(parts[i], parts[i + 1]) for i in range(0, len(parts), 2)]
    return parts[0]


def tree_sum(parts):
    return tree_of(parts, jnp.add)


def fold_rows(values):
    return jnp.sum(values.reshape(-1, 8, values.shape[-1]), axis=0)


def block_copy(index, values_ref, blocks, arrived):
    part = pl.ds(pl.multiple_of(index * FIRST_GROUP, FIRST_GROUP), FIRST_GROUP)
    return pltpu.make_async_copy(values_ref.at[part], blocks.at[part], arrived.at[index])


def for_slots(ids_ref, visit, finish, group=GROUP, before=None):
    count = ids_ref.shape[0] // 2

    def step(index, carry):
        if before is not None:
            before(index)
        slots = [index * group + inner for inner in range(group)]
        ids = [(ids_ref[slot], ids_ref[count + slot]) for slot in slots]
        terms = visit(slots, ids)
        for (row, col), term in zip(ids, terms):
            finish(row, col, term)
        return carry

    lax.fori_loop(0, count // group, step, 0)


def product_terms(vector_ref, tiles, blocks):
    width = vector_ref.shape[1]
    place = lax.broadcasted_iota(jnp.int32, (8, width), 0)
    terms = []
    for start in range(0, len(tiles), 4):
        rows = [one_row(vector_ref, tile) for tile in tiles[start : start + 4]]
        left = jnp.where(place == 0, rows[0], jnp.where(place == 1, rows[1], 0.0))
        right = jnp.where(place == 2, rows[2], jnp.where(place == 3, rows[3], 0.0))
        quad = blocks[start : start + 4]
        found = jnp.dot(
            jnp.concatenate([left, right], axis=1).astype(jnp.bfloat16),
            jnp.concatenate(
                [jnp.concatenate(quad[:2], axis=1), jnp.concatenate(quad[2:], axis=1)], axis=0
            ),
            preferred_element_type=jnp.float32,
        )
        for index in range(4):
            side = (index % 2) * width
            terms.append(found[index : index + 1, side : side + width])
    return terms


def row_max(values):
    return jnp.max(values, axis=0, keepdims=True)


def packed_max(values):
    folded = jnp.max(values.reshape(-1, 16, values.shape[-1]), axis=0)
    return row_max(folded.astype(jnp.float32))


def first_pass_kernel(count, ids_ref, values_ref, *refs):
    row_out, col_out, blocks = refs[:2], refs[2:6], refs[6]
    arrived, row_acc, col_acc = refs[7:]
    mask, across = col_mask(), row_mask()
    groups = values_ref.shape[0] // FIRST_GROUP
    for index in range(min(AHEAD, groups)):
        block_copy(index, values_ref, blocks, arrived).start()
    for acc in (row_acc, col_acc):
        acc[...] = jnp.zeros_like(acc)

    def before(index):
        block_copy(index, values_ref, blocks, arrived).wait()

        @pl.when(index + AHEAD < groups)
        def _():
            block_copy(index + AHEAD, values_ref, blocks, arrived).start()

    def visit(slots, ids):
        sizes = [jnp.abs(blocks[slot]) for slot in slots]
        return [(packed_max(size.T), packed_max(size)) for size in sizes]

    def finish(row, col, terms):
        add_row(row_acc, row_place(row, count, across), terms[0], jnp.maximum)
        add_row(col_acc, col_place(col, count, mask), terms[1], jnp.maximum)

    for_slots(ids_ref, visit, finish, FIRST_GROUP, before)
    store_pieces(row_acc, row_out, count)
    store_pieces(col_acc, col_out, count)


def first_product_kernel(count, ids_ref, blocks, dual_ref, *refs):
    product_out, turned, product_acc = refs[:4], refs[4], refs[5]
    mask = col_mask()
    product_acc[...] = jnp.zeros_like(product_acc)

    def visit(slots, ids):
        found = [blocks[slot] for slot in slots]
        for slot, block in zip(slots, found):
            turned[slot] = block.T
        return product_terms(dual_ref, [row for row, _ in ids], found)

    def finish(row, col, term):
        add_row(product_acc, col_place(col, count, mask), term, jnp.add)

    for_slots(ids_ref, visit, finish)
    store_pieces(product_acc, product_out, count)


def scaled_peaks(slots, scales, direct, flipped):
    width = direct.shape[-1]
    square = (width, width)
    diagonal = lax.broadcasted_iota(jnp.int32, square, 0) == lax.broadcasted_iota(
        jnp.int32, square, 1
    )
    diagonal = diagonal.astype(jnp.float32).astype(jnp.bfloat16)
    found = []
    for index, (slot, scale) in enumerate(zip(slots, scales)):
        if index % 2:
            scaled = (jnp.abs(flipped[slot]).astype(jnp.float32) * scale).T
        else:
            sizes = jnp.abs(direct[slot])
            high = scale.astype(jnp.bfloat16)
            low = (scale - high.astype(jnp.float32)).astype(jnp.bfloat16)
            scaled = jnp.dot(
                jnp.concatenate([diagonal * high, diagonal * low], axis=1),
                jnp.concatenate([sizes, sizes], axis=0),
                preferred_element_type=jnp.float32,
            )
        found.append(row_max(scaled))
    return found


def second_cols_kernel(count, ids_ref, blocks, turned, *refs):
    row_in, product_in, col_out, row_scale, col_acc = (
        refs[:2], refs[2:6], refs[6:10], refs[10], refs[11]
    )
    mask, across = col_mask(), row_mask()
    size = count // CHUNKS
    col_acc[...] = jnp.zeros_like(col_acc)
    for place in range(CHUNKS):
        piece, part = piece_chunk(row_in, place, size)
        row_scale[chunk_rows(place ^ across, size), :] = lax.rsqrt(piece[part, :] + SMALL_EPS)

    def visit(slots, ids):
        scales = [one_row(row_scale, row) for row, _ in ids]
        return scaled_peaks(slots, scales, blocks, turned)

    def finish(row, col, term):
        add_row(col_acc, col_place(col, count, mask), term, jnp.maximum)

    for_slots(ids_ref, visit, finish)
    quarter = count // QUARTERS
    for index, (piece, product) in enumerate(zip(col_out, product_in)):
        piece[pl.ds(0, quarter), :] = col_acc[pl.ds(index * quarter, quarter), :]
        piece[pl.ds(quarter, quarter), :] = product[...]


def second_rows_kernel(count, ids_ref, blocks, turned, *refs):
    col_in, row_out, col_scale, row_acc = refs[:4], refs[4:6], refs[6], refs[7]
    mask, across = col_mask(), row_mask()
    size = count // CHUNKS
    row_acc[...] = jnp.zeros_like(row_acc)
    for place in range(CHUNKS):
        piece, part = piece_chunk(col_in, place, size)
        col_scale[chunk_rows(place ^ mask, size), :] = lax.rsqrt(piece[part, :] + SMALL_EPS)

    def visit(slots, ids):
        scales = [one_row(col_scale, col) for _, col in ids]
        return scaled_peaks(slots, scales, turned, blocks)

    def finish(row, col, term):
        add_row(row_acc, row_place(row, count, across), term, jnp.maximum)

    for_slots(ids_ref, visit, finish)
    store_pieces(row_acc, row_out, count)


def next_scale(scale, piece, inside):
    return scale * lax.rsqrt(scale * piece[inside, :] + SMALL_EPS)


def row_scale_kernel(count, near, far, scale_ref, vector_ref, new_scale, squares):
    across = row_mask()
    size = count // CHUNKS
    sums = []
    for place in range(CHUNKS):
        part = chunk_rows(place ^ across, size)
        piece, inside = piece_chunk((near, far), place, size)
        scale = next_scale(scale_ref[part, :], piece, inside)
        new_scale[part, :] = scale
        scaled = scale * vector_ref[part, :]
        sums.append(fold_rows(scaled * scaled))
    half = CHUNKS // 2
    squares[...] = tree_sum(sums[:half]) + tree_sum(sums[half:])


def col_scale_kernel(count, *refs):
    pieces, (scale_ref, vector_ref, new_scale, squares) = refs[:4], refs[4:]
    mask = col_mask()
    size = count // CHUNKS
    sums = []
    for place in range(CHUNKS):
        part = chunk_rows(place ^ mask, size)
        piece, inside = piece_chunk(pieces, place, size)
        scale = next_scale(scale_ref[part, :], piece, inside)
        new_scale[part, :] = scale
        scaled = scale * vector_ref[part, :]
        sums.append(fold_rows(scaled * scaled))
    squares[...] = tree_sum(sums)


def norm_ratio(cost_squares, demand_squares):
    cost_total = jnp.sum(cost_squares[...], keepdims=True)
    demand_total = jnp.sum(demand_squares[...], keepdims=True)
    return jnp.sqrt(cost_total + SMALL_EPS) / jnp.sqrt(demand_total + SMALL_EPS)


def forward_kernel(count, first, last, ids_ref, turned, *refs):
    product, refs = refs[:4], refs[4:]
    scale_ref, cost_ref, low_ref, high_ref, kind_ref, primal_ref = refs[:6]
    cost_squares, demand_squares, primal_out = refs[6:9]
    row_out, refs = refs[9:11], refs[11:]
    shifted, row_acc = refs[:2]
    moved_ref = primal_out
    if last:
        moved_ref, written = refs[2:]
    mask, across = col_mask(), row_mask()
    size = count // CHUNKS
    row_acc[...] = jnp.zeros_like(row_acc)
    primal_step = STEP_SCALE / norm_ratio(cost_squares, demand_squares)
    for place in range(CHUNKS):
        part = chunk_rows(place ^ mask, size)
        piece, inside = piece_chunk(product, place, size)
        scale = scale_ref[part, :]
        inverse = 1.0 / scale
        primal = primal_ref[part, :]
        if first:
            primal = primal * inverse
        gradient = scale * piece[inside, :]
        moved = primal - primal_step * (scale * cost_ref[part, :] - gradient)
        kind = kind_ref[part, :]
        moved = jnp.where(
            (kind == 1) | (kind == 3), jnp.maximum(moved, low_ref[part, :] * inverse), moved
        )
        moved = jnp.where(
            (kind == 2) | (kind == 3), jnp.minimum(moved, high_ref[part, :] * inverse), moved
        )
        shifted[part, :] = scale * (2.0 * moved - primal)
        moved_ref[part, :] = scale * moved if last else moved

    if last:
        copy_out = pltpu.make_async_copy(moved_ref, primal_out, written)
        copy_out.start()

    def visit(slots, ids):
        return product_terms(shifted, [col for _, col in ids], [turned[slot] for slot in slots])

    def finish(row, col, term):
        add_row(row_acc, row_place(row, count, across), term, jnp.add)

    for_slots(ids_ref, visit, finish)
    store_pieces(row_acc, row_out, count)
    if last:
        copy_out.wait()


def next_dual(first, image, inside, scale, demand, dual, dual_step):
    if first:
        dual = dual / scale
    row_image = scale * image[inside, :]
    return jnp.maximum(dual + dual_step * (scale * demand - row_image), 0.0)


def transposed_kernel(count, first, ids_ref, blocks, *refs):
    image, refs = refs[:2], refs[2:]
    scale_ref, demand_ref, dual_ref, cost_squares, demand_squares, dual_out = refs[:6]
    product_out, (weights, product_acc) = refs[6:10], refs[10:]
    mask, across = col_mask(), row_mask()
    size = count // CHUNKS
    product_acc[...] = jnp.zeros_like(product_acc)
    dual_step = STEP_SCALE * norm_ratio(cost_squares, demand_squares)
    for place in range(CHUNKS):
        part = chunk_rows(place ^ across, size)
        piece, inside = piece_chunk(image, place, size)
        scale = scale_ref[part, :]
        dual = next_dual(
            first, piece, inside, scale, demand_ref[part, :], dual_ref[part, :], dual_step
        )
        dual_out[part, :] = dual
        weights[part, :] = scale * dual

    def visit(slots, ids):
        return product_terms(weights, [row for row, _ in ids], [blocks[slot] for slot in slots])

    def finish(row, col, term):
        add_row(product_acc, col_place(col, count, mask), term, jnp.add)

    for_slots(ids_ref, visit, finish)
    store_pieces(product_acc, product_out, count)


def last_dual_kernel(count, first, *refs):
    image, refs = refs[:2], refs[2:]
    scale_ref, demand_ref, dual_ref, cost_squares, demand_squares, dual_out = refs
    across = row_mask()
    size = count // CHUNKS
    dual_step = STEP_SCALE * norm_ratio(cost_squares, demand_squares)
    for place in range(CHUNKS):
        part = chunk_rows(place ^ across, size)
        piece, inside = piece_chunk(image, place, size)
        scale = scale_ref[part, :]
        dual = next_dual(
            first, piece, inside, scale, demand_ref[part, :], dual_ref[part, :], dual_step
        )
        dual_out[part, :] = scale * dual


def vectors(*row_counts):
    return [jax.ShapeDtypeStruct((rows, 128), jnp.float32) for rows in row_counts]


def call_plain(kernel, operands, out_shape):
    return pl.pallas_call(
        kernel,
        out_shape=out_shape,
        in_specs=[pl.BlockSpec(memory_space=pltpu.VMEM)] * len(operands),
        out_specs=[pl.BlockSpec(memory_space=pltpu.VMEM)] * len(out_shape),
        compiler_params=pltpu.CompilerParams(vmem_limit_bytes=SMALL_VMEM),
    )(*operands)


def call_blocks(kernel, ids, values, operands, out_shape, scratch, first=False, last=False):
    width = values.shape[1]
    scratch_shapes = [pltpu.VMEM((rows, width), jnp.float32) for rows in scratch]
    if first:
        arrivals = pltpu.SemaphoreType.DMA((values.shape[0] // FIRST_GROUP,))
        scratch_shapes = [arrivals] + scratch_shapes
    out_specs = [pl.BlockSpec(memory_space=pltpu.VMEM)] * len(out_shape)
    if last:
        out_specs[0] = pl.BlockSpec(memory_space=pl.ANY)
        scratch_shapes = scratch_shapes + [
            pltpu.VMEM(out_shape[0].shape, out_shape[0].dtype),
            pltpu.SemaphoreType.DMA,
        ]
    return pl.pallas_call(
        kernel,
        out_shape=out_shape,
        in_specs=[pl.BlockSpec(memory_space=pltpu.SMEM)]
        + [pl.BlockSpec(memory_space=pl.ANY if first else pltpu.VMEM)]
        + [pl.BlockSpec(memory_space=pltpu.VMEM)] * len(operands),
        out_specs=out_specs,
        scratch_shapes=scratch_shapes,
        compiler_params=pltpu.CompilerParams(
            vmem_limit_bytes=FIRST_VMEM if first else BLOCK_VMEM
        ),
        cost_estimate=pl.CostEstimate(
            flops=2 * values.size, bytes_accessed=2 * values.size, transcendentals=0
        ),
    )(ids, values, *operands)


def swap(vector, axis, size, bit):
    return lax.ppermute(vector, axis, [(i, i ^ bit) for i in range(size)])


def after(values, *earlier):
    return lax.optimization_barrier((values, earlier))[0]


def halve_rows(pieces, groups, combine):
    near, far = pieces
    return combine(near, swap(far, "col", groups, ROW_HALVING))


def exchange_rows(near, groups, combine):
    bit = 1
    while bit < groups:
        if bit != ROW_HALVING:
            near = combine(near, swap(near, "col", groups, bit))
        bit *= 2
    return near


def join_rows(near, groups):
    return [near, swap(near, "col", groups, ROW_HALVING)]


def send_quarters(pieces, groups):
    return [swap(pieces[mask], "row", groups, mask) for mask in range(1, QUARTERS)]


def scatter_cols(pieces, groups, combine):
    return tree_of([pieces[0]] + send_quarters(pieces, groups), combine)


def exchange_cols(piece, groups, combine):
    bit = QUARTERS
    while bit < groups:
        piece = combine(piece, swap(piece, "row", groups, bit))
        bit *= 2
    return piece


def gather_cols(piece, groups):
    diagonal = swap(piece, "row", groups, 3)
    return [piece, swap(piece, "row", groups, 1), swap(piece, "row", groups, 2), diagonal]


def sum_rows(vector, groups):
    vector = exchange_cols(vector, groups, jnp.add)
    return tree_sum([vector] + [swap(vector, "row", groups, mask) for mask in (1, 2, 3)])


def sum_cols(vector, groups):
    parts = [vector] + [swap(vector, "col", groups, mask) for mask in range(1, groups)]
    return tree_sum(parts)


def per_device(
    row_groups,
    col_groups,
    block_values,
    block_rows,
    block_cols,
    cost_vec,
    demand,
    lower,
    upper,
    bound_kind,
    primal_start,
    dual_start,
):
    values = block_values[0, 0]
    width = values.shape[1]
    ids = jnp.concatenate([block_rows[0, 0], block_cols[0, 0]])
    row_length, col_length = demand.shape[0], cost_vec.shape[0]
    cost_vec, demand, lower, upper, bound_kind, primal_start, dual_start = [
        v.reshape(-1, width)
        for v in (cost_vec, demand, lower, upper, bound_kind, primal_start, dual_start)
    ]
    count = demand.shape[0]
    half, quarter, spare = count // 2, count // QUARTERS, count + 8
    row_pieces, col_pieces = vectors(half, half), vectors(*[quarter] * QUARTERS)
    whole = vectors(count)
    squares = vectors(8)

    def over_col(pieces, combine):
        near = exchange_rows(halve_rows(pieces, col_groups, combine), col_groups, combine)
        return join_rows(near, col_groups)

    def over_row(pieces, combine):
        share = scatter_cols(pieces, row_groups, combine)
        return gather_cols(exchange_cols(share, row_groups, combine), row_groups)

    tile = lax.broadcasted_iota(jnp.int32, (2 * quarter, width), 0)

    def mixed(a, b):
        return jnp.where(tile < quarter, jnp.maximum(a, b), a + b)

    block_shape = jax.ShapeDtypeStruct(values.shape, values.dtype)
    out = call_blocks(
        functools.partial(first_pass_kernel, count),
        ids,
        values,
        [],
        row_pieces + col_pieces + [block_shape],
        [spare] * 2,
        first=True,
    )
    blocks = out[6]
    near = halve_rows(out[:2], col_groups, jnp.maximum)
    received = send_quarters(out[2:6], row_groups)
    near = exchange_rows(after(near, received[0]), col_groups, jnp.maximum)
    share = tree_of([out[2]] + received, jnp.maximum)
    *product_pieces, turned = call_blocks(
        functools.partial(first_product_kernel, count),
        ids,
        blocks,
        [after(dual_start, share)],
        col_pieces + [block_shape],
        [spare],
    )
    share = after(exchange_cols(share, row_groups, jnp.maximum), product_pieces)
    row_peaks = join_rows(after(near, share), col_groups)
    *col_pieces_2, row_scale = call_blocks(
        functools.partial(second_cols_kernel, count),
        ids,
        blocks,
        [turned] + row_peaks + product_pieces,
        vectors(*[2 * quarter] * QUARTERS) + whole,
        [spare],
    )
    col_peaks = gather_cols(share, row_groups)
    share = scatter_cols(after(col_pieces_2, col_peaks), row_groups, mixed)
    near, far, col_scale = call_blocks(
        functools.partial(second_rows_kernel, count),
        ids,
        blocks,
        [turned] + col_peaks,
        row_pieces + whole,
        [spare],
    )
    near, far = after((near, far), share)
    product = exchange_cols(share[quarter:], row_groups, jnp.add)
    share = exchange_cols(share[:quarter], row_groups, jnp.maximum)
    row_scale, demand_squares = call_plain(
        functools.partial(row_scale_kernel, count),
        over_col([near, far], jnp.maximum) + [row_scale, demand],
        whole + squares,
    )
    demand_squares = sum_rows(demand_squares, row_groups)
    product = gather_cols(product, row_groups)
    col_scale, cost_squares = call_plain(
        functools.partial(col_scale_kernel, count),
        gather_cols(share, row_groups) + [col_scale, cost_vec],
        whole + squares,
    )
    norms = [sum_cols(cost_squares, col_groups), demand_squares]

    def forward(first, last, product, primal):
        out = call_blocks(
            functools.partial(forward_kernel, count, first, last),
            ids,
            turned,
            product + [col_scale, cost_vec, lower, upper, bound_kind, primal] + norms,
            whole + row_pieces,
            [count, spare],
            last=last,
        )
        return out[0], over_col(out[1:], jnp.add)

    primal, image = forward(True, False, product, primal_start)
    out = call_blocks(
        functools.partial(transposed_kernel, count, True),
        ids,
        blocks,
        image + [row_scale, demand, dual_start] + norms,
        whole + col_pieces,
        [count, spare],
    )
    dual, product = out[0], over_row(out[1:], jnp.add)
    primal, image = forward(False, True, product, primal)
    (dual,) = call_plain(
        functools.partial(last_dual_kernel, count, False),
        image + [row_scale, demand, dual] + norms,
        whole,
    )
    return primal.reshape(col_length), dual.reshape(row_length)


def solution(mesh):
    def body(*args):
        return per_device(mesh.shape["row"], mesh.shape["col"], *args)

    return jax.shard_map(
        body,
        mesh=mesh,
        in_specs=(
            P("row", "col", None, None, None),
            P("row", "col", None),
            P("row", "col", None),
            P("col"),
            P("row"),
            P("col"),
            P("col"),
            P("col"),
            P("col"),
            P("row"),
        ),
        out_specs=(P("col"), P("row")),
        check_vma=False,
    )
```

```python
import functools

import jax
import jax.numpy as jnp
from jax import lax
from jax.experimental import pallas as pl
from jax.experimental.pallas import tpu as pltpu
from jax.sharding import PartitionSpec as P

SMALL_EPS = 1e-06
STEP_SCALE = 0.3

CHUNKS = 8
FIRST_GROUP = 32
GROUP = 64
AHEAD = 3
ROW_HALVING = 1
QUARTERS = 4
FIRST_VMEM = 44 * 1024 * 1024
BLOCK_VMEM = 20 * 1024 * 1024
SMALL_VMEM = 8 * 1024 * 1024


def bit_of(index, bit):
    return jnp.where((index & bit) != 0, 1, 0)


def row_mask():
    return bit_of(lax.axis_index("col"), ROW_HALVING) * (CHUNKS // 2)


def col_mask():
    return (lax.axis_index("row") & (QUARTERS - 1)) * (CHUNKS // QUARTERS)


def col_place(tile, count, mask):
    return jnp.where(tile < 0, count, tile ^ (mask * (count // CHUNKS)))


def row_place(tile, count, mask):
    return jnp.where(tile < 0, count, tile ^ (mask * (count // CHUNKS)))


def chunk_rows(chunk, size):
    return pl.ds(pl.multiple_of(chunk * size, size), size)


def piece_chunk(pieces, place, size, offset=0):
    per_piece = CHUNKS // len(pieces)
    start = offset + (place % per_piece) * size
    return pieces[place // per_piece], pl.ds(start, size)


def store_pieces(acc, pieces, count):
    size = count // len(pieces)
    for index, piece in enumerate(pieces):
        piece[...] = acc[pl.ds(index * size, size), :]


def add_row(acc, place, term, combine):
    acc[pl.ds(place, 1), :] = combine(acc[pl.ds(place, 1), :], term)


def one_row(ref, tile):
    return ref[pl.ds(jnp.maximum(tile, 0), 1), :]


def tree_of(parts, combine):
    while len(parts) > 1:
        parts = [combine(parts[i], parts[i + 1]) for i in range(0, len(parts), 2)]
    return parts[0]


def tree_sum(parts):
    return tree_of(parts, jnp.add)


def fold_rows(values):
    return jnp.sum(values.reshape(-1, 8, values.shape[-1]), axis=0)


def block_copy(index, values_ref, blocks, arrived):
    part = pl.ds(pl.multiple_of(index * FIRST_GROUP, FIRST_GROUP), FIRST_GROUP)
    return pltpu.make_async_copy(values_ref.at[part], blocks.at[part], arrived.at[index])


def for_slots(ids_ref, visit, finish, group=GROUP, before=None):
    count = ids_ref.shape[0] // 2

    def step(index, carry):
        if before is not None:
            before(index)
        slots = [index * group + inner for inner in range(group)]
        ids = [(ids_ref[slot], ids_ref[count + slot]) for slot in slots]
        terms = visit(slots, ids)
        for (row, col), term in zip(ids, terms):
            finish(row, col, term)
        return carry

    lax.fori_loop(0, count // group, step, 0)


def product_terms(vector_ref, tiles, blocks):
    width = vector_ref.shape[1]
    place = lax.broadcasted_iota(jnp.int32, (8, width), 0)
    terms = []
    for start in range(0, len(tiles), 4):
        rows = [one_row(vector_ref, tile) for tile in tiles[start : start + 4]]
        left = jnp.where(place == 0, rows[0], jnp.where(place == 1, rows[1], 0.0))
        right = jnp.where(place == 2, rows[2], jnp.where(place == 3, rows[3], 0.0))
        quad = blocks[start : start + 4]
        found = jnp.dot(
            jnp.concatenate([left, right], axis=1).astype(jnp.bfloat16),
            jnp.concatenate(
                [jnp.concatenate(quad[:2], axis=1), jnp.concatenate(quad[2:], axis=1)], axis=0
            ),
            preferred_element_type=jnp.float32,
        )
        for index in range(4):
            side = (index % 2) * width
            terms.append(found[index : index + 1, side : side + width])
    return terms


def row_max(values):
    return jnp.max(values, axis=0, keepdims=True)


def packed_max(values):
    folded = jnp.max(values.reshape(-1, 16, values.shape[-1]), axis=0)
    return row_max(folded.astype(jnp.float32))


def first_pass_kernel(count, ids_ref, values_ref, *refs):
    row_out, col_out, blocks = refs[:2], refs[2:6], refs[6]
    arrived, row_acc, col_acc = refs[7:]
    mask, across = col_mask(), row_mask()
    groups = values_ref.shape[0] // FIRST_GROUP
    for index in range(min(AHEAD, groups)):
        block_copy(index, values_ref, blocks, arrived).start()
    for acc in (row_acc, col_acc):
        acc[...] = jnp.zeros_like(acc)

    def before(index):
        block_copy(index, values_ref, blocks, arrived).wait()

        @pl.when(index + AHEAD < groups)
        def _():
            block_copy(index + AHEAD, values_ref, blocks, arrived).start()

    def visit(slots, ids):
        sizes = [jnp.abs(blocks[slot]) for slot in slots]
        return [(packed_max(size.T), packed_max(size)) for size in sizes]

    def finish(row, col, terms):
        add_row(row_acc, row_place(row, count, across), terms[0], jnp.maximum)
        add_row(col_acc, col_place(col, count, mask), terms[1], jnp.maximum)

    for_slots(ids_ref, visit, finish, FIRST_GROUP, before)
    store_pieces(row_acc, row_out, count)
    store_pieces(col_acc, col_out, count)


def first_product_kernel(count, ids_ref, blocks, dual_ref, *refs):
    product_out, turned, product_acc = refs[:4], refs[4], refs[5]
    mask = col_mask()
    product_acc[...] = jnp.zeros_like(product_acc)

    def visit(slots, ids):
        found = [blocks[slot] for slot in slots]
        for slot, block in zip(slots, found):
            turned[slot] = block.T
        return product_terms(dual_ref, [row for row, _ in ids], found)

    def finish(row, col, term):
        add_row(product_acc, col_place(col, count, mask), term, jnp.add)

    for_slots(ids_ref, visit, finish)
    store_pieces(product_acc, product_out, count)


def scaled_peaks(slots, scales, direct, flipped):
    width = direct.shape[-1]
    square = (width, width)
    diagonal = lax.broadcasted_iota(jnp.int32, square, 0) == lax.broadcasted_iota(
        jnp.int32, square, 1
    )
    diagonal = diagonal.astype(jnp.float32).astype(jnp.bfloat16)
    found = []
    for index, (slot, scale) in enumerate(zip(slots, scales)):
        if index % 2:
            scaled = (jnp.abs(flipped[slot]).astype(jnp.float32) * scale).T
        else:
            sizes = jnp.abs(direct[slot])
            high = scale.astype(jnp.bfloat16)
            low = (scale - high.astype(jnp.float32)).astype(jnp.bfloat16)
            scaled = jnp.dot(
                jnp.concatenate([diagonal * high, diagonal * low], axis=1),
                jnp.concatenate([sizes, sizes], axis=0),
                preferred_element_type=jnp.float32,
            )
        found.append(row_max(scaled))
    return found


def second_cols_kernel(count, ids_ref, blocks, turned, *refs):
    row_in, col_out, row_scale, col_acc = refs[:2], refs[2:6], refs[6], refs[7]
    mask, across = col_mask(), row_mask()
    size = count // CHUNKS
    col_acc[...] = jnp.zeros_like(col_acc)
    for place in range(CHUNKS):
        piece, part = piece_chunk(row_in, place, size)
        row_scale[chunk_rows(place ^ across, size), :] = lax.rsqrt(piece[part, :] + SMALL_EPS)

    def visit(slots, ids):
        scales = [one_row(row_scale, row) for row, _ in ids]
        return scaled_peaks(slots, scales, blocks, turned)

    def finish(row, col, term):
        add_row(col_acc, col_place(col, count, mask), term, jnp.maximum)

    for_slots(ids_ref, visit, finish)
    store_pieces(col_acc, col_out, count)


def second_rows_kernel(count, ids_ref, blocks, turned, *refs):
    col_in, row_out, col_scale, row_acc = refs[:4], refs[4:6], refs[6], refs[7]
    mask, across = col_mask(), row_mask()
    size = count // CHUNKS
    row_acc[...] = jnp.zeros_like(row_acc)
    for place in range(CHUNKS):
        piece, part = piece_chunk(col_in, place, size)
        col_scale[chunk_rows(place ^ mask, size), :] = lax.rsqrt(piece[part, :] + SMALL_EPS)

    def visit(slots, ids):
        scales = [one_row(col_scale, col) for _, col in ids]
        return scaled_peaks(slots, scales, turned, blocks)

    def finish(row, col, term):
        add_row(row_acc, row_place(row, count, across), term, jnp.maximum)

    for_slots(ids_ref, visit, finish)
    store_pieces(row_acc, row_out, count)


def next_scale(scale, piece, inside):
    return scale * lax.rsqrt(scale * piece[inside, :] + SMALL_EPS)


def row_scale_kernel(count, near, far, scale_ref, vector_ref, new_scale, squares):
    across = row_mask()
    size = count // CHUNKS
    sums = []
    for place in range(CHUNKS):
        part = chunk_rows(place ^ across, size)
        piece, inside = piece_chunk((near, far), place, size)
        scale = next_scale(scale_ref[part, :], piece, inside)
        new_scale[part, :] = scale
        scaled = scale * vector_ref[part, :]
        sums.append(fold_rows(scaled * scaled))
    half = CHUNKS // 2
    squares[...] = tree_sum(sums[:half]) + tree_sum(sums[half:])


def col_scale_kernel(count, *refs):
    pieces, (scale_ref, vector_ref, new_scale, squares) = refs[:4], refs[4:]
    mask = col_mask()
    size = count // CHUNKS
    sums = []
    for place in range(CHUNKS):
        part = chunk_rows(place ^ mask, size)
        piece, inside = piece_chunk(pieces, place, size)
        scale = next_scale(scale_ref[part, :], piece, inside)
        new_scale[part, :] = scale
        scaled = scale * vector_ref[part, :]
        sums.append(fold_rows(scaled * scaled))
    squares[...] = tree_sum(sums)


def norm_ratio(cost_squares, demand_squares):
    cost_total = jnp.sum(cost_squares[...], keepdims=True)
    demand_total = jnp.sum(demand_squares[...], keepdims=True)
    return jnp.sqrt(cost_total + SMALL_EPS) / jnp.sqrt(demand_total + SMALL_EPS)


def forward_kernel(count, first, last, ids_ref, turned, *refs):
    product, refs = refs[:4], refs[4:]
    scale_ref, cost_ref, low_ref, high_ref, kind_ref, primal_ref = refs[:6]
    cost_squares, demand_squares, primal_out = refs[6:9]
    row_out, refs = refs[9:11], refs[11:]
    shifted, row_acc = refs[:2]
    moved_ref = primal_out
    if last:
        moved_ref, written = refs[2:]
    mask, across = col_mask(), row_mask()
    size = count // CHUNKS
    row_acc[...] = jnp.zeros_like(row_acc)
    primal_step = STEP_SCALE / norm_ratio(cost_squares, demand_squares)
    for place in range(CHUNKS):
        part = chunk_rows(place ^ mask, size)
        behind = product[0].shape[0] - count // QUARTERS
        piece, inside = piece_chunk(product, place, size, behind)
        scale = scale_ref[part, :]
        inverse = 1.0 / scale
        primal = primal_ref[part, :]
        if first:
            primal = primal * inverse
        gradient = scale * piece[inside, :]
        moved = primal - primal_step * (scale * cost_ref[part, :] - gradient)
        kind = kind_ref[part, :]
        moved = jnp.where(
            (kind == 1) | (kind == 3), jnp.maximum(moved, low_ref[part, :] * inverse), moved
        )
        moved = jnp.where(
            (kind == 2) | (kind == 3), jnp.minimum(moved, high_ref[part, :] * inverse), moved
        )
        shifted[part, :] = scale * (2.0 * moved - primal)
        moved_ref[part, :] = scale * moved if last else moved

    if last:
        copy_out = pltpu.make_async_copy(moved_ref, primal_out, written)
        copy_out.start()

    def visit(slots, ids):
        return product_terms(shifted, [col for _, col in ids], [turned[slot] for slot in slots])

    def finish(row, col, term):
        add_row(row_acc, row_place(row, count, across), term, jnp.add)

    for_slots(ids_ref, visit, finish)
    store_pieces(row_acc, row_out, count)
    if last:
        copy_out.wait()


def next_dual(first, image, inside, scale, demand, dual, dual_step):
    if first:
        dual = dual / scale
    row_image = scale * image[inside, :]
    return jnp.maximum(dual + dual_step * (scale * demand - row_image), 0.0)


def transposed_kernel(count, first, ids_ref, blocks, *refs):
    image, refs = refs[:2], refs[2:]
    scale_ref, demand_ref, dual_ref, cost_squares, demand_squares, dual_out = refs[:6]
    product_out, (weights, product_acc) = refs[6:10], refs[10:]
    mask, across = col_mask(), row_mask()
    size = count // CHUNKS
    product_acc[...] = jnp.zeros_like(product_acc)
    dual_step = STEP_SCALE * norm_ratio(cost_squares, demand_squares)
    for place in range(CHUNKS):
        part = chunk_rows(place ^ across, size)
        piece, inside = piece_chunk(image, place, size)
        scale = scale_ref[part, :]
        dual = next_dual(
            first, piece, inside, scale, demand_ref[part, :], dual_ref[part, :], dual_step
        )
        dual_out[part, :] = dual
        weights[part, :] = scale * dual

    def visit(slots, ids):
        return product_terms(weights, [row for row, _ in ids], [blocks[slot] for slot in slots])

    def finish(row, col, term):
        add_row(product_acc, col_place(col, count, mask), term, jnp.add)

    for_slots(ids_ref, visit, finish)
    store_pieces(product_acc, product_out, count)


def last_dual_kernel(count, first, *refs):
    image, refs = refs[:2], refs[2:]
    scale_ref, demand_ref, dual_ref, cost_squares, demand_squares, dual_out = refs
    across = row_mask()
    size = count // CHUNKS
    dual_step = STEP_SCALE * norm_ratio(cost_squares, demand_squares)
    for place in range(CHUNKS):
        part = chunk_rows(place ^ across, size)
        piece, inside = piece_chunk(image, place, size)
        scale = scale_ref[part, :]
        dual = next_dual(
            first, piece, inside, scale, demand_ref[part, :], dual_ref[part, :], dual_step
        )
        dual_out[part, :] = scale * dual


def vectors(*row_counts):
    return [jax.ShapeDtypeStruct((rows, 128), jnp.float32) for rows in row_counts]


def call_plain(kernel, operands, out_shape):
    return pl.pallas_call(
        kernel,
        out_shape=out_shape,
        in_specs=[pl.BlockSpec(memory_space=pltpu.VMEM)] * len(operands),
        out_specs=[pl.BlockSpec(memory_space=pltpu.VMEM)] * len(out_shape),
        compiler_params=pltpu.CompilerParams(vmem_limit_bytes=SMALL_VMEM),
    )(*operands)


def call_blocks(kernel, ids, values, operands, out_shape, scratch, first=False, last=False):
    width = values.shape[1]
    scratch_shapes = [pltpu.VMEM((rows, width), jnp.float32) for rows in scratch]
    if first:
        arrivals = pltpu.SemaphoreType.DMA((values.shape[0] // FIRST_GROUP,))
        scratch_shapes = [arrivals] + scratch_shapes
    out_specs = [pl.BlockSpec(memory_space=pltpu.VMEM)] * len(out_shape)
    if last:
        out_specs[0] = pl.BlockSpec(memory_space=pl.ANY)
        scratch_shapes = scratch_shapes + [
            pltpu.VMEM(out_shape[0].shape, out_shape[0].dtype),
            pltpu.SemaphoreType.DMA,
        ]
    return pl.pallas_call(
        kernel,
        out_shape=out_shape,
        in_specs=[pl.BlockSpec(memory_space=pltpu.SMEM)]
        + [pl.BlockSpec(memory_space=pl.ANY if first else pltpu.VMEM)]
        + [pl.BlockSpec(memory_space=pltpu.VMEM)] * len(operands),
        out_specs=out_specs,
        scratch_shapes=scratch_shapes,
        compiler_params=pltpu.CompilerParams(
            vmem_limit_bytes=FIRST_VMEM if first else BLOCK_VMEM
        ),
        cost_estimate=pl.CostEstimate(
            flops=2 * values.size, bytes_accessed=2 * values.size, transcendentals=0
        ),
    )(ids, values, *operands)


def swap(vector, axis, size, bit):
    return lax.ppermute(vector, axis, [(i, i ^ bit) for i in range(size)])


def after(values, *earlier):
    return lax.optimization_barrier((values, earlier))[0]


def halve_rows(pieces, groups, combine):
    near, far = pieces
    return combine(near, swap(far, "col", groups, ROW_HALVING))


def exchange_rows(near, groups, combine):
    bit = 1
    while bit < groups:
        if bit != ROW_HALVING:
            near = combine(near, swap(near, "col", groups, bit))
        bit *= 2
    return near


def join_rows(near, groups):
    return [near, swap(near, "col", groups, ROW_HALVING)]


def scatter_cols(pieces, groups, combine, tie=None):
    diagonal = swap(pieces[3], "row", groups, 3)
    first, second = pieces[1:3] if tie is None else after((pieces[1], pieces[2]), tie)
    first, second = swap(first, "row", groups, 1), swap(second, "row", groups, 2)
    return tree_of([pieces[0], first, second, diagonal], combine)


def exchange_cols(piece, groups, combine):
    bit = QUARTERS
    while bit < groups:
        piece = combine(piece, swap(piece, "row", groups, bit))
        bit *= 2
    return piece


def gather_cols(piece, groups):
    diagonal = swap(piece, "row", groups, 3)
    return [piece, swap(piece, "row", groups, 1), swap(piece, "row", groups, 2), diagonal]


def sum_rows(vector, groups):
    vector = exchange_cols(vector, groups, jnp.add)
    return tree_sum([vector] + [swap(vector, "row", groups, mask) for mask in (1, 2, 3)])


def sum_cols(vector, groups):
    parts = [vector] + [swap(vector, "col", groups, mask) for mask in range(1, groups)]
    return tree_sum(parts)


def per_device(
    row_groups,
    col_groups,
    block_values,
    block_rows,
    block_cols,
    cost_vec,
    demand,
    lower,
    upper,
    bound_kind,
    primal_start,
    dual_start,
):
    values = block_values[0, 0]
    width = values.shape[1]
    ids = jnp.concatenate([block_rows[0, 0], block_cols[0, 0]])
    row_length, col_length = demand.shape[0], cost_vec.shape[0]
    cost_vec, demand, lower, upper, bound_kind, primal_start, dual_start = [
        v.reshape(-1, width)
        for v in (cost_vec, demand, lower, upper, bound_kind, primal_start, dual_start)
    ]
    count = demand.shape[0]
    half, quarter, spare = count // 2, count // QUARTERS, count + 8
    row_pieces, col_pieces = vectors(half, half), vectors(*[quarter] * QUARTERS)
    whole = vectors(count)
    squares = vectors(8)

    def over_col(pieces, combine):
        near = exchange_rows(halve_rows(pieces, col_groups, combine), col_groups, combine)
        return join_rows(near, col_groups)

    def over_row(pieces, combine):
        share = scatter_cols(pieces, row_groups, combine)
        return gather_cols(exchange_cols(share, row_groups, combine), row_groups)

    block_shape = jax.ShapeDtypeStruct(values.shape, values.dtype)
    out = call_blocks(
        functools.partial(first_pass_kernel, count),
        ids,
        values,
        [],
        row_pieces + col_pieces + [block_shape],
        [spare] * 2,
        first=True,
    )
    blocks = out[6]
    near = halve_rows(out[:2], col_groups, jnp.maximum)
    *product_pieces, turned = call_blocks(
        functools.partial(first_product_kernel, count),
        ids,
        blocks,
        [after(dual_start, near)],
        col_pieces + [block_shape],
        [spare],
    )
    share = scatter_cols(out[2:6], row_groups, jnp.maximum, near)
    near = exchange_rows(near, col_groups, jnp.maximum)
    product = scatter_cols(after(product_pieces, near), row_groups, jnp.add)
    share = after(exchange_cols(share, row_groups, jnp.maximum), product_pieces)
    row_peaks = join_rows(near, col_groups)
    *col_pieces_2, row_scale = call_blocks(
        functools.partial(second_cols_kernel, count),
        ids,
        blocks,
        [turned] + after(row_peaks, share),
        col_pieces + whole,
        [spare],
    )
    col_peaks = gather_cols(share, row_groups)
    share = scatter_cols(after(col_pieces_2, col_peaks), row_groups, jnp.maximum)
    product = exchange_cols(product, row_groups, jnp.add)
    near, far, col_scale = call_blocks(
        functools.partial(second_rows_kernel, count),
        ids,
        blocks,
        [turned] + col_peaks,
        row_pieces + whole,
        [spare],
    )
    near, far = after((near, far), (share, product))
    share = exchange_cols(share, row_groups, jnp.maximum)
    row_scale, demand_squares = call_plain(
        functools.partial(row_scale_kernel, count),
        over_col([near, far], jnp.maximum) + [row_scale, demand],
        whole + squares,
    )
    demand_squares = sum_rows(demand_squares, row_groups)
    gathered = gather_cols(jnp.concatenate([share, product], axis=0), row_groups)
    col_scale, cost_squares = call_plain(
        functools.partial(col_scale_kernel, count),
        gathered + [col_scale, cost_vec],
        whole + squares,
    )
    norms = [sum_cols(cost_squares, col_groups), demand_squares]

    def forward(first, last, product, primal):
        out = call_blocks(
            functools.partial(forward_kernel, count, first, last),
            ids,
            turned,
            product + [col_scale, cost_vec, lower, upper, bound_kind, primal] + norms,
            whole + row_pieces,
            [count, spare],
            last=last,
        )
        return out[0], over_col(out[1:], jnp.add)

    primal, image = forward(True, False, gathered, primal_start)
    out = call_blocks(
        functools.partial(transposed_kernel, count, True),
        ids,
        blocks,
        image + [row_scale, demand, dual_start] + norms,
        whole + col_pieces,
        [count, spare],
    )
    dual, product = out[0], over_row(out[1:], jnp.add)
    primal, image = forward(False, True, product, primal)
    (dual,) = call_plain(
        functools.partial(last_dual_kernel, count, False),
        image + [row_scale, demand, dual] + norms,
        whole,
    )
    return primal.reshape(col_length), dual.reshape(row_length)


def solution(mesh):
    def body(*args):
        return per_device(mesh.shape["row"], mesh.shape["col"], *args)

    return jax.shard_map(
        body,
        mesh=mesh,
        in_specs=(
            P("row", "col", None, None, None),
            P("row", "col", None),
            P("row", "col", None),
            P("col"),
            P("row"),
            P("col"),
            P("col"),
            P("col"),
            P("col"),
            P("row"),
        ),
        out_specs=(P("col"), P("row")),
        check_vma=False,
    )
```

```python
import functools

import jax
import jax.numpy as jnp
from jax import lax
from jax.experimental import pallas as pl
from jax.experimental.pallas import tpu as pltpu
from jax.sharding import PartitionSpec as P

SMALL_EPS = 1e-06
STEP_SCALE = 0.3

CHUNKS = 8
FIRST_GROUP = 32
GROUP = 64
AHEAD = 3
ROW_HALVING = 1
QUARTERS = 4
FIRST_VMEM = 44 * 1024 * 1024
BLOCK_VMEM = 20 * 1024 * 1024
SMALL_VMEM = 8 * 1024 * 1024


def bit_of(index, bit):
    return jnp.where((index & bit) != 0, 1, 0)


def row_mask():
    return bit_of(lax.axis_index("col"), ROW_HALVING) * (CHUNKS // 2)


def col_mask():
    return (lax.axis_index("row") & (QUARTERS - 1)) * (CHUNKS // QUARTERS)


def col_place(tile, count, mask):
    return jnp.where(tile < 0, count, tile ^ (mask * (count // CHUNKS)))


def row_place(tile, count, mask):
    return jnp.where(tile < 0, count, tile ^ (mask * (count // CHUNKS)))


def chunk_rows(chunk, size):
    return pl.ds(pl.multiple_of(chunk * size, size), size)


def piece_chunk(pieces, place, size, offset=0):
    per_piece = CHUNKS // len(pieces)
    start = offset + (place % per_piece) * size
    return pieces[place // per_piece], pl.ds(start, size)


def store_pieces(acc, pieces, count):
    size = count // len(pieces)
    for index, piece in enumerate(pieces):
        piece[...] = acc[pl.ds(index * size, size), :]


def add_row(acc, place, term, combine):
    acc[pl.ds(place, 1), :] = combine(acc[pl.ds(place, 1), :], term)


def one_row(ref, tile):
    return ref[pl.ds(jnp.maximum(tile, 0), 1), :]


def tree_of(parts, combine):
    while len(parts) > 1:
        parts = [combine(parts[i], parts[i + 1]) for i in range(0, len(parts), 2)]
    return parts[0]


def tree_sum(parts):
    return tree_of(parts, jnp.add)


def fold_rows(values):
    return jnp.sum(values.reshape(-1, 8, values.shape[-1]), axis=0)


def block_copy(index, values_ref, blocks, arrived):
    part = pl.ds(pl.multiple_of(index * FIRST_GROUP, FIRST_GROUP), FIRST_GROUP)
    return pltpu.make_async_copy(values_ref.at[part], blocks.at[part], arrived.at[index])


def for_slots(ids_ref, visit, finish, group=GROUP, before=None):
    count = ids_ref.shape[0] // 2

    def step(index, carry):
        if before is not None:
            before(index)
        slots = [index * group + inner for inner in range(group)]
        ids = [(ids_ref[slot], ids_ref[count + slot]) for slot in slots]
        terms = visit(slots, ids)
        for (row, col), term in zip(ids, terms):
            finish(row, col, term)
        return carry

    lax.fori_loop(0, count // group, step, 0)


def product_terms(vector_ref, tiles, blocks):
    width = vector_ref.shape[1]
    place = lax.broadcasted_iota(jnp.int32, (8, width), 0)
    terms = []
    for start in range(0, len(tiles), 4):
        rows = [one_row(vector_ref, tile) for tile in tiles[start : start + 4]]
        left = jnp.where(place == 0, rows[0], jnp.where(place == 1, rows[1], 0.0))
        right = jnp.where(place == 2, rows[2], jnp.where(place == 3, rows[3], 0.0))
        quad = blocks[start : start + 4]
        found = jnp.dot(
            jnp.concatenate([left, right], axis=1).astype(jnp.bfloat16),
            jnp.concatenate(
                [jnp.concatenate(quad[:2], axis=1), jnp.concatenate(quad[2:], axis=1)], axis=0
            ),
            preferred_element_type=jnp.float32,
        )
        for index in range(4):
            side = (index % 2) * width
            terms.append(found[index : index + 1, side : side + width])
    return terms


def row_max(values):
    return jnp.max(values, axis=0, keepdims=True)


def packed_max(values):
    folded = jnp.max(values.reshape(-1, 16, values.shape[-1]), axis=0)
    return row_max(folded.astype(jnp.float32))


def first_pass_kernel(count, ids_ref, values_ref, *refs):
    row_out, col_out, blocks = refs[:2], refs[2:6], refs[6]
    arrived, row_acc, col_acc = refs[7:]
    mask, across = col_mask(), row_mask()
    groups = values_ref.shape[0] // FIRST_GROUP
    for index in range(min(AHEAD, groups)):
        block_copy(index, values_ref, blocks, arrived).start()
    for acc in (row_acc, col_acc):
        acc[...] = jnp.zeros_like(acc)

    def before(index):
        block_copy(index, values_ref, blocks, arrived).wait()

        @pl.when(index + AHEAD < groups)
        def _():
            block_copy(index + AHEAD, values_ref, blocks, arrived).start()

    def visit(slots, ids):
        sizes = [jnp.abs(blocks[slot]) for slot in slots]
        return [(packed_max(size.T), packed_max(size)) for size in sizes]

    def finish(row, col, terms):
        add_row(row_acc, row_place(row, count, across), terms[0], jnp.maximum)
        add_row(col_acc, col_place(col, count, mask), terms[1], jnp.maximum)

    for_slots(ids_ref, visit, finish, FIRST_GROUP, before)
    store_pieces(row_acc, row_out, count)
    store_pieces(col_acc, col_out, count)


def first_product_kernel(count, ids_ref, blocks, dual_ref, *refs):
    product_out, turned, product_acc = refs[:4], refs[4], refs[5]
    mask = col_mask()
    product_acc[...] = jnp.zeros_like(product_acc)

    def visit(slots, ids):
        found = [blocks[slot] for slot in slots]
        for slot, block in zip(slots, found):
            turned[slot] = block.T
        return product_terms(dual_ref, [row for row, _ in ids], found)

    def finish(row, col, term):
        add_row(product_acc, col_place(col, count, mask), term, jnp.add)

    for_slots(ids_ref, visit, finish)
    store_pieces(product_acc, product_out, count)


def scaled_peaks(slots, scales, direct, flipped):
    width = direct.shape[-1]
    square = (width, width)
    diagonal = lax.broadcasted_iota(jnp.int32, square, 0) == lax.broadcasted_iota(
        jnp.int32, square, 1
    )
    diagonal = diagonal.astype(jnp.float32).astype(jnp.bfloat16)
    found = []
    for index, (slot, scale) in enumerate(zip(slots, scales)):
        if index % 2:
            scaled = (jnp.abs(flipped[slot]).astype(jnp.float32) * scale).T
        else:
            sizes = jnp.abs(direct[slot])
            high = scale.astype(jnp.bfloat16)
            low = (scale - high.astype(jnp.float32)).astype(jnp.bfloat16)
            scaled = jnp.dot(
                jnp.concatenate([diagonal * high, diagonal * low], axis=1),
                jnp.concatenate([sizes, sizes], axis=0),
                preferred_element_type=jnp.float32,
            )
        found.append(row_max(scaled))
    return found


def second_cols_kernel(count, ids_ref, blocks, turned, *refs):
    row_in, product_in, col_out, refs = refs[:2], refs[2:6], refs[6:10], refs[10:]
    row_scale, col_acc = refs
    mask, across = col_mask(), row_mask()
    size = count // CHUNKS
    col_acc[...] = jnp.zeros_like(col_acc)
    for place in range(CHUNKS):
        piece, part = piece_chunk(row_in, place, size)
        row_scale[chunk_rows(place ^ across, size), :] = lax.rsqrt(piece[part, :] + SMALL_EPS)

    def visit(slots, ids):
        scales = [one_row(row_scale, row) for row, _ in ids]
        return scaled_peaks(slots, scales, blocks, turned)

    def finish(row, col, term):
        add_row(col_acc, col_place(col, count, mask), term, jnp.maximum)

    for_slots(ids_ref, visit, finish)
    quarter = count // QUARTERS
    for index, (piece, product) in enumerate(zip(col_out, product_in)):
        piece[pl.ds(0, quarter), :] = col_acc[pl.ds(index * quarter, quarter), :]
        piece[pl.ds(quarter, quarter), :] = product[...]


def second_rows_kernel(count, ids_ref, blocks, turned, *refs):
    col_in, row_out, col_scale, row_acc = refs[:4], refs[4:6], refs[6], refs[7]
    mask, across = col_mask(), row_mask()
    size = count // CHUNKS
    row_acc[...] = jnp.zeros_like(row_acc)
    for place in range(CHUNKS):
        piece, part = piece_chunk(col_in, place, size)
        col_scale[chunk_rows(place ^ mask, size), :] = lax.rsqrt(piece[part, :] + SMALL_EPS)

    def visit(slots, ids):
        scales = [one_row(col_scale, col) for _, col in ids]
        return scaled_peaks(slots, scales, turned, blocks)

    def finish(row, col, term):
        add_row(row_acc, row_place(row, count, across), term, jnp.maximum)

    for_slots(ids_ref, visit, finish)
    store_pieces(row_acc, row_out, count)


def next_scale(scale, piece, inside):
    return scale * lax.rsqrt(scale * piece[inside, :] + SMALL_EPS)


def row_scale_kernel(count, near, far, scale_ref, vector_ref, new_scale, squares):
    across = row_mask()
    size = count // CHUNKS
    sums = []
    for place in range(CHUNKS):
        part = chunk_rows(place ^ across, size)
        piece, inside = piece_chunk((near, far), place, size)
        scale = next_scale(scale_ref[part, :], piece, inside)
        new_scale[part, :] = scale
        scaled = scale * vector_ref[part, :]
        sums.append(fold_rows(scaled * scaled))
    half = CHUNKS // 2
    squares[...] = tree_sum(sums[:half]) + tree_sum(sums[half:])


def col_scale_kernel(count, *refs):
    pieces, (scale_ref, vector_ref, new_scale, squares) = refs[:4], refs[4:]
    mask = col_mask()
    size = count // CHUNKS
    sums = []
    for place in range(CHUNKS):
        part = chunk_rows(place ^ mask, size)
        piece, inside = piece_chunk(pieces, place, size)
        scale = next_scale(scale_ref[part, :], piece, inside)
        new_scale[part, :] = scale
        scaled = scale * vector_ref[part, :]
        sums.append(fold_rows(scaled * scaled))
    squares[...] = tree_sum(sums)


def norm_ratio(cost_squares, demand_squares):
    cost_total = jnp.sum(cost_squares[...], keepdims=True)
    demand_total = jnp.sum(demand_squares[...], keepdims=True)
    return jnp.sqrt(cost_total + SMALL_EPS) / jnp.sqrt(demand_total + SMALL_EPS)


def forward_kernel(count, first, last, ids_ref, turned, *refs):
    product, refs = refs[:4], refs[4:]
    scale_ref, cost_ref, low_ref, high_ref, kind_ref, primal_ref = refs[:6]
    cost_squares, demand_squares, primal_out = refs[6:9]
    row_out, refs = refs[9:11], refs[11:]
    shifted, row_acc = refs[:2]
    moved_ref = primal_out
    if last:
        moved_ref, written = refs[2:]
    mask, across = col_mask(), row_mask()
    size = count // CHUNKS
    row_acc[...] = jnp.zeros_like(row_acc)
    primal_step = STEP_SCALE / norm_ratio(cost_squares, demand_squares)
    for place in range(CHUNKS):
        part = chunk_rows(place ^ mask, size)
        behind = product[0].shape[0] - count // QUARTERS
        piece, inside = piece_chunk(product, place, size, behind)
        scale = scale_ref[part, :]
        inverse = 1.0 / scale
        primal = primal_ref[part, :]
        if first:
            primal = primal * inverse
        gradient = scale * piece[inside, :]
        moved = primal - primal_step * (scale * cost_ref[part, :] - gradient)
        kind = kind_ref[part, :]
        moved = jnp.where(
            (kind == 1) | (kind == 3), jnp.maximum(moved, low_ref[part, :] * inverse), moved
        )
        moved = jnp.where(
            (kind == 2) | (kind == 3), jnp.minimum(moved, high_ref[part, :] * inverse), moved
        )
        shifted[part, :] = scale * (2.0 * moved - primal)
        moved_ref[part, :] = scale * moved if last else moved

    if last:
        copy_out = pltpu.make_async_copy(moved_ref, primal_out, written)
        copy_out.start()

    def visit(slots, ids):
        return product_terms(shifted, [col for _, col in ids], [turned[slot] for slot in slots])

    def finish(row, col, term):
        add_row(row_acc, row_place(row, count, across), term, jnp.add)

    for_slots(ids_ref, visit, finish)
    store_pieces(row_acc, row_out, count)
    if last:
        copy_out.wait()


def next_dual(first, image, inside, scale, demand, dual, dual_step):
    if first:
        dual = dual / scale
    row_image = scale * image[inside, :]
    return jnp.maximum(dual + dual_step * (scale * demand - row_image), 0.0)


def transposed_kernel(count, first, ids_ref, blocks, *refs):
    image, refs = refs[:2], refs[2:]
    scale_ref, demand_ref, dual_ref, cost_squares, demand_squares, dual_out = refs[:6]
    product_out, (weights, product_acc) = refs[6:10], refs[10:]
    mask, across = col_mask(), row_mask()
    size = count // CHUNKS
    product_acc[...] = jnp.zeros_like(product_acc)
    dual_step = STEP_SCALE * norm_ratio(cost_squares, demand_squares)
    for place in range(CHUNKS):
        part = chunk_rows(place ^ across, size)
        piece, inside = piece_chunk(image, place, size)
        scale = scale_ref[part, :]
        dual = next_dual(
            first, piece, inside, scale, demand_ref[part, :], dual_ref[part, :], dual_step
        )
        dual_out[part, :] = dual
        weights[part, :] = scale * dual

    def visit(slots, ids):
        return product_terms(weights, [row for row, _ in ids], [blocks[slot] for slot in slots])

    def finish(row, col, term):
        add_row(product_acc, col_place(col, count, mask), term, jnp.add)

    for_slots(ids_ref, visit, finish)
    store_pieces(product_acc, product_out, count)


def last_dual_kernel(count, first, *refs):
    image, refs = refs[:2], refs[2:]
    scale_ref, demand_ref, dual_ref, cost_squares, demand_squares, dual_out = refs
    across = row_mask()
    size = count // CHUNKS
    dual_step = STEP_SCALE * norm_ratio(cost_squares, demand_squares)
    for place in range(CHUNKS):
        part = chunk_rows(place ^ across, size)
        piece, inside = piece_chunk(image, place, size)
        scale = scale_ref[part, :]
        dual = next_dual(
            first, piece, inside, scale, demand_ref[part, :], dual_ref[part, :], dual_step
        )
        dual_out[part, :] = scale * dual


def vectors(*row_counts):
    return [jax.ShapeDtypeStruct((rows, 128), jnp.float32) for rows in row_counts]


def call_plain(kernel, operands, out_shape):
    return pl.pallas_call(
        kernel,
        out_shape=out_shape,
        in_specs=[pl.BlockSpec(memory_space=pltpu.VMEM)] * len(operands),
        out_specs=[pl.BlockSpec(memory_space=pltpu.VMEM)] * len(out_shape),
        compiler_params=pltpu.CompilerParams(vmem_limit_bytes=SMALL_VMEM),
    )(*operands)


def call_blocks(kernel, ids, values, operands, out_shape, scratch, first=False, last=False):
    width = values.shape[1]
    scratch_shapes = [pltpu.VMEM((rows, width), jnp.float32) for rows in scratch]
    if first:
        arrivals = pltpu.SemaphoreType.DMA((values.shape[0] // FIRST_GROUP,))
        scratch_shapes = [arrivals] + scratch_shapes
    out_specs = [pl.BlockSpec(memory_space=pltpu.VMEM)] * len(out_shape)
    if last:
        out_specs[0] = pl.BlockSpec(memory_space=pl.ANY)
        scratch_shapes = scratch_shapes + [
            pltpu.VMEM(out_shape[0].shape, out_shape[0].dtype),
            pltpu.SemaphoreType.DMA,
        ]
    return pl.pallas_call(
        kernel,
        out_shape=out_shape,
        in_specs=[pl.BlockSpec(memory_space=pltpu.SMEM)]
        + [pl.BlockSpec(memory_space=pl.ANY if first else pltpu.VMEM)]
        + [pl.BlockSpec(memory_space=pltpu.VMEM)] * len(operands),
        out_specs=out_specs,
        scratch_shapes=scratch_shapes,
        compiler_params=pltpu.CompilerParams(
            vmem_limit_bytes=FIRST_VMEM if first else BLOCK_VMEM
        ),
        cost_estimate=pl.CostEstimate(
            flops=2 * values.size, bytes_accessed=2 * values.size, transcendentals=0
        ),
    )(ids, values, *operands)


def swap(vector, axis, size, bit):
    return lax.ppermute(vector, axis, [(i, i ^ bit) for i in range(size)])


def after(values, *earlier):
    return lax.optimization_barrier((values, earlier))[0]


def halve_rows(pieces, groups, combine):
    near, far = pieces
    return combine(near, swap(far, "col", groups, ROW_HALVING))


def exchange_rows(near, groups, combine):
    bit = 1
    while bit < groups:
        if bit != ROW_HALVING:
            near = combine(near, swap(near, "col", groups, bit))
        bit *= 2
    return near


def join_rows(near, groups):
    return [near, swap(near, "col", groups, ROW_HALVING)]


def scatter_cols(pieces, groups, combine, tie=None):
    diagonal = swap(pieces[3], "row", groups, 3)
    first, second = pieces[1:3] if tie is None else after((pieces[1], pieces[2]), tie)
    first, second = swap(first, "row", groups, 1), swap(second, "row", groups, 2)
    return tree_of([pieces[0], first, second, diagonal], combine)


def exchange_cols(piece, groups, combine, tie=None):
    bit = QUARTERS
    while bit < groups:
        got = swap(piece, "row", groups, bit)
        piece = combine(piece, got if tie is None else after(got, tie))
        bit *= 2
    return piece


def gather_cols(piece, groups):
    diagonal = swap(piece, "row", groups, 3)
    return [piece, swap(piece, "row", groups, 1), swap(piece, "row", groups, 2), diagonal]


def sum_rows(vector, groups):
    vector = exchange_cols(vector, groups, jnp.add)
    return [vector] + [swap(vector, "row", groups, mask) for mask in (1, 2, 3)]


def sum_cols(vector, groups):
    parts = [vector] + [swap(vector, "col", groups, mask) for mask in range(1, groups)]
    return tree_sum(parts)


def per_device(
    row_groups,
    col_groups,
    block_values,
    block_rows,
    block_cols,
    cost_vec,
    demand,
    lower,
    upper,
    bound_kind,
    primal_start,
    dual_start,
):
    values = block_values[0, 0]
    width = values.shape[1]
    ids = jnp.concatenate([block_rows[0, 0], block_cols[0, 0]])
    row_length, col_length = demand.shape[0], cost_vec.shape[0]
    cost_vec, demand, lower, upper, bound_kind, primal_start, dual_start = [
        v.reshape(-1, width)
        for v in (cost_vec, demand, lower, upper, bound_kind, primal_start, dual_start)
    ]
    count = demand.shape[0]
    half, quarter, spare = count // 2, count // QUARTERS, count + 8
    row_pieces, col_pieces = vectors(half, half), vectors(*[quarter] * QUARTERS)
    whole = vectors(count)
    squares = vectors(8)

    def over_col(pieces, combine):
        near = exchange_rows(halve_rows(pieces, col_groups, combine), col_groups, combine)
        return join_rows(near, col_groups)

    def over_row(pieces, combine):
        share = scatter_cols(pieces, row_groups, combine)
        return gather_cols(exchange_cols(share, row_groups, combine), row_groups)

    block_shape = jax.ShapeDtypeStruct(values.shape, values.dtype)
    out = call_blocks(
        functools.partial(first_pass_kernel, count),
        ids,
        values,
        [],
        row_pieces + col_pieces + [block_shape],
        [spare] * 2,
        first=True,
    )
    blocks = out[6]
    near = halve_rows(out[:2], col_groups, jnp.maximum)
    *product_pieces, turned = call_blocks(
        functools.partial(first_product_kernel, count),
        ids,
        blocks,
        [after(dual_start, near)],
        col_pieces + [block_shape],
        [spare],
    )
    share = scatter_cols(out[2:6], row_groups, jnp.maximum, near)
    share = after(share, product_pieces)
    row_peaks = join_rows(exchange_rows(near, col_groups, jnp.maximum), col_groups)
    *col_terms, row_scale = call_blocks(
        functools.partial(second_cols_kernel, count),
        ids,
        blocks,
        [turned] + after(row_peaks, share) + product_pieces,
        vectors(*[2 * quarter] * QUARTERS) + whole,
        [spare],
    )
    share = exchange_cols(share, row_groups, jnp.maximum, col_terms)
    col_peaks = gather_cols(share, row_groups)
    tile = lax.broadcasted_iota(jnp.int32, (2 * quarter, width), 0)

    def mixed(a, b):
        return jnp.where(tile < quarter, jnp.maximum(a, b), a + b)

    share = scatter_cols(after(col_terms, share), row_groups, mixed)
    near, far, col_scale = call_blocks(
        functools.partial(second_rows_kernel, count),
        ids,
        blocks,
        [turned] + col_peaks,
        row_pieces + whole,
        [spare],
    )
    near, far = after((near, far), share)
    share = exchange_cols(share, row_groups, mixed)
    row_scale, demand_squares = call_plain(
        functools.partial(row_scale_kernel, count),
        over_col([near, far], jnp.maximum) + [row_scale, demand],
        whole + squares,
    )
    demand_parts = sum_rows(demand_squares, row_groups)
    gathered = gather_cols(share, row_groups)
    col_scale, cost_squares = call_plain(
        functools.partial(col_scale_kernel, count),
        gathered + [col_scale, cost_vec],
        whole + squares,
    )
    cost_squares = sum_cols(after(cost_squares, demand_parts[1]), col_groups)
    norms = [cost_squares, tree_sum(demand_parts)]

    def forward(first, last, product, primal):
        out = call_blocks(
            functools.partial(forward_kernel, count, first, last),
            ids,
            turned,
            product + [col_scale, cost_vec, lower, upper, bound_kind, primal] + norms,
            whole + row_pieces,
            [count, spare],
            last=last,
        )
        return out[0], over_col(out[1:], jnp.add)

    primal, image = forward(True, False, gathered, primal_start)
    out = call_blocks(
        functools.partial(transposed_kernel, count, True),
        ids,
        blocks,
        image + [row_scale, demand, dual_start] + norms,
        whole + col_pieces,
        [count, spare],
    )
    dual, product = out[0], over_row(out[1:], jnp.add)
    primal, image = forward(False, True, product, primal)
    (dual,) = call_plain(
        functools.partial(last_dual_kernel, count, False),
        image + [row_scale, demand, dual] + norms,
        whole,
    )
    return primal.reshape(col_length), dual.reshape(row_length)


def solution(mesh):
    def body(*args):
        return per_device(mesh.shape["row"], mesh.shape["col"], *args)

    return jax.shard_map(
        body,
        mesh=mesh,
        in_specs=(
            P("row", "col", None, None, None),
            P("row", "col", None),
            P("row", "col", None),
            P("col"),
            P("row"),
            P("col"),
            P("col"),
            P("col"),
            P("col"),
            P("row"),
        ),
        out_specs=(P("col"), P("row")),
        check_vma=False,
    )
```

```python
import functools

import jax
import jax.numpy as jnp
from jax import lax
from jax.experimental import pallas as pl
from jax.experimental.pallas import tpu as pltpu
from jax.sharding import PartitionSpec as P

SMALL_EPS = 1e-06
STEP_SCALE = 0.3

CHUNKS = 8
FIRST_GROUP = 32
GROUP = 64
AHEAD = 3
ROW_HALVING = 1
QUARTERS = 4
FIRST_VMEM = 44 * 1024 * 1024
BLOCK_VMEM = 20 * 1024 * 1024
SMALL_VMEM = 8 * 1024 * 1024


def bit_of(index, bit):
    return jnp.where((index & bit) != 0, 1, 0)


def row_mask():
    return bit_of(lax.axis_index("col"), ROW_HALVING) * (CHUNKS // 2)


def col_mask():
    return (lax.axis_index("row") & (QUARTERS - 1)) * (CHUNKS // QUARTERS)


def col_place(tile, count, mask):
    return jnp.where(tile < 0, count, tile ^ (mask * (count // CHUNKS)))


def row_place(tile, count, mask):
    return jnp.where(tile < 0, count, tile ^ (mask * (count // CHUNKS)))


def chunk_rows(chunk, size):
    return pl.ds(pl.multiple_of(chunk * size, size), size)


def piece_chunk(pieces, place, size, offset=0):
    per_piece = CHUNKS // len(pieces)
    start = offset + (place % per_piece) * size
    return pieces[place // per_piece], pl.ds(start, size)


def store_pieces(acc, pieces, count):
    size = count // len(pieces)
    for index, piece in enumerate(pieces):
        piece[...] = acc[pl.ds(index * size, size), :]


def add_row(acc, place, term, combine):
    acc[pl.ds(place, 1), :] = combine(acc[pl.ds(place, 1), :], term)


def one_row(ref, tile):
    return ref[pl.ds(jnp.maximum(tile, 0), 1), :]


def tree_of(parts, combine):
    while len(parts) > 1:
        parts = [combine(parts[i], parts[i + 1]) for i in range(0, len(parts), 2)]
    return parts[0]


def tree_sum(parts):
    return tree_of(parts, jnp.add)


def fold_rows(values):
    return jnp.sum(values.reshape(-1, 8, values.shape[-1]), axis=0)


def block_copy(index, values_ref, blocks, arrived):
    part = pl.ds(pl.multiple_of(index * FIRST_GROUP, FIRST_GROUP), FIRST_GROUP)
    return pltpu.make_async_copy(values_ref.at[part], blocks.at[part], arrived.at[index])


def for_slots(ids_ref, visit, finish, group=GROUP, before=None):
    count = ids_ref.shape[0] // 2

    def step(index, carry):
        if before is not None:
            before(index)
        slots = [index * group + inner for inner in range(group)]
        ids = [(ids_ref[slot], ids_ref[count + slot]) for slot in slots]
        terms = visit(slots, ids)
        for (row, col), term in zip(ids, terms):
            finish(row, col, term)
        return carry

    lax.fori_loop(0, count // group, step, 0)


def product_terms(vector_ref, tiles, blocks):
    width = vector_ref.shape[1]
    place = lax.broadcasted_iota(jnp.int32, (8, width), 0)
    terms = []
    for start in range(0, len(tiles), 4):
        rows = [one_row(vector_ref, tile) for tile in tiles[start : start + 4]]
        left = jnp.where(place == 0, rows[0], jnp.where(place == 1, rows[1], 0.0))
        right = jnp.where(place == 2, rows[2], jnp.where(place == 3, rows[3], 0.0))
        quad = blocks[start : start + 4]
        found = jnp.dot(
            jnp.concatenate([left, right], axis=1).astype(jnp.bfloat16),
            jnp.concatenate(
                [jnp.concatenate(quad[:2], axis=1), jnp.concatenate(quad[2:], axis=1)], axis=0
            ),
            preferred_element_type=jnp.float32,
        )
        for index in range(4):
            side = (index % 2) * width
            terms.append(found[index : index + 1, side : side + width])
    return terms


def row_max(values):
    return jnp.max(values, axis=0, keepdims=True)


def packed_max(values):
    folded = jnp.max(values.reshape(-1, 16, values.shape[-1]), axis=0)
    return row_max(folded.astype(jnp.float32))


def first_pass_kernel(count, ids_ref, values_ref, *refs):
    row_out, col_out, blocks = refs[:2], refs[2:6], refs[6]
    arrived, row_acc, col_acc = refs[7:]
    mask, across = col_mask(), row_mask()
    groups = values_ref.shape[0] // FIRST_GROUP
    for index in range(min(AHEAD, groups)):
        block_copy(index, values_ref, blocks, arrived).start()
    for acc in (row_acc, col_acc):
        acc[...] = jnp.zeros_like(acc)

    def before(index):
        block_copy(index, values_ref, blocks, arrived).wait()

        @pl.when(index + AHEAD < groups)
        def _():
            block_copy(index + AHEAD, values_ref, blocks, arrived).start()

    def visit(slots, ids):
        sizes = [jnp.abs(blocks[slot]) for slot in slots]
        return [(packed_max(size.T), packed_max(size)) for size in sizes]

    def finish(row, col, terms):
        add_row(row_acc, row_place(row, count, across), terms[0], jnp.maximum)
        add_row(col_acc, col_place(col, count, mask), terms[1], jnp.maximum)

    for_slots(ids_ref, visit, finish, FIRST_GROUP, before)
    store_pieces(row_acc, row_out, count)
    store_pieces(col_acc, col_out, count)


def first_product_kernel(count, ids_ref, blocks, dual_ref, *refs):
    product_out, turned, product_acc = refs[:4], refs[4], refs[5]
    mask = col_mask()
    product_acc[...] = jnp.zeros_like(product_acc)

    def visit(slots, ids):
        found = [blocks[slot] for slot in slots]
        for slot, block in zip(slots, found):
            turned[slot] = block.T
        return product_terms(dual_ref, [row for row, _ in ids], found)

    def finish(row, col, term):
        add_row(product_acc, col_place(col, count, mask), term, jnp.add)

    for_slots(ids_ref, visit, finish)
    store_pieces(product_acc, product_out, count)


def scaled_peaks(slots, scales, direct, flipped):
    width = direct.shape[-1]
    square = (width, width)
    diagonal = lax.broadcasted_iota(jnp.int32, square, 0) == lax.broadcasted_iota(
        jnp.int32, square, 1
    )
    diagonal = diagonal.astype(jnp.float32).astype(jnp.bfloat16)
    found = []
    for index, (slot, scale) in enumerate(zip(slots, scales)):
        if index % 2:
            scaled = (jnp.abs(flipped[slot]).astype(jnp.float32) * scale).T
        else:
            sizes = jnp.abs(direct[slot])
            high = scale.astype(jnp.bfloat16)
            low = (scale - high.astype(jnp.float32)).astype(jnp.bfloat16)
            scaled = jnp.dot(
                jnp.concatenate([diagonal * high, diagonal * low], axis=1),
                jnp.concatenate([sizes, sizes], axis=0),
                preferred_element_type=jnp.float32,
            )
        found.append(row_max(scaled))
    return found


def second_cols_kernel(count, ids_ref, blocks, turned, *refs):
    row_in, col_out, row_scale, col_acc = refs[:2], refs[2:6], refs[6], refs[7]
    mask, across = col_mask(), row_mask()
    size = count // CHUNKS
    col_acc[...] = jnp.zeros_like(col_acc)
    for place in range(CHUNKS):
        piece, part = piece_chunk(row_in, place, size)
        row_scale[chunk_rows(place ^ across, size), :] = lax.rsqrt(piece[part, :] + SMALL_EPS)

    def visit(slots, ids):
        scales = [one_row(row_scale, row) for row, _ in ids]
        return scaled_peaks(slots, scales, blocks, turned)

    def finish(row, col, term):
        add_row(col_acc, col_place(col, count, mask), term, jnp.maximum)

    for_slots(ids_ref, visit, finish)
    store_pieces(col_acc, col_out, count)


def second_rows_kernel(count, ids_ref, blocks, turned, *refs):
    col_in, row_out, col_scale, row_acc = refs[:4], refs[4:6], refs[6], refs[7]
    mask, across = col_mask(), row_mask()
    size = count // CHUNKS
    row_acc[...] = jnp.zeros_like(row_acc)
    for place in range(CHUNKS):
        piece, part = piece_chunk(col_in, place, size)
        col_scale[chunk_rows(place ^ mask, size), :] = lax.rsqrt(piece[part, :] + SMALL_EPS)

    def visit(slots, ids):
        scales = [one_row(col_scale, col) for _, col in ids]
        return scaled_peaks(slots, scales, turned, blocks)

    def finish(row, col, term):
        add_row(row_acc, row_place(row, count, across), term, jnp.maximum)

    for_slots(ids_ref, visit, finish)
    store_pieces(row_acc, row_out, count)


def next_scale(scale, piece, inside):
    return scale * lax.rsqrt(scale * piece[inside, :] + SMALL_EPS)


def row_scale_kernel(count, near, far, scale_ref, vector_ref, new_scale, squares):
    across = row_mask()
    size = count // CHUNKS
    sums = []
    for place in range(CHUNKS):
        part = chunk_rows(place ^ across, size)
        piece, inside = piece_chunk((near, far), place, size)
        scale = next_scale(scale_ref[part, :], piece, inside)
        new_scale[part, :] = scale
        scaled = scale * vector_ref[part, :]
        sums.append(fold_rows(scaled * scaled))
    half = CHUNKS // 2
    squares[...] = tree_sum(sums[:half]) + tree_sum(sums[half:])


def col_scale_kernel(count, *refs):
    pieces, (scale_ref, vector_ref, new_scale, squares) = refs[:4], refs[4:]
    mask = col_mask()
    size = count // CHUNKS
    sums = []
    for place in range(CHUNKS):
        part = chunk_rows(place ^ mask, size)
        piece, inside = piece_chunk(pieces, place, size)
        scale = next_scale(scale_ref[part, :], piece, inside)
        new_scale[part, :] = scale
        scaled = scale * vector_ref[part, :]
        sums.append(fold_rows(scaled * scaled))
    squares[...] = tree_sum(sums)


def norm_ratio(cost_squares, demand_squares):
    cost_total = jnp.sum(cost_squares[...], keepdims=True)
    demand_total = jnp.sum(demand_squares[...], keepdims=True)
    return jnp.sqrt(cost_total + SMALL_EPS) / jnp.sqrt(demand_total + SMALL_EPS)


def forward_kernel(count, first, last, ids_ref, turned, *refs):
    product, refs = refs[:4], refs[4:]
    scale_ref, cost_ref, low_ref, high_ref, kind_ref, primal_ref = refs[:6]
    cost_squares, demand_squares, primal_out = refs[6:9]
    row_out, refs = refs[9:11], refs[11:]
    shifted, row_acc = refs[:2]
    moved_ref = primal_out
    if last:
        moved_ref, written = refs[2:]
    mask, across = col_mask(), row_mask()
    size = count // CHUNKS
    row_acc[...] = jnp.zeros_like(row_acc)
    primal_step = STEP_SCALE / norm_ratio(cost_squares, demand_squares)
    for place in range(CHUNKS):
        part = chunk_rows(place ^ mask, size)
        behind = product[0].shape[0] - count // QUARTERS
        piece, inside = piece_chunk(product, place, size, behind)
        scale = scale_ref[part, :]
        inverse = 1.0 / scale
        primal = primal_ref[part, :]
        if first:
            primal = primal * inverse
        gradient = scale * piece[inside, :]
        moved = primal - primal_step * (scale * cost_ref[part, :] - gradient)
        kind = kind_ref[part, :]
        moved = jnp.where(
            (kind == 1) | (kind == 3), jnp.maximum(moved, low_ref[part, :] * inverse), moved
        )
        moved = jnp.where(
            (kind == 2) | (kind == 3), jnp.minimum(moved, high_ref[part, :] * inverse), moved
        )
        shifted[part, :] = scale * (2.0 * moved - primal)
        moved_ref[part, :] = scale * moved if last else moved

    if last:
        copy_out = pltpu.make_async_copy(moved_ref, primal_out, written)
        copy_out.start()

    def visit(slots, ids):
        return product_terms(shifted, [col for _, col in ids], [turned[slot] for slot in slots])

    def finish(row, col, term):
        add_row(row_acc, row_place(row, count, across), term, jnp.add)

    for_slots(ids_ref, visit, finish)
    store_pieces(row_acc, row_out, count)
    if last:
        copy_out.wait()


def next_dual(first, image, inside, scale, demand, dual, dual_step):
    if first:
        dual = dual / scale
    row_image = scale * image[inside, :]
    return jnp.maximum(dual + dual_step * (scale * demand - row_image), 0.0)


def transposed_kernel(count, first, ids_ref, blocks, *refs):
    image, refs = refs[:2], refs[2:]
    scale_ref, demand_ref, dual_ref, cost_squares, demand_squares, dual_out = refs[:6]
    product_out, (weights, product_acc) = refs[6:10], refs[10:]
    mask, across = col_mask(), row_mask()
    size = count // CHUNKS
    product_acc[...] = jnp.zeros_like(product_acc)
    dual_step = STEP_SCALE * norm_ratio(cost_squares, demand_squares)
    for place in range(CHUNKS):
        part = chunk_rows(place ^ across, size)
        piece, inside = piece_chunk(image, place, size)
        scale = scale_ref[part, :]
        dual = next_dual(
            first, piece, inside, scale, demand_ref[part, :], dual_ref[part, :], dual_step
        )
        dual_out[part, :] = dual
        weights[part, :] = scale * dual

    def visit(slots, ids):
        return product_terms(weights, [row for row, _ in ids], [blocks[slot] for slot in slots])

    def finish(row, col, term):
        add_row(product_acc, col_place(col, count, mask), term, jnp.add)

    for_slots(ids_ref, visit, finish)
    store_pieces(product_acc, product_out, count)


def last_dual_kernel(count, first, *refs):
    image, refs = refs[:2], refs[2:]
    scale_ref, demand_ref, dual_ref, cost_squares, demand_squares, dual_out = refs
    across = row_mask()
    size = count // CHUNKS
    dual_step = STEP_SCALE * norm_ratio(cost_squares, demand_squares)
    for place in range(CHUNKS):
        part = chunk_rows(place ^ across, size)
        piece, inside = piece_chunk(image, place, size)
        scale = scale_ref[part, :]
        dual = next_dual(
            first, piece, inside, scale, demand_ref[part, :], dual_ref[part, :], dual_step
        )
        dual_out[part, :] = scale * dual


def vectors(*row_counts):
    return [jax.ShapeDtypeStruct((rows, 128), jnp.float32) for rows in row_counts]


def call_plain(kernel, operands, out_shape):
    return pl.pallas_call(
        kernel,
        out_shape=out_shape,
        in_specs=[pl.BlockSpec(memory_space=pltpu.VMEM)] * len(operands),
        out_specs=[pl.BlockSpec(memory_space=pltpu.VMEM)] * len(out_shape),
        compiler_params=pltpu.CompilerParams(vmem_limit_bytes=SMALL_VMEM),
    )(*operands)


def call_blocks(kernel, ids, values, operands, out_shape, scratch, first=False, last=False):
    width = values.shape[1]
    scratch_shapes = [pltpu.VMEM((rows, width), jnp.float32) for rows in scratch]
    if first:
        arrivals = pltpu.SemaphoreType.DMA((values.shape[0] // FIRST_GROUP,))
        scratch_shapes = [arrivals] + scratch_shapes
    out_specs = [pl.BlockSpec(memory_space=pltpu.VMEM)] * len(out_shape)
    if last:
        out_specs[0] = pl.BlockSpec(memory_space=pl.ANY)
        scratch_shapes = scratch_shapes + [
            pltpu.VMEM(out_shape[0].shape, out_shape[0].dtype),
            pltpu.SemaphoreType.DMA,
        ]
    return pl.pallas_call(
        kernel,
        out_shape=out_shape,
        in_specs=[pl.BlockSpec(memory_space=pltpu.SMEM)]
        + [pl.BlockSpec(memory_space=pl.ANY if first else pltpu.VMEM)]
        + [pl.BlockSpec(memory_space=pltpu.VMEM)] * len(operands),
        out_specs=out_specs,
        scratch_shapes=scratch_shapes,
        compiler_params=pltpu.CompilerParams(
            vmem_limit_bytes=FIRST_VMEM if first else BLOCK_VMEM
        ),
        cost_estimate=pl.CostEstimate(
            flops=2 * values.size, bytes_accessed=2 * values.size, transcendentals=0
        ),
    )(ids, values, *operands)


def swap(vector, axis, size, bit):
    return lax.ppermute(vector, axis, [(i, i ^ bit) for i in range(size)])


def after(values, *earlier):
    return lax.optimization_barrier((values, earlier))[0]


def halve_rows(pieces, groups, combine):
    near, far = pieces
    return combine(near, swap(far, "col", groups, ROW_HALVING))


def exchange_rows(near, groups, combine):
    bit = 1
    while bit < groups:
        if bit != ROW_HALVING:
            near = combine(near, swap(near, "col", groups, bit))
        bit *= 2
    return near


def join_rows(near, groups):
    return [near, swap(near, "col", groups, ROW_HALVING)]


def scatter_cols(pieces, groups, combine, tie=None):
    diagonal = swap(pieces[3], "row", groups, 3)
    first, second = pieces[1:3] if tie is None else after((pieces[1], pieces[2]), tie)
    first, second = swap(first, "row", groups, 1), swap(second, "row", groups, 2)
    return tree_of([pieces[0], first, second, diagonal], combine)


def exchange_cols(piece, groups, combine):
    bit = QUARTERS
    while bit < groups:
        piece = combine(piece, swap(piece, "row", groups, bit))
        bit *= 2
    return piece


def gather_cols(piece, groups):
    diagonal = swap(piece, "row", groups, 3)
    return [piece, swap(piece, "row", groups, 1), swap(piece, "row", groups, 2), diagonal]


def sum_rows(vector, groups):
    vector = exchange_cols(vector, groups, jnp.add)
    return [vector] + [swap(vector, "row", groups, mask) for mask in (1, 2, 3)]


def sum_cols(vector, groups):
    parts = [vector] + [swap(vector, "col", groups, mask) for mask in range(1, groups)]
    return tree_sum(parts)


def per_device(
    row_groups,
    col_groups,
    block_values,
    block_rows,
    block_cols,
    cost_vec,
    demand,
    lower,
    upper,
    bound_kind,
    primal_start,
    dual_start,
):
    values = block_values[0, 0]
    width = values.shape[1]
    ids = jnp.concatenate([block_rows[0, 0], block_cols[0, 0]])
    row_length, col_length = demand.shape[0], cost_vec.shape[0]
    cost_vec, demand, lower, upper, bound_kind, primal_start, dual_start = [
        v.reshape(-1, width)
        for v in (cost_vec, demand, lower, upper, bound_kind, primal_start, dual_start)
    ]
    count = demand.shape[0]
    half, quarter, spare = count // 2, count // QUARTERS, count + 8
    row_pieces, col_pieces = vectors(half, half), vectors(*[quarter] * QUARTERS)
    whole = vectors(count)
    squares = vectors(8)

    def over_col(pieces, combine):
        near = exchange_rows(halve_rows(pieces, col_groups, combine), col_groups, combine)
        return join_rows(near, col_groups)

    def over_row(pieces, combine):
        share = scatter_cols(pieces, row_groups, combine)
        return gather_cols(exchange_cols(share, row_groups, combine), row_groups)

    block_shape = jax.ShapeDtypeStruct(values.shape, values.dtype)
    out = call_blocks(
        functools.partial(first_pass_kernel, count),
        ids,
        values,
        [],
        row_pieces + col_pieces + [block_shape],
        [spare] * 2,
        first=True,
    )
    blocks = out[6]
    near = halve_rows(out[:2], col_groups, jnp.maximum)
    *product_pieces, turned = call_blocks(
        functools.partial(first_product_kernel, count),
        ids,
        blocks,
        [after(dual_start, near)],
        col_pieces + [block_shape],
        [spare],
    )
    share = scatter_cols(out[2:6], row_groups, jnp.maximum, near)
    near = exchange_rows(near, col_groups, jnp.maximum)
    product = scatter_cols(after(product_pieces, near), row_groups, jnp.add)
    share = after(exchange_cols(share, row_groups, jnp.maximum), product_pieces)
    row_peaks = join_rows(near, col_groups)
    *col_pieces_2, row_scale = call_blocks(
        functools.partial(second_cols_kernel, count),
        ids,
        blocks,
        [turned] + after(row_peaks, share),
        col_pieces + whole,
        [spare],
    )
    col_peaks = gather_cols(share, row_groups)
    share = scatter_cols(after(col_pieces_2, col_peaks), row_groups, jnp.maximum)
    product = exchange_cols(product, row_groups, jnp.add)
    near, far, col_scale = call_blocks(
        functools.partial(second_rows_kernel, count),
        ids,
        blocks,
        [turned] + col_peaks,
        row_pieces + whole,
        [spare],
    )
    near, far = after((near, far), (share, product))
    share = exchange_cols(share, row_groups, jnp.maximum)
    row_scale, demand_squares = call_plain(
        functools.partial(row_scale_kernel, count),
        over_col([near, far], jnp.maximum) + [row_scale, demand],
        whole + squares,
    )
    demand_parts = sum_rows(demand_squares, row_groups)
    gathered = gather_cols(jnp.concatenate([share, product], axis=0), row_groups)
    col_scale, cost_squares = call_plain(
        functools.partial(col_scale_kernel, count),
        gathered + [col_scale, cost_vec],
        whole + squares,
    )
    cost_squares = sum_cols(after(cost_squares, demand_parts[1]), col_groups)
    norms = [cost_squares, tree_sum(demand_parts)]

    def forward(first, last, product, primal):
        out = call_blocks(
            functools.partial(forward_kernel, count, first, last),
            ids,
            turned,
            product + [col_scale, cost_vec, lower, upper, bound_kind, primal] + norms,
            whole + row_pieces,
            [count, spare],
            last=last,
        )
        return out[0], over_col(out[1:], jnp.add)

    primal, image = forward(True, False, gathered, primal_start)
    out = call_blocks(
        functools.partial(transposed_kernel, count, True),
        ids,
        blocks,
        image + [row_scale, demand, dual_start] + norms,
        whole + col_pieces,
        [count, spare],
    )
    dual, product = out[0], over_row(out[1:], jnp.add)
    primal, image = forward(False, True, product, primal)
    (dual,) = call_plain(
        functools.partial(last_dual_kernel, count, False),
        image + [row_scale, demand, dual] + norms,
        whole,
    )
    return primal.reshape(col_length), dual.reshape(row_length)


def solution(mesh):
    def body(*args):
        return per_device(mesh.shape["row"], mesh.shape["col"], *args)

    return jax.shard_map(
        body,
        mesh=mesh,
        in_specs=(
            P("row", "col", None, None, None),
            P("row", "col", None),
            P("row", "col", None),
            P("col"),
            P("row"),
            P("col"),
            P("col"),
            P("col"),
            P("col"),
            P("row"),
        ),
        out_specs=(P("col"), P("row")),
        check_vma=False,
    )
```

```python
import functools

import jax
import jax.numpy as jnp
from jax import lax
from jax.experimental import pallas as pl
from jax.experimental.pallas import tpu as pltpu
from jax.sharding import PartitionSpec as P

SMALL_EPS = 1e-06
STEP_SCALE = 0.3

CHUNKS = 8
FIRST_GROUP = 32
GROUP = 128
AHEAD = 3
ROW_HALVING = 1
QUARTERS = 4
FIRST_VMEM = 44 * 1024 * 1024
BLOCK_VMEM = 20 * 1024 * 1024
SMALL_VMEM = 8 * 1024 * 1024


def bit_of(index, bit):
    return jnp.where((index & bit) != 0, 1, 0)


def row_mask():
    return bit_of(lax.axis_index("col"), ROW_HALVING) * (CHUNKS // 2)


def col_mask():
    return (lax.axis_index("row") & (QUARTERS - 1)) * (CHUNKS // QUARTERS)


def col_place(tile, count, mask):
    return jnp.where(tile < 0, count, tile ^ (mask * (count // CHUNKS)))


def row_place(tile, count, mask):
    return jnp.where(tile < 0, count, tile ^ (mask * (count // CHUNKS)))


def chunk_rows(chunk, size):
    return pl.ds(pl.multiple_of(chunk * size, size), size)


def piece_chunk(pieces, place, size, offset=0):
    per_piece = CHUNKS // len(pieces)
    start = offset + (place % per_piece) * size
    return pieces[place // per_piece], pl.ds(start, size)


def store_pieces(acc, pieces, count):
    size = count // len(pieces)
    for index, piece in enumerate(pieces):
        piece[...] = acc[pl.ds(index * size, size), :]


def add_row(acc, place, term, combine):
    acc[pl.ds(place, 1), :] = combine(acc[pl.ds(place, 1), :], term)


def one_row(ref, tile):
    return ref[pl.ds(jnp.maximum(tile, 0), 1), :]


def tree_of(parts, combine):
    while len(parts) > 1:
        parts = [combine(parts[i], parts[i + 1]) for i in range(0, len(parts), 2)]
    return parts[0]


def tree_sum(parts):
    return tree_of(parts, jnp.add)


def fold_rows(values):
    return jnp.sum(values.reshape(-1, 8, values.shape[-1]), axis=0)


def block_copy(index, values_ref, blocks, arrived):
    part = pl.ds(pl.multiple_of(index * FIRST_GROUP, FIRST_GROUP), FIRST_GROUP)
    return pltpu.make_async_copy(values_ref.at[part], blocks.at[part], arrived.at[index])


def for_slots(ids_ref, visit, finish, group=GROUP, before=None):
    count = ids_ref.shape[0] // 2

    def step(index, carry):
        if before is not None:
            before(index)
        slots = [index * group + inner for inner in range(group)]
        ids = [(ids_ref[slot], ids_ref[count + slot]) for slot in slots]
        terms = visit(slots, ids)
        for (row, col), term in zip(ids, terms):
            finish(row, col, term)
        return carry

    lax.fori_loop(0, count // group, step, 0)


def product_terms(vector_ref, tiles, blocks):
    width = vector_ref.shape[1]
    place = lax.broadcasted_iota(jnp.int32, (8, width), 0)
    terms = []
    for start in range(0, len(tiles), 4):
        rows = [one_row(vector_ref, tile) for tile in tiles[start : start + 4]]
        left = jnp.where(place == 0, rows[0], jnp.where(place == 1, rows[1], 0.0))
        right = jnp.where(place == 2, rows[2], jnp.where(place == 3, rows[3], 0.0))
        quad = blocks[start : start + 4]
        found = jnp.dot(
            jnp.concatenate([left, right], axis=1).astype(jnp.bfloat16),
            jnp.concatenate(
                [jnp.concatenate(quad[:2], axis=1), jnp.concatenate(quad[2:], axis=1)], axis=0
            ),
            preferred_element_type=jnp.float32,
        )
        for index in range(4):
            side = (index % 2) * width
            terms.append(found[index : index + 1, side : side + width])
    return terms


def row_max(values):
    return jnp.max(values, axis=0, keepdims=True)


def packed_max(values):
    folded = jnp.max(values.reshape(-1, 16, values.shape[-1]), axis=0)
    return row_max(folded.astype(jnp.float32))


def first_pass_kernel(count, ids_ref, values_ref, *refs):
    row_out, col_out, blocks = refs[:2], refs[2:6], refs[6]
    arrived, row_acc, col_acc = refs[7:]
    mask, across = col_mask(), row_mask()
    groups = values_ref.shape[0] // FIRST_GROUP
    for index in range(min(AHEAD, groups)):
        block_copy(index, values_ref, blocks, arrived).start()
    for acc in (row_acc, col_acc):
        acc[...] = jnp.zeros_like(acc)

    def before(index):
        block_copy(index, values_ref, blocks, arrived).wait()

        @pl.when(index + AHEAD < groups)
        def _():
            block_copy(index + AHEAD, values_ref, blocks, arrived).start()

    def visit(slots, ids):
        sizes = [jnp.abs(blocks[slot]) for slot in slots]
        return [(packed_max(size.T), packed_max(size)) for size in sizes]

    def finish(row, col, terms):
        add_row(row_acc, row_place(row, count, across), terms[0], jnp.maximum)
        add_row(col_acc, col_place(col, count, mask), terms[1], jnp.maximum)

    for_slots(ids_ref, visit, finish, FIRST_GROUP, before)
    store_pieces(row_acc, row_out, count)
    store_pieces(col_acc, col_out, count)


def first_product_kernel(count, ids_ref, blocks, dual_ref, *refs):
    product_out, turned, product_acc = refs[:4], refs[4], refs[5]
    mask = col_mask()
    product_acc[...] = jnp.zeros_like(product_acc)

    def visit(slots, ids):
        found = [blocks[slot] for slot in slots]
        for slot, block in zip(slots, found):
            turned[slot] = block.T
        return product_terms(dual_ref, [row for row, _ in ids], found)

    def finish(row, col, term):
        add_row(product_acc, col_place(col, count, mask), term, jnp.add)

    for_slots(ids_ref, visit, finish)
    store_pieces(product_acc, product_out, count)


def scaled_peaks(slots, scales, direct, flipped):
    width = direct.shape[-1]
    square = (width, width)
    diagonal = lax.broadcasted_iota(jnp.int32, square, 0) == lax.broadcasted_iota(
        jnp.int32, square, 1
    )
    diagonal = diagonal.astype(jnp.float32).astype(jnp.bfloat16)
    found = []
    for index, (slot, scale) in enumerate(zip(slots, scales)):
        if index % 2:
            scaled = (jnp.abs(flipped[slot]).astype(jnp.float32) * scale).T
        else:
            sizes = jnp.abs(direct[slot])
            high = scale.astype(jnp.bfloat16)
            low = (scale - high.astype(jnp.float32)).astype(jnp.bfloat16)
            scaled = jnp.dot(
                jnp.concatenate([diagonal * high, diagonal * low], axis=1),
                jnp.concatenate([sizes, sizes], axis=0),
                preferred_element_type=jnp.float32,
            )
        found.append(row_max(scaled))
    return found


def second_cols_kernel(count, ids_ref, blocks, turned, *refs):
    row_in, col_out, row_scale, col_acc = refs[:2], refs[2:6], refs[6], refs[7]
    mask, across = col_mask(), row_mask()
    size = count // CHUNKS
    col_acc[...] = jnp.zeros_like(col_acc)
    for place in range(CHUNKS):
        piece, part = piece_chunk(row_in, place, size)
        row_scale[chunk_rows(place ^ across, size), :] = lax.rsqrt(piece[part, :] + SMALL_EPS)

    def visit(slots, ids):
        scales = [one_row(row_scale, row) for row, _ in ids]
        return scaled_peaks(slots, scales, blocks, turned)

    def finish(row, col, term):
        add_row(col_acc, col_place(col, count, mask), term, jnp.maximum)

    for_slots(ids_ref, visit, finish)
    store_pieces(col_acc, col_out, count)


def second_rows_kernel(count, ids_ref, blocks, turned, *refs):
    col_in, row_out, col_scale, row_acc = refs[:4], refs[4:6], refs[6], refs[7]
    mask, across = col_mask(), row_mask()
    size = count // CHUNKS
    row_acc[...] = jnp.zeros_like(row_acc)
    for place in range(CHUNKS):
        piece, part = piece_chunk(col_in, place, size)
        col_scale[chunk_rows(place ^ mask, size), :] = lax.rsqrt(piece[part, :] + SMALL_EPS)

    def visit(slots, ids):
        scales = [one_row(col_scale, col) for _, col in ids]
        return scaled_peaks(slots, scales, turned, blocks)

    def finish(row, col, term):
        add_row(row_acc, row_place(row, count, across), term, jnp.maximum)

    for_slots(ids_ref, visit, finish)
    store_pieces(row_acc, row_out, count)


def next_scale(scale, piece, inside):
    return scale * lax.rsqrt(scale * piece[inside, :] + SMALL_EPS)


def row_scale_kernel(count, near, far, scale_ref, new_scale):
    across = row_mask()
    size = count // CHUNKS
    for place in range(CHUNKS):
        part = chunk_rows(place ^ across, size)
        piece, inside = piece_chunk((near, far), place, size)
        new_scale[part, :] = next_scale(scale_ref[part, :], piece, inside)


def demand_kernel(count, near, scale_ref, demand_ref, squares):
    across = row_mask()
    size = count // CHUNKS
    sums = []
    for place in range(CHUNKS // 2):
        part = chunk_rows(place ^ across, size)
        scale = next_scale(scale_ref[part, :], near, pl.ds(place * size, size))
        scaled = scale * demand_ref[part, :]
        sums.append(fold_rows(scaled * scaled))
    squares[...] = tree_sum(sums)


def col_scale_kernel(count, *refs):
    pieces, (scale_ref, vector_ref, new_scale, squares) = refs[:4], refs[4:]
    mask = col_mask()
    size = count // CHUNKS
    sums = []
    for place in range(CHUNKS):
        part = chunk_rows(place ^ mask, size)
        piece, inside = piece_chunk(pieces, place, size)
        scale = next_scale(scale_ref[part, :], piece, inside)
        new_scale[part, :] = scale
        scaled = scale * vector_ref[part, :]
        sums.append(fold_rows(scaled * scaled))
    squares[...] = tree_sum(sums)


def norm_ratio(cost_squares, demand_squares):
    cost_total = jnp.sum(cost_squares[...], keepdims=True)
    demand_total = jnp.sum(demand_squares[...], keepdims=True)
    return jnp.sqrt(cost_total + SMALL_EPS) / jnp.sqrt(demand_total + SMALL_EPS)


def forward_kernel(count, first, last, ids_ref, turned, *refs):
    product, refs = refs[:4], refs[4:]
    scale_ref, cost_ref, low_ref, high_ref, kind_ref, primal_ref = refs[:6]
    cost_squares, demand_squares, primal_out = refs[6:9]
    row_out, refs = refs[9:11], refs[11:]
    shifted, row_acc = refs[:2]
    moved_ref = primal_out
    if last:
        moved_ref, written = refs[2:]
    mask, across = col_mask(), row_mask()
    size = count // CHUNKS
    row_acc[...] = jnp.zeros_like(row_acc)
    primal_step = STEP_SCALE / norm_ratio(cost_squares, demand_squares)
    for place in range(CHUNKS):
        part = chunk_rows(place ^ mask, size)
        behind = product[0].shape[0] - count // QUARTERS
        piece, inside = piece_chunk(product, place, size, behind)
        scale = scale_ref[part, :]
        inverse = 1.0 / scale
        primal = primal_ref[part, :]
        if first:
            primal = primal * inverse
        gradient = scale * piece[inside, :]
        moved = primal - primal_step * (scale * cost_ref[part, :] - gradient)
        kind = kind_ref[part, :]
        moved = jnp.where(
            (kind == 1) | (kind == 3), jnp.maximum(moved, low_ref[part, :] * inverse), moved
        )
        moved = jnp.where(
            (kind == 2) | (kind == 3), jnp.minimum(moved, high_ref[part, :] * inverse), moved
        )
        shifted[part, :] = scale * (2.0 * moved - primal)
        moved_ref[part, :] = scale * moved if last else moved

    if last:
        copy_out = pltpu.make_async_copy(moved_ref, primal_out, written)
        copy_out.start()

    def visit(slots, ids):
        return product_terms(shifted, [col for _, col in ids], [turned[slot] for slot in slots])

    def finish(row, col, term):
        add_row(row_acc, row_place(row, count, across), term, jnp.add)

    for_slots(ids_ref, visit, finish)
    store_pieces(row_acc, row_out, count)
    if last:
        copy_out.wait()


def next_dual(first, image, inside, scale, demand, dual, dual_step):
    if first:
        dual = dual / scale
    row_image = scale * image[inside, :]
    return jnp.maximum(dual + dual_step * (scale * demand - row_image), 0.0)


def transposed_kernel(count, first, ids_ref, blocks, *refs):
    image, refs = refs[:2], refs[2:]
    scale_ref, demand_ref, dual_ref, cost_squares, demand_squares, dual_out = refs[:6]
    product_out, (weights, product_acc) = refs[6:10], refs[10:]
    mask, across = col_mask(), row_mask()
    size = count // CHUNKS
    product_acc[...] = jnp.zeros_like(product_acc)
    dual_step = STEP_SCALE * norm_ratio(cost_squares, demand_squares)
    for place in range(CHUNKS):
        part = chunk_rows(place ^ across, size)
        piece, inside = piece_chunk(image, place, size)
        scale = scale_ref[part, :]
        dual = next_dual(
            first, piece, inside, scale, demand_ref[part, :], dual_ref[part, :], dual_step
        )
        dual_out[part, :] = dual
        weights[part, :] = scale * dual

    def visit(slots, ids):
        return product_terms(weights, [row for row, _ in ids], [blocks[slot] for slot in slots])

    def finish(row, col, term):
        add_row(product_acc, col_place(col, count, mask), term, jnp.add)

    for_slots(ids_ref, visit, finish)
    store_pieces(product_acc, product_out, count)


def last_dual_kernel(count, first, *refs):
    image, refs = refs[:2], refs[2:]
    scale_ref, demand_ref, dual_ref, cost_squares, demand_squares, dual_out = refs
    across = row_mask()
    size = count // CHUNKS
    dual_step = STEP_SCALE * norm_ratio(cost_squares, demand_squares)
    for place in range(CHUNKS):
        part = chunk_rows(place ^ across, size)
        piece, inside = piece_chunk(image, place, size)
        scale = scale_ref[part, :]
        dual = next_dual(
            first, piece, inside, scale, demand_ref[part, :], dual_ref[part, :], dual_step
        )
        dual_out[part, :] = scale * dual


def vectors(*row_counts):
    return [jax.ShapeDtypeStruct((rows, 128), jnp.float32) for rows in row_counts]


def call_plain(kernel, operands, out_shape):
    return pl.pallas_call(
        kernel,
        out_shape=out_shape,
        in_specs=[pl.BlockSpec(memory_space=pltpu.VMEM)] * len(operands),
        out_specs=[pl.BlockSpec(memory_space=pltpu.VMEM)] * len(out_shape),
        compiler_params=pltpu.CompilerParams(vmem_limit_bytes=SMALL_VMEM),
    )(*operands)


def call_blocks(kernel, ids, values, operands, out_shape, scratch, first=False, last=False):
    width = values.shape[1]
    scratch_shapes = [pltpu.VMEM((rows, width), jnp.float32) for rows in scratch]
    if first:
        arrivals = pltpu.SemaphoreType.DMA((values.shape[0] // FIRST_GROUP,))
        scratch_shapes = [arrivals] + scratch_shapes
    out_specs = [pl.BlockSpec(memory_space=pltpu.VMEM)] * len(out_shape)
    if last:
        out_specs[0] = pl.BlockSpec(memory_space=pl.ANY)
        scratch_shapes = scratch_shapes + [
            pltpu.VMEM(out_shape[0].shape, out_shape[0].dtype),
            pltpu.SemaphoreType.DMA,
        ]
    return pl.pallas_call(
        kernel,
        out_shape=out_shape,
        in_specs=[pl.BlockSpec(memory_space=pltpu.SMEM)]
        + [pl.BlockSpec(memory_space=pl.ANY if first else pltpu.VMEM)]
        + [pl.BlockSpec(memory_space=pltpu.VMEM)] * len(operands),
        out_specs=out_specs,
        scratch_shapes=scratch_shapes,
        compiler_params=pltpu.CompilerParams(
            vmem_limit_bytes=FIRST_VMEM if first else BLOCK_VMEM
        ),
        cost_estimate=pl.CostEstimate(
            flops=2 * values.size, bytes_accessed=2 * values.size, transcendentals=0
        ),
    )(ids, values, *operands)


def swap(vector, axis, size, bit):
    return lax.ppermute(vector, axis, [(i, i ^ bit) for i in range(size)])


def after(values, *earlier):
    return lax.optimization_barrier((values, earlier))[0]


def halve_rows(pieces, groups, combine):
    near, far = pieces
    return combine(near, swap(far, "col", groups, ROW_HALVING))


def exchange_rows(near, groups, combine):
    bit = 1
    while bit < groups:
        if bit != ROW_HALVING:
            near = combine(near, swap(near, "col", groups, bit))
        bit *= 2
    return near


def join_rows(near, groups):
    return [near, swap(near, "col", groups, ROW_HALVING)]


def scatter_cols(pieces, groups, combine, tie=None):
    diagonal = swap(pieces[3], "row", groups, 3)
    first, second = pieces[1:3] if tie is None else after((pieces[1], pieces[2]), tie)
    first, second = swap(first, "row", groups, 1), swap(second, "row", groups, 2)
    return tree_of([pieces[0], first, second, diagonal], combine)


def exchange_cols(piece, groups, combine, tie=None):
    bit = QUARTERS
    while bit < groups:
        got = swap(piece, "row", groups, bit)
        piece = combine(piece, got if tie is None else after(got, tie))
        bit *= 2
    return piece


def gather_cols(piece, groups):
    diagonal = swap(piece, "row", groups, 3)
    return [piece, swap(piece, "row", groups, 1), swap(piece, "row", groups, 2), diagonal]


def sum_rows(vector, groups, tie):
    vector = exchange_cols(vector, groups, jnp.add, tie)
    return [vector] + [swap(vector, "row", groups, mask) for mask in (1, 2, 3)]


def sum_norms(cost_squares, demand_squares, groups):
    rows = cost_squares.shape[0]
    both = jnp.concatenate([cost_squares, demand_squares], axis=0)
    parts = [both] + [swap(both, "col", groups, mask) for mask in range(1, groups)]
    cost_total = tree_sum([part[:rows] for part in parts])
    demand_total = parts[0][rows:] + parts[ROW_HALVING][rows:]
    return [cost_total, demand_total]


def per_device(
    row_groups,
    col_groups,
    block_values,
    block_rows,
    block_cols,
    cost_vec,
    demand,
    lower,
    upper,
    bound_kind,
    primal_start,
    dual_start,
):
    values = block_values[0, 0]
    width = values.shape[1]
    ids = jnp.concatenate([block_rows[0, 0], block_cols[0, 0]])
    row_length, col_length = demand.shape[0], cost_vec.shape[0]
    cost_vec, demand, lower, upper, bound_kind, primal_start, dual_start = [
        v.reshape(-1, width)
        for v in (cost_vec, demand, lower, upper, bound_kind, primal_start, dual_start)
    ]
    count = demand.shape[0]
    half, quarter, spare = count // 2, count // QUARTERS, count + 8
    row_pieces, col_pieces = vectors(half, half), vectors(*[quarter] * QUARTERS)
    whole = vectors(count)
    squares = vectors(8)

    def over_col(pieces, combine):
        near = exchange_rows(halve_rows(pieces, col_groups, combine), col_groups, combine)
        return join_rows(near, col_groups)

    def over_row(pieces, combine):
        share = scatter_cols(pieces, row_groups, combine)
        return gather_cols(exchange_cols(share, row_groups, combine), row_groups)

    block_shape = jax.ShapeDtypeStruct(values.shape, values.dtype)
    out = call_blocks(
        functools.partial(first_pass_kernel, count),
        ids,
        values,
        [],
        row_pieces + col_pieces + [block_shape],
        [spare] * 2,
        first=True,
    )
    blocks = out[6]
    near = halve_rows(out[:2], col_groups, jnp.maximum)
    *product_pieces, turned = call_blocks(
        functools.partial(first_product_kernel, count),
        ids,
        blocks,
        [after(dual_start, near)],
        col_pieces + [block_shape],
        [spare],
    )
    share = scatter_cols(out[2:6], row_groups, jnp.maximum, near)
    near = exchange_rows(near, col_groups, jnp.maximum)
    product = scatter_cols(after(product_pieces, near), row_groups, jnp.add)
    share = after(exchange_cols(share, row_groups, jnp.maximum), product_pieces)
    row_peaks = join_rows(near, col_groups)
    *col_pieces_2, row_scale = call_blocks(
        functools.partial(second_cols_kernel, count),
        ids,
        blocks,
        [turned] + after(row_peaks, share),
        col_pieces + whole,
        [spare],
    )
    col_peaks = gather_cols(share, row_groups)
    share = scatter_cols(after(col_pieces_2, col_peaks), row_groups, jnp.maximum)
    product = exchange_cols(product, row_groups, jnp.add)
    near, far, col_scale = call_blocks(
        functools.partial(second_rows_kernel, count),
        ids,
        blocks,
        [turned] + col_peaks,
        row_pieces + whole,
        [spare],
    )
    near, far = after((near, far), (share, product))
    near = halve_rows([near, far], col_groups, jnp.maximum)
    near = exchange_rows(near, col_groups, jnp.maximum)
    (demand_squares,) = call_plain(
        functools.partial(demand_kernel, count), [near, row_scale, demand], squares
    )
    (row_scale,) = call_plain(
        functools.partial(row_scale_kernel, count),
        join_rows(near, col_groups) + [row_scale],
        whole,
    )
    share = exchange_cols(share, row_groups, jnp.maximum, demand_squares)
    gathered = gather_cols(jnp.concatenate([share, product], axis=0), row_groups)
    demand_parts = sum_rows(demand_squares, row_groups, gathered[1])
    col_scale, cost_squares = call_plain(
        functools.partial(col_scale_kernel, count),
        gathered + [col_scale, cost_vec],
        whole + squares,
    )
    norms = sum_norms(cost_squares, tree_sum(demand_parts), col_groups)

    def forward(first, last, product, primal):
        out = call_blocks(
            functools.partial(forward_kernel, count, first, last),
            ids,
            turned,
            product + [col_scale, cost_vec, lower, upper, bound_kind, primal] + norms,
            whole + row_pieces,
            [count, spare],
            last=last,
        )
        return out[0], over_col(out[1:], jnp.add)

    primal, image = forward(True, False, gathered, primal_start)
    out = call_blocks(
        functools.partial(transposed_kernel, count, True),
        ids,
        blocks,
        image + [row_scale, demand, dual_start] + norms,
        whole + col_pieces,
        [count, spare],
    )
    dual, product = out[0], over_row(out[1:], jnp.add)
    primal, image = forward(False, True, product, primal)
    (dual,) = call_plain(
        functools.partial(last_dual_kernel, count, False),
        image + [row_scale, demand, dual] + norms,
        whole,
    )
    return primal.reshape(col_length), dual.reshape(row_length)


def solution(mesh):
    def body(*args):
        return per_device(mesh.shape["row"], mesh.shape["col"], *args)

    return jax.shard_map(
        body,
        mesh=mesh,
        in_specs=(
            P("row", "col", None, None, None),
            P("row", "col", None),
            P("row", "col", None),
            P("col"),
            P("row"),
            P("col"),
            P("col"),
            P("col"),
            P("col"),
            P("row"),
        ),
        out_specs=(P("col"), P("row")),
        check_vma=False,
    )
```

```python
import functools

import jax
import jax.numpy as jnp
from jax import lax
from jax.experimental import pallas as pl
from jax.experimental.pallas import tpu as pltpu
from jax.sharding import PartitionSpec as P

SMALL_EPS = 1e-06
STEP_SCALE = 0.3

CHUNKS = 8
FIRST_GROUP = 32
GROUP = 128
AHEAD = 3
ROW_HALVING = 1
QUARTERS = 4
FIRST_VMEM = 44 * 1024 * 1024
BLOCK_VMEM = 20 * 1024 * 1024
SMALL_VMEM = 8 * 1024 * 1024


def bit_of(index, bit):
    return jnp.where((index & bit) != 0, 1, 0)


def row_mask():
    return bit_of(lax.axis_index("col"), ROW_HALVING) * (CHUNKS // 2)


def col_mask():
    return (lax.axis_index("row") & (QUARTERS - 1)) * (CHUNKS // QUARTERS)


def col_place(tile, count, mask):
    return jnp.where(tile < 0, count, tile ^ (mask * (count // CHUNKS)))


def row_place(tile, count, mask):
    return jnp.where(tile < 0, count, tile ^ (mask * (count // CHUNKS)))


def chunk_rows(chunk, size):
    return pl.ds(pl.multiple_of(chunk * size, size), size)


def piece_chunk(pieces, place, size, offset=0):
    per_piece = CHUNKS // len(pieces)
    start = offset + (place % per_piece) * size
    return pieces[place // per_piece], pl.ds(start, size)


def store_pieces(acc, pieces, count):
    size = count // len(pieces)
    for index, piece in enumerate(pieces):
        piece[...] = acc[pl.ds(index * size, size), :]


def add_row(acc, place, term, combine):
    acc[pl.ds(place, 1), :] = combine(acc[pl.ds(place, 1), :], term)


def one_row(ref, tile):
    return ref[pl.ds(jnp.maximum(tile, 0), 1), :]


def tree_of(parts, combine):
    while len(parts) > 1:
        parts = [combine(parts[i], parts[i + 1]) for i in range(0, len(parts), 2)]
    return parts[0]


def tree_sum(parts):
    return tree_of(parts, jnp.add)


def fold_rows(values):
    return jnp.sum(values.reshape(-1, 8, values.shape[-1]), axis=0)


def block_copy(index, values_ref, blocks, arrived):
    part = pl.ds(pl.multiple_of(index * FIRST_GROUP, FIRST_GROUP), FIRST_GROUP)
    return pltpu.make_async_copy(values_ref.at[part], blocks.at[part], arrived.at[index])


def for_slots(ids_ref, visit, finish, group=GROUP, before=None):
    count = ids_ref.shape[0] // 2

    def step(index, carry):
        if before is not None:
            before(index)
        slots = [index * group + inner for inner in range(group)]
        ids = [(ids_ref[slot], ids_ref[count + slot]) for slot in slots]
        terms = visit(slots, ids)
        for (row, col), term in zip(ids, terms):
            finish(row, col, term)
        return carry

    lax.fori_loop(0, count // group, step, 0)


def product_terms(vector_ref, tiles, blocks):
    width = vector_ref.shape[1]
    place = lax.broadcasted_iota(jnp.int32, (8, width), 0)
    terms = []
    for start in range(0, len(tiles), 4):
        rows = [one_row(vector_ref, tile) for tile in tiles[start : start + 4]]
        left = jnp.where(place == 0, rows[0], jnp.where(place == 1, rows[1], 0.0))
        right = jnp.where(place == 2, rows[2], jnp.where(place == 3, rows[3], 0.0))
        quad = blocks[start : start + 4]
        found = jnp.dot(
            jnp.concatenate([left, right], axis=1).astype(jnp.bfloat16),
            jnp.concatenate(
                [jnp.concatenate(quad[:2], axis=1), jnp.concatenate(quad[2:], axis=1)], axis=0
            ),
            preferred_element_type=jnp.float32,
        )
        for index in range(4):
            side = (index % 2) * width
            terms.append(found[index : index + 1, side : side + width])
    return terms


def row_max(values):
    return jnp.max(values, axis=0, keepdims=True)


def packed_max(values):
    folded = jnp.max(values.reshape(-1, 16, values.shape[-1]), axis=0)
    return row_max(folded.astype(jnp.float32))


def first_pass_kernel(count, ids_ref, values_ref, *refs):
    row_out, col_out, blocks = refs[:2], refs[2:6], refs[6]
    arrived, row_acc, col_acc = refs[7:]
    mask, across = col_mask(), row_mask()
    groups = values_ref.shape[0] // FIRST_GROUP
    for index in range(min(AHEAD, groups)):
        block_copy(index, values_ref, blocks, arrived).start()
    for acc in (row_acc, col_acc):
        acc[...] = jnp.zeros_like(acc)

    def before(index):
        block_copy(index, values_ref, blocks, arrived).wait()

        @pl.when(index + AHEAD < groups)
        def _():
            block_copy(index + AHEAD, values_ref, blocks, arrived).start()

    def visit(slots, ids):
        sizes = [jnp.abs(blocks[slot]) for slot in slots]
        return [(packed_max(size.T), packed_max(size)) for size in sizes]

    def finish(row, col, terms):
        add_row(row_acc, row_place(row, count, across), terms[0], jnp.maximum)
        add_row(col_acc, col_place(col, count, mask), terms[1], jnp.maximum)

    for_slots(ids_ref, visit, finish, FIRST_GROUP, before)
    store_pieces(row_acc, row_out, count)
    store_pieces(col_acc, col_out, count)


def first_product_kernel(count, ids_ref, blocks, dual_ref, *refs):
    product_out, turned, product_acc = refs[:4], refs[4], refs[5]
    mask = col_mask()
    product_acc[...] = jnp.zeros_like(product_acc)

    def visit(slots, ids):
        found = [blocks[slot] for slot in slots]
        for slot, block in zip(slots, found):
            turned[slot] = block.T
        return product_terms(dual_ref, [row for row, _ in ids], found)

    def finish(row, col, term):
        add_row(product_acc, col_place(col, count, mask), term, jnp.add)

    for_slots(ids_ref, visit, finish)
    store_pieces(product_acc, product_out, count)


def scaled_peaks(slots, scales, direct, flipped):
    width = direct.shape[-1]
    square = (width, width)
    diagonal = lax.broadcasted_iota(jnp.int32, square, 0) == lax.broadcasted_iota(
        jnp.int32, square, 1
    )
    diagonal = diagonal.astype(jnp.float32).astype(jnp.bfloat16)
    found = []
    for index, (slot, scale) in enumerate(zip(slots, scales)):
        if index % 2:
            scaled = (jnp.abs(flipped[slot]).astype(jnp.float32) * scale).T
        else:
            sizes = jnp.abs(direct[slot])
            high = scale.astype(jnp.bfloat16)
            low = (scale - high.astype(jnp.float32)).astype(jnp.bfloat16)
            scaled = jnp.dot(
                jnp.concatenate([diagonal * high, diagonal * low], axis=1),
                jnp.concatenate([sizes, sizes], axis=0),
                preferred_element_type=jnp.float32,
            )
        found.append(row_max(scaled))
    return found


def second_cols_kernel(count, ids_ref, blocks, turned, *refs):
    row_in, col_out, row_scale, col_acc = refs[:2], refs[2:6], refs[6], refs[7]
    mask, across = col_mask(), row_mask()
    size = count // CHUNKS
    col_acc[...] = jnp.zeros_like(col_acc)
    for place in range(CHUNKS):
        piece, part = piece_chunk(row_in, place, size)
        row_scale[chunk_rows(place ^ across, size), :] = lax.rsqrt(piece[part, :] + SMALL_EPS)

    def visit(slots, ids):
        scales = [one_row(row_scale, row) for row, _ in ids]
        return scaled_peaks(slots, scales, blocks, turned)

    def finish(row, col, term):
        add_row(col_acc, col_place(col, count, mask), term, jnp.maximum)

    for_slots(ids_ref, visit, finish)
    store_pieces(col_acc, col_out, count)


def second_rows_kernel(count, ids_ref, blocks, turned, *refs):
    col_in, row_out, col_scale, row_acc = refs[:4], refs[4:6], refs[6], refs[7]
    mask, across = col_mask(), row_mask()
    size = count // CHUNKS
    row_acc[...] = jnp.zeros_like(row_acc)
    for place in range(CHUNKS):
        piece, part = piece_chunk(col_in, place, size)
        col_scale[chunk_rows(place ^ mask, size), :] = lax.rsqrt(piece[part, :] + SMALL_EPS)

    def visit(slots, ids):
        scales = [one_row(col_scale, col) for _, col in ids]
        return scaled_peaks(slots, scales, turned, blocks)

    def finish(row, col, term):
        add_row(row_acc, row_place(row, count, across), term, jnp.maximum)

    for_slots(ids_ref, visit, finish)
    store_pieces(row_acc, row_out, count)


def next_scale(scale, piece, inside):
    return scale * lax.rsqrt(scale * piece[inside, :] + SMALL_EPS)


def row_scale_kernel(count, near, far, scale_ref, vector_ref, new_scale, squares):
    across = row_mask()
    size = count // CHUNKS
    sums = []
    for place in range(CHUNKS):
        part = chunk_rows(place ^ across, size)
        piece, inside = piece_chunk((near, far), place, size)
        scale = next_scale(scale_ref[part, :], piece, inside)
        new_scale[part, :] = scale
        scaled = scale * vector_ref[part, :]
        sums.append(fold_rows(scaled * scaled))
    half = CHUNKS // 2
    squares[...] = tree_sum(sums[:half]) + tree_sum(sums[half:])


def col_scale_kernel(count, *refs):
    pieces, (scale_ref, vector_ref, new_scale, squares) = refs[:4], refs[4:]
    mask = col_mask()
    size = count // CHUNKS
    sums = []
    for place in range(CHUNKS):
        part = chunk_rows(place ^ mask, size)
        piece, inside = piece_chunk(pieces, place, size)
        scale = next_scale(scale_ref[part, :], piece, inside)
        new_scale[part, :] = scale
        scaled = scale * vector_ref[part, :]
        sums.append(fold_rows(scaled * scaled))
    squares[...] = tree_sum(sums)


def norm_ratio(cost_squares, demand_squares):
    cost_total = jnp.sum(cost_squares[...], keepdims=True)
    demand_total = jnp.sum(demand_squares[...], keepdims=True)
    return jnp.sqrt(cost_total + SMALL_EPS) / jnp.sqrt(demand_total + SMALL_EPS)


def forward_kernel(count, first, last, ids_ref, turned, *refs):
    product, refs = refs[:4], refs[4:]
    scale_ref, cost_ref, low_ref, high_ref, kind_ref, primal_ref = refs[:6]
    cost_squares, demand_squares, primal_out = refs[6:9]
    row_out, refs = refs[9:11], refs[11:]
    shifted, row_acc = refs[:2]
    moved_ref = primal_out
    if last:
        moved_ref, written = refs[2:]
    mask, across = col_mask(), row_mask()
    size = count // CHUNKS
    row_acc[...] = jnp.zeros_like(row_acc)
    primal_step = STEP_SCALE / norm_ratio(cost_squares, demand_squares)
    for place in range(CHUNKS):
        part = chunk_rows(place ^ mask, size)
        behind = product[0].shape[0] - count // QUARTERS
        piece, inside = piece_chunk(product, place, size, behind)
        scale = scale_ref[part, :]
        inverse = 1.0 / scale
        primal = primal_ref[part, :]
        if first:
            primal = primal * inverse
        gradient = scale * piece[inside, :]
        moved = primal - primal_step * (scale * cost_ref[part, :] - gradient)
        kind = kind_ref[part, :]
        moved = jnp.where(
            (kind == 1) | (kind == 3), jnp.maximum(moved, low_ref[part, :] * inverse), moved
        )
        moved = jnp.where(
            (kind == 2) | (kind == 3), jnp.minimum(moved, high_ref[part, :] * inverse), moved
        )
        shifted[part, :] = scale * (2.0 * moved - primal)
        moved_ref[part, :] = scale * moved if last else moved

    if last:
        copy_out = pltpu.make_async_copy(moved_ref, primal_out, written)
        copy_out.start()

    def visit(slots, ids):
        return product_terms(shifted, [col for _, col in ids], [turned[slot] for slot in slots])

    def finish(row, col, term):
        add_row(row_acc, row_place(row, count, across), term, jnp.add)

    for_slots(ids_ref, visit, finish)
    store_pieces(row_acc, row_out, count)
    if last:
        copy_out.wait()


def next_dual(first, image, inside, scale, demand, dual, dual_step):
    if first:
        dual = dual / scale
    row_image = scale * image[inside, :]
    return jnp.maximum(dual + dual_step * (scale * demand - row_image), 0.0)


def transposed_kernel(count, first, ids_ref, blocks, *refs):
    image, refs = refs[:2], refs[2:]
    scale_ref, demand_ref, dual_ref, cost_squares, demand_squares, dual_out = refs[:6]
    product_out, (weights, product_acc) = refs[6:10], refs[10:]
    mask, across = col_mask(), row_mask()
    size = count // CHUNKS
    product_acc[...] = jnp.zeros_like(product_acc)
    dual_step = STEP_SCALE * norm_ratio(cost_squares, demand_squares)
    for place in range(CHUNKS):
        part = chunk_rows(place ^ across, size)
        piece, inside = piece_chunk(image, place, size)
        scale = scale_ref[part, :]
        dual = next_dual(
            first, piece, inside, scale, demand_ref[part, :], dual_ref[part, :], dual_step
        )
        dual_out[part, :] = dual
        weights[part, :] = scale * dual

    def visit(slots, ids):
        return product_terms(weights, [row for row, _ in ids], [blocks[slot] for slot in slots])

    def finish(row, col, term):
        add_row(product_acc, col_place(col, count, mask), term, jnp.add)

    for_slots(ids_ref, visit, finish)
    store_pieces(product_acc, product_out, count)


def last_dual_kernel(count, first, *refs):
    image, refs = refs[:2], refs[2:]
    scale_ref, demand_ref, dual_ref, cost_squares, demand_squares, dual_out = refs
    across = row_mask()
    size = count // CHUNKS
    dual_step = STEP_SCALE * norm_ratio(cost_squares, demand_squares)
    for place in range(CHUNKS):
        part = chunk_rows(place ^ across, size)
        piece, inside = piece_chunk(image, place, size)
        scale = scale_ref[part, :]
        dual = next_dual(
            first, piece, inside, scale, demand_ref[part, :], dual_ref[part, :], dual_step
        )
        dual_out[part, :] = scale * dual


def vectors(*row_counts):
    return [jax.ShapeDtypeStruct((rows, 128), jnp.float32) for rows in row_counts]


def call_plain(kernel, operands, out_shape):
    return pl.pallas_call(
        kernel,
        out_shape=out_shape,
        in_specs=[pl.BlockSpec(memory_space=pltpu.VMEM)] * len(operands),
        out_specs=[pl.BlockSpec(memory_space=pltpu.VMEM)] * len(out_shape),
        compiler_params=pltpu.CompilerParams(vmem_limit_bytes=SMALL_VMEM),
    )(*operands)


def call_blocks(kernel, ids, values, operands, out_shape, scratch, first=False, last=False):
    width = values.shape[1]
    scratch_shapes = [pltpu.VMEM((rows, width), jnp.float32) for rows in scratch]
    if first:
        arrivals = pltpu.SemaphoreType.DMA((values.shape[0] // FIRST_GROUP,))
        scratch_shapes = [arrivals] + scratch_shapes
    out_specs = [pl.BlockSpec(memory_space=pltpu.VMEM)] * len(out_shape)
    if last:
        out_specs[0] = pl.BlockSpec(memory_space=pl.ANY)
        scratch_shapes = scratch_shapes + [
            pltpu.VMEM(out_shape[0].shape, out_shape[0].dtype),
            pltpu.SemaphoreType.DMA,
        ]
    return pl.pallas_call(
        kernel,
        out_shape=out_shape,
        in_specs=[pl.BlockSpec(memory_space=pltpu.SMEM)]
        + [pl.BlockSpec(memory_space=pl.ANY if first else pltpu.VMEM)]
        + [pl.BlockSpec(memory_space=pltpu.VMEM)] * len(operands),
        out_specs=out_specs,
        scratch_shapes=scratch_shapes,
        compiler_params=pltpu.CompilerParams(
            vmem_limit_bytes=FIRST_VMEM if first else BLOCK_VMEM
        ),
        cost_estimate=pl.CostEstimate(
            flops=2 * values.size, bytes_accessed=2 * values.size, transcendentals=0
        ),
    )(ids, values, *operands)


def swap(vector, axis, size, bit):
    return lax.ppermute(vector, axis, [(i, i ^ bit) for i in range(size)])


def after(values, *earlier):
    return lax.optimization_barrier((values, earlier))[0]


def halve_rows(pieces, groups, combine):
    near, far = pieces
    return combine(near, swap(far, "col", groups, ROW_HALVING))


def exchange_rows(near, groups, combine):
    bit = 1
    while bit < groups:
        if bit != ROW_HALVING:
            near = combine(near, swap(near, "col", groups, bit))
        bit *= 2
    return near


def join_rows(near, groups):
    return [near, swap(near, "col", groups, ROW_HALVING)]


def scatter_cols(pieces, groups, combine, tie=None):
    diagonal = swap(pieces[3], "row", groups, 3)
    first, second = pieces[1:3] if tie is None else after((pieces[1], pieces[2]), tie)
    first, second = swap(first, "row", groups, 1), swap(second, "row", groups, 2)
    return tree_of([pieces[0], first, second, diagonal], combine)


def exchange_cols(piece, groups, combine):
    bit = QUARTERS
    while bit < groups:
        piece = combine(piece, swap(piece, "row", groups, bit))
        bit *= 2
    return piece


def gather_cols(piece, groups):
    diagonal = swap(piece, "row", groups, 3)
    return [piece, swap(piece, "row", groups, 1), swap(piece, "row", groups, 2), diagonal]


def sum_rows(vector, groups):
    vector = exchange_cols(vector, groups, jnp.add)
    return [vector] + [swap(vector, "row", groups, mask) for mask in (1, 2, 3)]


def sum_cols(vector, groups):
    parts = [vector] + [swap(vector, "col", groups, mask) for mask in range(1, groups)]
    return tree_sum(parts)


def per_device(
    row_groups,
    col_groups,
    block_values,
    block_rows,
    block_cols,
    cost_vec,
    demand,
    lower,
    upper,
    bound_kind,
    primal_start,
    dual_start,
):
    values = block_values[0, 0]
    width = values.shape[1]
    ids = jnp.concatenate([block_rows[0, 0], block_cols[0, 0]])
    row_length, col_length = demand.shape[0], cost_vec.shape[0]
    cost_vec, demand, lower, upper, bound_kind, primal_start, dual_start = [
        v.reshape(-1, width)
        for v in (cost_vec, demand, lower, upper, bound_kind, primal_start, dual_start)
    ]
    count = demand.shape[0]
    half, quarter, spare = count // 2, count // QUARTERS, count + 8
    row_pieces, col_pieces = vectors(half, half), vectors(*[quarter] * QUARTERS)
    whole = vectors(count)
    squares = vectors(8)

    def over_col(pieces, combine):
        near = exchange_rows(halve_rows(pieces, col_groups, combine), col_groups, combine)
        return join_rows(near, col_groups)

    def over_row(pieces, combine):
        share = scatter_cols(pieces, row_groups, combine)
        return gather_cols(exchange_cols(share, row_groups, combine), row_groups)

    block_shape = jax.ShapeDtypeStruct(values.shape, values.dtype)
    out = call_blocks(
        functools.partial(first_pass_kernel, count),
        ids,
        values,
        [],
        row_pieces + col_pieces + [block_shape],
        [spare] * 2,
        first=True,
    )
    blocks = out[6]
    near = halve_rows(out[:2], col_groups, jnp.maximum)
    *product_pieces, turned = call_blocks(
        functools.partial(first_product_kernel, count),
        ids,
        blocks,
        [after(dual_start, near)],
        col_pieces + [block_shape],
        [spare],
    )
    share = scatter_cols(out[2:6], row_groups, jnp.maximum, near)
    near = exchange_rows(near, col_groups, jnp.maximum)
    product = scatter_cols(after(product_pieces, near), row_groups, jnp.add)
    share = after(exchange_cols(share, row_groups, jnp.maximum), product_pieces)
    row_peaks = join_rows(near, col_groups)
    *col_pieces_2, row_scale = call_blocks(
        functools.partial(second_cols_kernel, count),
        ids,
        blocks,
        [turned] + after(row_peaks, share),
        col_pieces + whole,
        [spare],
    )
    col_peaks = gather_cols(share, row_groups)
    share = scatter_cols(after(col_pieces_2, col_peaks), row_groups, jnp.maximum)
    product = exchange_cols(after(product, col_pieces_2), row_groups, jnp.add)
    near, far, col_scale = call_blocks(
        functools.partial(second_rows_kernel, count),
        ids,
        blocks,
        [turned] + col_peaks,
        row_pieces + whole,
        [spare],
    )
    near, far = after((near, far), (share, product))
    share = exchange_cols(share, row_groups, jnp.maximum)
    row_scale, demand_squares = call_plain(
        functools.partial(row_scale_kernel, count),
        over_col([near, far], jnp.maximum) + [row_scale, demand],
        whole + squares,
    )
    demand_parts = sum_rows(demand_squares, row_groups)
    gathered = gather_cols(jnp.concatenate([share, product], axis=0), row_groups)
    col_scale, cost_squares = call_plain(
        functools.partial(col_scale_kernel, count),
        gathered + [col_scale, cost_vec],
        whole + squares,
    )
    cost_squares = sum_cols(after(cost_squares, demand_parts[1]), col_groups)
    norms = [cost_squares, tree_sum(demand_parts)]

    def forward(first, last, product, primal):
        out = call_blocks(
            functools.partial(forward_kernel, count, first, last),
            ids,
            turned,
            product + [col_scale, cost_vec, lower, upper, bound_kind, primal] + norms,
            whole + row_pieces,
            [count, spare],
            last=last,
        )
        return out[0], over_col(out[1:], jnp.add)

    primal, image = forward(True, False, gathered, primal_start)
    out = call_blocks(
        functools.partial(transposed_kernel, count, True),
        ids,
        blocks,
        image + [row_scale, demand, dual_start] + norms,
        whole + col_pieces,
        [count, spare],
    )
    dual, product = out[0], over_row(out[1:], jnp.add)
    primal, image = forward(False, True, product, primal)
    (dual,) = call_plain(
        functools.partial(last_dual_kernel, count, False),
        image + [row_scale, demand, dual] + norms,
        whole,
    )
    return primal.reshape(col_length), dual.reshape(row_length)


def solution(mesh):
    def body(*args):
        return per_device(mesh.shape["row"], mesh.shape["col"], *args)

    return jax.shard_map(
        body,
        mesh=mesh,
        in_specs=(
            P("row", "col", None, None, None),
            P("row", "col", None),
            P("row", "col", None),
            P("col"),
            P("row"),
            P("col"),
            P("col"),
            P("col"),
            P("col"),
            P("row"),
        ),
        out_specs=(P("col"), P("row")),
        check_vma=False,
    )
```

```python
import functools

import jax
import jax.numpy as jnp
from jax import lax
from jax.experimental import pallas as pl
from jax.experimental.pallas import tpu as pltpu
from jax.sharding import PartitionSpec as P

SMALL_EPS = 1e-06
STEP_SCALE = 0.3

CHUNKS = 8
FIRST_GROUP = 32
GROUP = 128
AHEAD = 3
ROW_HALVING = 1
QUARTERS = 4
FIRST_VMEM = 44 * 1024 * 1024
BLOCK_VMEM = 20 * 1024 * 1024
SMALL_VMEM = 8 * 1024 * 1024


def bit_of(index, bit):
    return jnp.where((index & bit) != 0, 1, 0)


def row_mask():
    return bit_of(lax.axis_index("col"), ROW_HALVING) * (CHUNKS // 2)


def col_mask():
    return (lax.axis_index("row") & (QUARTERS - 1)) * (CHUNKS // QUARTERS)


def col_place(tile, count, mask):
    return jnp.where(tile < 0, count, tile ^ (mask * (count // CHUNKS)))


def row_place(tile, count, mask):
    return jnp.where(tile < 0, count, tile ^ (mask * (count // CHUNKS)))


def chunk_rows(chunk, size):
    return pl.ds(pl.multiple_of(chunk * size, size), size)


def piece_chunk(pieces, place, size, offset=0):
    per_piece = CHUNKS // len(pieces)
    start = offset + (place % per_piece) * size
    return pieces[place // per_piece], pl.ds(start, size)


def store_pieces(acc, pieces, count):
    size = count // len(pieces)
    for index, piece in enumerate(pieces):
        piece[...] = acc[pl.ds(index * size, size), :]


def add_row(acc, place, term, combine):
    acc[pl.ds(place, 1), :] = combine(acc[pl.ds(place, 1), :], term)


def one_row(ref, tile):
    return ref[pl.ds(jnp.maximum(tile, 0), 1), :]


def tree_of(parts, combine):
    while len(parts) > 1:
        parts = [combine(parts[i], parts[i + 1]) for i in range(0, len(parts), 2)]
    return parts[0]


def tree_sum(parts):
    return tree_of(parts, jnp.add)


def fold_rows(values):
    return jnp.sum(values.reshape(-1, 8, values.shape[-1]), axis=0)


def block_copy(index, values_ref, blocks, arrived):
    part = pl.ds(pl.multiple_of(index * FIRST_GROUP, FIRST_GROUP), FIRST_GROUP)
    return pltpu.make_async_copy(values_ref.at[part], blocks.at[part], arrived.at[index])


def for_slots(ids_ref, visit, finish, group=GROUP, before=None):
    count = ids_ref.shape[0] // 2

    def step(index, carry):
        if before is not None:
            before(index)
        slots = [index * group + inner for inner in range(group)]
        ids = [(ids_ref[slot], ids_ref[count + slot]) for slot in slots]
        terms = visit(slots, ids)
        for (row, col), term in zip(ids, terms):
            finish(row, col, term)
        return carry

    lax.fori_loop(0, count // group, step, 0)


def product_terms(vector_ref, tiles, blocks):
    width = vector_ref.shape[1]
    place = lax.broadcasted_iota(jnp.int32, (8, width), 0)
    terms = []
    for start in range(0, len(tiles), 4):
        rows = [one_row(vector_ref, tile) for tile in tiles[start : start + 4]]
        left = jnp.where(place == 0, rows[0], jnp.where(place == 1, rows[1], 0.0))
        right = jnp.where(place == 2, rows[2], jnp.where(place == 3, rows[3], 0.0))
        quad = blocks[start : start + 4]
        found = jnp.dot(
            jnp.concatenate([left, right], axis=1).astype(jnp.bfloat16),
            jnp.concatenate(
                [jnp.concatenate(quad[:2], axis=1), jnp.concatenate(quad[2:], axis=1)], axis=0
            ),
            preferred_element_type=jnp.float32,
        )
        for index in range(4):
            side = (index % 2) * width
            terms.append(found[index : index + 1, side : side + width])
    return terms


def row_max(values):
    return jnp.max(values, axis=0, keepdims=True)


def packed_max(values):
    folded = jnp.max(values.reshape(-1, 16, values.shape[-1]), axis=0)
    return row_max(folded.astype(jnp.float32))


def first_pass_kernel(count, ids_ref, values_ref, *refs):
    row_out, col_out, blocks = refs[:2], refs[2:6], refs[6]
    arrived, row_acc, col_acc = refs[7:]
    mask, across = col_mask(), row_mask()
    groups = values_ref.shape[0] // FIRST_GROUP
    for index in range(min(AHEAD, groups)):
        block_copy(index, values_ref, blocks, arrived).start()
    for acc in (row_acc, col_acc):
        acc[...] = jnp.zeros_like(acc)

    def before(index):
        block_copy(index, values_ref, blocks, arrived).wait()

        @pl.when(index + AHEAD < groups)
        def _():
            block_copy(index + AHEAD, values_ref, blocks, arrived).start()

    def visit(slots, ids):
        sizes = [jnp.abs(blocks[slot]) for slot in slots]
        return [(packed_max(size.T), packed_max(size)) for size in sizes]

    def finish(row, col, terms):
        add_row(row_acc, row_place(row, count, across), terms[0], jnp.maximum)
        add_row(col_acc, col_place(col, count, mask), terms[1], jnp.maximum)

    for_slots(ids_ref, visit, finish, FIRST_GROUP, before)
    store_pieces(row_acc, row_out, count)
    store_pieces(col_acc, col_out, count)


def first_product_kernel(count, ids_ref, blocks, dual_ref, *refs):
    product_out, turned, product_acc = refs[:4], refs[4], refs[5]
    mask = col_mask()
    product_acc[...] = jnp.zeros_like(product_acc)

    def visit(slots, ids):
        found = [blocks[slot] for slot in slots]
        for slot, block in zip(slots, found):
            turned[slot] = block.T
        return product_terms(dual_ref, [row for row, _ in ids], found)

    def finish(row, col, term):
        add_row(product_acc, col_place(col, count, mask), term, jnp.add)

    for_slots(ids_ref, visit, finish)
    store_pieces(product_acc, product_out, count)


def scaled_peaks(slots, scales, direct, flipped):
    width = direct.shape[-1]
    square = (width, width)
    diagonal = lax.broadcasted_iota(jnp.int32, square, 0) == lax.broadcasted_iota(
        jnp.int32, square, 1
    )
    diagonal = diagonal.astype(jnp.float32).astype(jnp.bfloat16)
    found = []
    for index, (slot, scale) in enumerate(zip(slots, scales)):
        if index % 2:
            scaled = (jnp.abs(flipped[slot]).astype(jnp.float32) * scale).T
        else:
            sizes = jnp.abs(direct[slot])
            high = scale.astype(jnp.bfloat16)
            low = (scale - high.astype(jnp.float32)).astype(jnp.bfloat16)
            scaled = jnp.dot(
                jnp.concatenate([diagonal * high, diagonal * low], axis=1),
                jnp.concatenate([sizes, sizes], axis=0),
                preferred_element_type=jnp.float32,
            )
        found.append(row_max(scaled))
    return found


def second_cols_kernel(count, ids_ref, blocks, turned, *refs):
    row_in, col_out, row_scale, col_acc = refs[:2], refs[2:6], refs[6], refs[7]
    mask, across = col_mask(), row_mask()
    size = count // CHUNKS
    col_acc[...] = jnp.zeros_like(col_acc)
    for place in range(CHUNKS):
        piece, part = piece_chunk(row_in, place, size)
        row_scale[chunk_rows(place ^ across, size), :] = lax.rsqrt(piece[part, :] + SMALL_EPS)

    def visit(slots, ids):
        scales = [one_row(row_scale, row) for row, _ in ids]
        return scaled_peaks(slots, scales, blocks, turned)

    def finish(row, col, term):
        add_row(col_acc, col_place(col, count, mask), term, jnp.maximum)

    for_slots(ids_ref, visit, finish)
    store_pieces(col_acc, col_out, count)


def second_rows_kernel(count, ids_ref, blocks, turned, *refs):
    col_in, row_out, col_scale, row_acc = refs[:4], refs[4:6], refs[6], refs[7]
    mask, across = col_mask(), row_mask()
    size = count // CHUNKS
    row_acc[...] = jnp.zeros_like(row_acc)
    for place in range(CHUNKS):
        piece, part = piece_chunk(col_in, place, size)
        col_scale[chunk_rows(place ^ mask, size), :] = lax.rsqrt(piece[part, :] + SMALL_EPS)

    def visit(slots, ids):
        scales = [one_row(col_scale, col) for _, col in ids]
        return scaled_peaks(slots, scales, turned, blocks)

    def finish(row, col, term):
        add_row(row_acc, row_place(row, count, across), term, jnp.maximum)

    for_slots(ids_ref, visit, finish)
    store_pieces(row_acc, row_out, count)


def next_scale(scale, piece, inside):
    return scale * lax.rsqrt(scale * piece[inside, :] + SMALL_EPS)


def row_scale_kernel(count, near, far, scale_ref, new_scale):
    across = row_mask()
    size = count // CHUNKS
    for place in range(CHUNKS):
        part = chunk_rows(place ^ across, size)
        piece, inside = piece_chunk((near, far), place, size)
        new_scale[part, :] = next_scale(scale_ref[part, :], piece, inside)


def demand_kernel(count, near, scale_ref, demand_ref, squares):
    across = row_mask()
    size = count // CHUNKS
    sums = []
    for place in range(CHUNKS // 2):
        part = chunk_rows(place ^ across, size)
        scale = next_scale(scale_ref[part, :], near, pl.ds(place * size, size))
        scaled = scale * demand_ref[part, :]
        sums.append(fold_rows(scaled * scaled))
    squares[...] = tree_sum(sums)


def col_scale_kernel(count, *refs):
    pieces, (scale_ref, vector_ref, new_scale, squares, demand_squares) = refs[:4], refs[4:]
    mask = col_mask()
    size = count // CHUNKS
    sums = []
    for place in range(CHUNKS):
        part = chunk_rows(place ^ mask, size)
        piece, inside = piece_chunk(pieces, place, size)
        scale = next_scale(scale_ref[part, :], piece, inside)
        new_scale[part, :] = scale
        scaled = scale * vector_ref[part, :]
        sums.append(fold_rows(scaled * scaled))
    squares[...] = tree_sum(sums)
    tail = pl.ds(count // QUARTERS, 8)
    demand_squares[...] = tree_sum([piece[tail, :] for piece in pieces])


def norm_ratio(cost_squares, demand_squares):
    cost_total = jnp.sum(cost_squares[...], keepdims=True)
    demand_total = jnp.sum(demand_squares[...], keepdims=True)
    return jnp.sqrt(cost_total + SMALL_EPS) / jnp.sqrt(demand_total + SMALL_EPS)


def forward_kernel(count, first, last, ids_ref, turned, *refs):
    product, refs = refs[:4], refs[4:]
    scale_ref, cost_ref, low_ref, high_ref, kind_ref, primal_ref = refs[:6]
    cost_squares, demand_squares, primal_out = refs[6:9]
    row_out, refs = refs[9:11], refs[11:]
    shifted, row_acc = refs[:2]
    moved_ref = primal_out
    if last:
        moved_ref, written = refs[2:]
    mask, across = col_mask(), row_mask()
    size = count // CHUNKS
    row_acc[...] = jnp.zeros_like(row_acc)
    primal_step = STEP_SCALE / norm_ratio(cost_squares, demand_squares)
    for place in range(CHUNKS):
        part = chunk_rows(place ^ mask, size)
        behind = product[0].shape[0] - count // QUARTERS
        piece, inside = piece_chunk(product, place, size, behind)
        scale = scale_ref[part, :]
        inverse = 1.0 / scale
        primal = primal_ref[part, :]
        if first:
            primal = primal * inverse
        gradient = scale * piece[inside, :]
        moved = primal - primal_step * (scale * cost_ref[part, :] - gradient)
        kind = kind_ref[part, :]
        moved = jnp.where(
            (kind == 1) | (kind == 3), jnp.maximum(moved, low_ref[part, :] * inverse), moved
        )
        moved = jnp.where(
            (kind == 2) | (kind == 3), jnp.minimum(moved, high_ref[part, :] * inverse), moved
        )
        shifted[part, :] = scale * (2.0 * moved - primal)
        moved_ref[part, :] = scale * moved if last else moved

    if last:
        copy_out = pltpu.make_async_copy(moved_ref, primal_out, written)
        copy_out.start()

    def visit(slots, ids):
        return product_terms(shifted, [col for _, col in ids], [turned[slot] for slot in slots])

    def finish(row, col, term):
        add_row(row_acc, row_place(row, count, across), term, jnp.add)

    for_slots(ids_ref, visit, finish)
    store_pieces(row_acc, row_out, count)
    if last:
        copy_out.wait()


def next_dual(first, image, inside, scale, demand, dual, dual_step):
    if first:
        dual = dual / scale
    row_image = scale * image[inside, :]
    return jnp.maximum(dual + dual_step * (scale * demand - row_image), 0.0)


def transposed_kernel(count, first, ids_ref, blocks, *refs):
    image, refs = refs[:2], refs[2:]
    scale_ref, demand_ref, dual_ref, cost_squares, demand_squares, dual_out = refs[:6]
    product_out, (weights, product_acc) = refs[6:10], refs[10:]
    mask, across = col_mask(), row_mask()
    size = count // CHUNKS
    product_acc[...] = jnp.zeros_like(product_acc)
    dual_step = STEP_SCALE * norm_ratio(cost_squares, demand_squares)
    for place in range(CHUNKS):
        part = chunk_rows(place ^ across, size)
        piece, inside = piece_chunk(image, place, size)
        scale = scale_ref[part, :]
        dual = next_dual(
            first, piece, inside, scale, demand_ref[part, :], dual_ref[part, :], dual_step
        )
        dual_out[part, :] = dual
        weights[part, :] = scale * dual

    def visit(slots, ids):
        return product_terms(weights, [row for row, _ in ids], [blocks[slot] for slot in slots])

    def finish(row, col, term):
        add_row(product_acc, col_place(col, count, mask), term, jnp.add)

    for_slots(ids_ref, visit, finish)
    store_pieces(product_acc, product_out, count)


def last_dual_kernel(count, first, *refs):
    image, refs = refs[:2], refs[2:]
    scale_ref, demand_ref, dual_ref, cost_squares, demand_squares, dual_out = refs
    across = row_mask()
    size = count // CHUNKS
    dual_step = STEP_SCALE * norm_ratio(cost_squares, demand_squares)
    for place in range(CHUNKS):
        part = chunk_rows(place ^ across, size)
        piece, inside = piece_chunk(image, place, size)
        scale = scale_ref[part, :]
        dual = next_dual(
            first, piece, inside, scale, demand_ref[part, :], dual_ref[part, :], dual_step
        )
        dual_out[part, :] = scale * dual


def vectors(*row_counts):
    return [jax.ShapeDtypeStruct((rows, 128), jnp.float32) for rows in row_counts]


def call_plain(kernel, operands, out_shape):
    return pl.pallas_call(
        kernel,
        out_shape=out_shape,
        in_specs=[pl.BlockSpec(memory_space=pltpu.VMEM)] * len(operands),
        out_specs=[pl.BlockSpec(memory_space=pltpu.VMEM)] * len(out_shape),
        compiler_params=pltpu.CompilerParams(vmem_limit_bytes=SMALL_VMEM),
    )(*operands)


def call_blocks(kernel, ids, values, operands, out_shape, scratch, first=False, last=False):
    width = values.shape[1]
    scratch_shapes = [pltpu.VMEM((rows, width), jnp.float32) for rows in scratch]
    if first:
        arrivals = pltpu.SemaphoreType.DMA((values.shape[0] // FIRST_GROUP,))
        scratch_shapes = [arrivals] + scratch_shapes
    out_specs = [pl.BlockSpec(memory_space=pltpu.VMEM)] * len(out_shape)
    if last:
        out_specs[0] = pl.BlockSpec(memory_space=pl.ANY)
        scratch_shapes = scratch_shapes + [
            pltpu.VMEM(out_shape[0].shape, out_shape[0].dtype),
            pltpu.SemaphoreType.DMA,
        ]
    return pl.pallas_call(
        kernel,
        out_shape=out_shape,
        in_specs=[pl.BlockSpec(memory_space=pltpu.SMEM)]
        + [pl.BlockSpec(memory_space=pl.ANY if first else pltpu.VMEM)]
        + [pl.BlockSpec(memory_space=pltpu.VMEM)] * len(operands),
        out_specs=out_specs,
        scratch_shapes=scratch_shapes,
        compiler_params=pltpu.CompilerParams(
            vmem_limit_bytes=FIRST_VMEM if first else BLOCK_VMEM
        ),
        cost_estimate=pl.CostEstimate(
            flops=2 * values.size, bytes_accessed=2 * values.size, transcendentals=0
        ),
    )(ids, values, *operands)


def swap(vector, axis, size, bit):
    return lax.ppermute(vector, axis, [(i, i ^ bit) for i in range(size)])


def after(values, *earlier):
    return lax.optimization_barrier((values, earlier))[0]


def halve_rows(pieces, groups, combine):
    near, far = pieces
    return combine(near, swap(far, "col", groups, ROW_HALVING))


def exchange_rows(near, groups, combine):
    bit = 1
    while bit < groups:
        if bit != ROW_HALVING:
            near = combine(near, swap(near, "col", groups, bit))
        bit *= 2
    return near


def join_rows(near, groups):
    return [near, swap(near, "col", groups, ROW_HALVING)]


def scatter_cols(pieces, groups, combine, tie=None):
    diagonal = swap(pieces[3], "row", groups, 3)
    first, second = pieces[1:3] if tie is None else after((pieces[1], pieces[2]), tie)
    first, second = swap(first, "row", groups, 1), swap(second, "row", groups, 2)
    return tree_of([pieces[0], first, second, diagonal], combine)


def exchange_cols(piece, groups, combine, tie=None):
    bit = QUARTERS
    while bit < groups:
        got = swap(piece, "row", groups, bit)
        piece = combine(piece, got if tie is None else after(got, tie))
        bit *= 2
    return piece


def gather_cols(piece, groups):
    diagonal = swap(piece, "row", groups, 3)
    return [piece, swap(piece, "row", groups, 1), swap(piece, "row", groups, 2), diagonal]


def sum_cols(vector, groups):
    parts = [vector] + [swap(vector, "col", groups, mask) for mask in range(1, groups)]
    return tree_sum(parts)


def per_device(
    row_groups,
    col_groups,
    block_values,
    block_rows,
    block_cols,
    cost_vec,
    demand,
    lower,
    upper,
    bound_kind,
    primal_start,
    dual_start,
):
    values = block_values[0, 0]
    width = values.shape[1]
    ids = jnp.concatenate([block_rows[0, 0], block_cols[0, 0]])
    row_length, col_length = demand.shape[0], cost_vec.shape[0]
    cost_vec, demand, lower, upper, bound_kind, primal_start, dual_start = [
        v.reshape(-1, width)
        for v in (cost_vec, demand, lower, upper, bound_kind, primal_start, dual_start)
    ]
    count = demand.shape[0]
    half, quarter, spare = count // 2, count // QUARTERS, count + 8
    row_pieces, col_pieces = vectors(half, half), vectors(*[quarter] * QUARTERS)
    whole = vectors(count)
    squares = vectors(8)

    def over_col(pieces, combine):
        near = exchange_rows(halve_rows(pieces, col_groups, combine), col_groups, combine)
        return join_rows(near, col_groups)

    def over_row(pieces, combine):
        share = scatter_cols(pieces, row_groups, combine)
        return gather_cols(exchange_cols(share, row_groups, combine), row_groups)

    block_shape = jax.ShapeDtypeStruct(values.shape, values.dtype)
    out = call_blocks(
        functools.partial(first_pass_kernel, count),
        ids,
        values,
        [],
        row_pieces + col_pieces + [block_shape],
        [spare] * 2,
        first=True,
    )
    blocks = out[6]
    near = halve_rows(out[:2], col_groups, jnp.maximum)
    *product_pieces, turned = call_blocks(
        functools.partial(first_product_kernel, count),
        ids,
        blocks,
        [after(dual_start, near)],
        col_pieces + [block_shape],
        [spare],
    )
    share = scatter_cols(out[2:6], row_groups, jnp.maximum, near)
    near = exchange_rows(near, col_groups, jnp.maximum)
    product = scatter_cols(after(product_pieces, near), row_groups, jnp.add)
    share = after(exchange_cols(share, row_groups, jnp.maximum), product_pieces)
    row_peaks = join_rows(near, col_groups)
    *col_pieces_2, row_scale = call_blocks(
        functools.partial(second_cols_kernel, count),
        ids,
        blocks,
        [turned] + after(row_peaks, share),
        col_pieces + whole,
        [spare],
    )
    col_peaks = gather_cols(share, row_groups)
    share = scatter_cols(after(col_pieces_2, col_peaks), row_groups, jnp.maximum)
    product = exchange_cols(after(product, col_pieces_2), row_groups, jnp.add)
    near, far, col_scale = call_blocks(
        functools.partial(second_rows_kernel, count),
        ids,
        blocks,
        [turned] + col_peaks,
        row_pieces + whole,
        [spare],
    )
    near, far = after((near, far), (share, product))
    near = exchange_rows(
        halve_rows([near, far], col_groups, jnp.maximum), col_groups, jnp.maximum
    )
    (demand_squares,) = call_plain(
        functools.partial(demand_kernel, count), [near, row_scale, demand], squares
    )
    demand_squares = demand_squares + swap(demand_squares, "col", col_groups, ROW_HALVING)
    (row_scale,) = call_plain(
        functools.partial(row_scale_kernel, count),
        join_rows(near, col_groups) + [row_scale],
        whole,
    )
    share = exchange_cols(share, row_groups, jnp.maximum, demand_squares)
    gathered = gather_cols(
        jnp.concatenate([share, demand_squares, product], axis=0), row_groups
    )
    col_scale, cost_squares, demand_squares = call_plain(
        functools.partial(col_scale_kernel, count),
        gathered + [col_scale, cost_vec],
        whole + squares + squares,
    )
    demand_squares = exchange_cols(demand_squares, row_groups, jnp.add)
    norms = [sum_cols(cost_squares, col_groups), demand_squares]

    def forward(first, last, product, primal):
        out = call_blocks(
            functools.partial(forward_kernel, count, first, last),
            ids,
            turned,
            product + [col_scale, cost_vec, lower, upper, bound_kind, primal] + norms,
            whole + row_pieces,
            [count, spare],
            last=last,
        )
        return out[0], over_col(out[1:], jnp.add)

    primal, image = forward(True, False, gathered, primal_start)
    out = call_blocks(
        functools.partial(transposed_kernel, count, True),
        ids,
        blocks,
        image + [row_scale, demand, dual_start] + norms,
        whole + col_pieces,
        [count, spare],
    )
    dual, product = out[0], over_row(out[1:], jnp.add)
    primal, image = forward(False, True, product, primal)
    (dual,) = call_plain(
        functools.partial(last_dual_kernel, count, False),
        image + [row_scale, demand, dual] + norms,
        whole,
    )
    return primal.reshape(col_length), dual.reshape(row_length)


def solution(mesh):
    def body(*args):
        return per_device(mesh.shape["row"], mesh.shape["col"], *args)

    return jax.shard_map(
        body,
        mesh=mesh,
        in_specs=(
            P("row", "col", None, None, None),
            P("row", "col", None),
            P("row", "col", None),
            P("col"),
            P("row"),
            P("col"),
            P("col"),
            P("col"),
            P("col"),
            P("row"),
        ),
        out_specs=(P("col"), P("row")),
        check_vma=False,
    )
```

```python
import functools

import jax
import jax.numpy as jnp
from jax import lax
from jax.experimental import pallas as pl
from jax.experimental.pallas import tpu as pltpu
from jax.sharding import PartitionSpec as P

SMALL_EPS = 1e-06
STEP_SCALE = 0.3

CHUNKS = 8
FIRST_GROUP = 64
GROUP = 128
AHEAD = 3
ROW_HALVING = 1
QUARTERS = 4
FIRST_VMEM = 44 * 1024 * 1024
BLOCK_VMEM = 20 * 1024 * 1024
SMALL_VMEM = 8 * 1024 * 1024


def bit_of(index, bit):
    return jnp.where((index & bit) != 0, 1, 0)


def row_mask():
    return bit_of(lax.axis_index("col"), ROW_HALVING) * (CHUNKS // 2)


def col_mask():
    return (lax.axis_index("row") & (QUARTERS - 1)) * (CHUNKS // QUARTERS)


def col_place(tile, count, mask):
    return jnp.where(tile < 0, count, tile ^ (mask * (count // CHUNKS)))


def row_place(tile, count, mask):
    return jnp.where(tile < 0, count, tile ^ (mask * (count // CHUNKS)))


def chunk_rows(chunk, size):
    return pl.ds(pl.multiple_of(chunk * size, size), size)


def piece_chunk(pieces, place, size, offset=0):
    per_piece = CHUNKS // len(pieces)
    start = offset + (place % per_piece) * size
    return pieces[place // per_piece], pl.ds(start, size)


def store_pieces(acc, pieces, count):
    size = count // len(pieces)
    for index, piece in enumerate(pieces):
        piece[...] = acc[pl.ds(index * size, size), :]


def add_row(acc, place, term, combine):
    acc[pl.ds(place, 1), :] = combine(acc[pl.ds(place, 1), :], term)


def one_row(ref, tile):
    return ref[pl.ds(jnp.maximum(tile, 0), 1), :]


def tree_of(parts, combine):
    while len(parts) > 1:
        parts = [combine(parts[i], parts[i + 1]) for i in range(0, len(parts), 2)]
    return parts[0]


def tree_sum(parts):
    return tree_of(parts, jnp.add)


def fold_rows(values):
    return jnp.sum(values.reshape(-1, 8, values.shape[-1]), axis=0)


def block_copy(index, values_ref, blocks, arrived):
    part = pl.ds(pl.multiple_of(index * FIRST_GROUP, FIRST_GROUP), FIRST_GROUP)
    return pltpu.make_async_copy(values_ref.at[part], blocks.at[part], arrived.at[index])


def for_slots(ids_ref, visit, finish, group=GROUP, before=None):
    count = ids_ref.shape[0] // 2

    def step(index, carry):
        if before is not None:
            before(index)
        slots = [index * group + inner for inner in range(group)]
        ids = [(ids_ref[slot], ids_ref[count + slot]) for slot in slots]
        terms = visit(slots, ids)
        for (row, col), term in zip(ids, terms):
            finish(row, col, term)
        return carry

    lax.fori_loop(0, count // group, step, 0)


def product_terms(vector_ref, tiles, blocks):
    width = vector_ref.shape[1]
    place = lax.broadcasted_iota(jnp.int32, (8, width), 0)
    terms = []
    for start in range(0, len(tiles), 4):
        rows = [one_row(vector_ref, tile) for tile in tiles[start : start + 4]]
        left = jnp.where(place == 0, rows[0], jnp.where(place == 1, rows[1], 0.0))
        right = jnp.where(place == 2, rows[2], jnp.where(place == 3, rows[3], 0.0))
        quad = blocks[start : start + 4]
        found = jnp.dot(
            jnp.concatenate([left, right], axis=1).astype(jnp.bfloat16),
            jnp.concatenate(
                [jnp.concatenate(quad[:2], axis=1), jnp.concatenate(quad[2:], axis=1)], axis=0
            ),
            preferred_element_type=jnp.float32,
        )
        for index in range(4):
            side = (index % 2) * width
            terms.append(found[index : index + 1, side : side + width])
    return terms


def row_max(values):
    return jnp.max(values, axis=0, keepdims=True)


def packed_max(values):
    folded = jnp.max(values.reshape(-1, 16, values.shape[-1]), axis=0)
    return row_max(folded.astype(jnp.float32))


def first_pass_kernel(count, ids_ref, values_ref, *refs):
    row_out, col_out, blocks = refs[:2], refs[2:6], refs[6]
    arrived, row_acc, col_acc = refs[7:]
    mask, across = col_mask(), row_mask()
    groups = values_ref.shape[0] // FIRST_GROUP
    for index in range(min(AHEAD, groups)):
        block_copy(index, values_ref, blocks, arrived).start()
    for acc in (row_acc, col_acc):
        acc[...] = jnp.zeros_like(acc)

    def before(index):
        block_copy(index, values_ref, blocks, arrived).wait()

        @pl.when(index + AHEAD < groups)
        def _():
            block_copy(index + AHEAD, values_ref, blocks, arrived).start()

    def visit(slots, ids):
        sizes = [jnp.abs(blocks[slot]) for slot in slots]
        return [(packed_max(size.T), packed_max(size)) for size in sizes]

    def finish(row, col, terms):
        add_row(row_acc, row_place(row, count, across), terms[0], jnp.maximum)
        add_row(col_acc, col_place(col, count, mask), terms[1], jnp.maximum)

    for_slots(ids_ref, visit, finish, FIRST_GROUP, before)
    store_pieces(row_acc, row_out, count)
    store_pieces(col_acc, col_out, count)


def first_product_kernel(count, ids_ref, blocks, dual_ref, *refs):
    product_out, turned, product_acc = refs[:4], refs[4], refs[5]
    mask = col_mask()
    product_acc[...] = jnp.zeros_like(product_acc)

    def visit(slots, ids):
        found = [blocks[slot] for slot in slots]
        for slot, block in zip(slots, found):
            turned[slot] = block.T
        return product_terms(dual_ref, [row for row, _ in ids], found)

    def finish(row, col, term):
        add_row(product_acc, col_place(col, count, mask), term, jnp.add)

    for_slots(ids_ref, visit, finish)
    store_pieces(product_acc, product_out, count)


def scaled_peaks(slots, scales, direct, flipped):
    width = direct.shape[-1]
    square = (width, width)
    diagonal = lax.broadcasted_iota(jnp.int32, square, 0) == lax.broadcasted_iota(
        jnp.int32, square, 1
    )
    diagonal = diagonal.astype(jnp.float32).astype(jnp.bfloat16)
    found = []
    for index, (slot, scale) in enumerate(zip(slots, scales)):
        if index % 2:
            scaled = (jnp.abs(flipped[slot]).astype(jnp.float32) * scale).T
        else:
            sizes = jnp.abs(direct[slot])
            high = scale.astype(jnp.bfloat16)
            low = (scale - high.astype(jnp.float32)).astype(jnp.bfloat16)
            scaled = jnp.dot(
                jnp.concatenate([diagonal * high, diagonal * low], axis=1),
                jnp.concatenate([sizes, sizes], axis=0),
                preferred_element_type=jnp.float32,
            )
        found.append(row_max(scaled))
    return found


def second_cols_kernel(count, ids_ref, blocks, turned, *refs):
    row_in, col_out, row_scale, col_acc = refs[:2], refs[2:6], refs[6], refs[7]
    mask, across = col_mask(), row_mask()
    size = count // CHUNKS
    col_acc[...] = jnp.zeros_like(col_acc)
    for place in range(CHUNKS):
        piece, part = piece_chunk(row_in, place, size)
        row_scale[chunk_rows(place ^ across, size), :] = lax.rsqrt(piece[part, :] + SMALL_EPS)

    def visit(slots, ids):
        scales = [one_row(row_scale, row) for row, _ in ids]
        return scaled_peaks(slots, scales, blocks, turned)

    def finish(row, col, term):
        add_row(col_acc, col_place(col, count, mask), term, jnp.maximum)

    for_slots(ids_ref, visit, finish)
    store_pieces(col_acc, col_out, count)


def second_rows_kernel(count, ids_ref, blocks, turned, *refs):
    col_in, row_out, col_scale, row_acc = refs[:4], refs[4:6], refs[6], refs[7]
    mask, across = col_mask(), row_mask()
    size = count // CHUNKS
    row_acc[...] = jnp.zeros_like(row_acc)
    for place in range(CHUNKS):
        piece, part = piece_chunk(col_in, place, size)
        col_scale[chunk_rows(place ^ mask, size), :] = lax.rsqrt(piece[part, :] + SMALL_EPS)

    def visit(slots, ids):
        scales = [one_row(col_scale, col) for _, col in ids]
        return scaled_peaks(slots, scales, turned, blocks)

    def finish(row, col, term):
        add_row(row_acc, row_place(row, count, across), term, jnp.maximum)

    for_slots(ids_ref, visit, finish)
    store_pieces(row_acc, row_out, count)


def next_scale(scale, piece, inside):
    return scale * lax.rsqrt(scale * piece[inside, :] + SMALL_EPS)


def row_scale_kernel(count, near, far, scale_ref, new_scale):
    across = row_mask()
    size = count // CHUNKS
    for place in range(CHUNKS):
        part = chunk_rows(place ^ across, size)
        piece, inside = piece_chunk((near, far), place, size)
        new_scale[part, :] = next_scale(scale_ref[part, :], piece, inside)


def demand_kernel(count, near, scale_ref, demand_ref, squares):
    across = row_mask()
    size = count // CHUNKS
    sums = []
    for place in range(CHUNKS // 2):
        part = chunk_rows(place ^ across, size)
        scale = next_scale(scale_ref[part, :], near, pl.ds(place * size, size))
        scaled = scale * demand_ref[part, :]
        sums.append(fold_rows(scaled * scaled))
    squares[...] = tree_sum(sums)


def col_scale_kernel(count, *refs):
    pieces, (scale_ref, vector_ref, new_scale, squares, demand_squares) = refs[:4], refs[4:]
    mask = col_mask()
    size = count // CHUNKS
    sums = []
    for place in range(CHUNKS):
        part = chunk_rows(place ^ mask, size)
        piece, inside = piece_chunk(pieces, place, size)
        scale = next_scale(scale_ref[part, :], piece, inside)
        new_scale[part, :] = scale
        scaled = scale * vector_ref[part, :]
        sums.append(fold_rows(scaled * scaled))
    squares[...] = tree_sum(sums)
    tail = pl.ds(count // QUARTERS, 8)
    demand_squares[...] = tree_sum([piece[tail, :] for piece in pieces])


def norm_ratio(cost_squares, demand_squares):
    cost_total = jnp.sum(cost_squares[...], keepdims=True)
    demand_total = jnp.sum(demand_squares[...], keepdims=True)
    return jnp.sqrt(cost_total + SMALL_EPS) / jnp.sqrt(demand_total + SMALL_EPS)


def forward_kernel(count, first, last, ids_ref, turned, *refs):
    product, refs = refs[:4], refs[4:]
    scale_ref, cost_ref, low_ref, high_ref, kind_ref, primal_ref = refs[:6]
    cost_squares, demand_squares, primal_out = refs[6:9]
    row_out, refs = refs[9:11], refs[11:]
    shifted, row_acc = refs[:2]
    moved_ref = primal_out
    if last:
        moved_ref, written = refs[2:]
    mask, across = col_mask(), row_mask()
    size = count // CHUNKS
    row_acc[...] = jnp.zeros_like(row_acc)
    primal_step = STEP_SCALE / norm_ratio(cost_squares, demand_squares)
    for place in range(CHUNKS):
        part = chunk_rows(place ^ mask, size)
        behind = product[0].shape[0] - count // QUARTERS
        piece, inside = piece_chunk(product, place, size, behind)
        scale = scale_ref[part, :]
        inverse = 1.0 / scale
        primal = primal_ref[part, :]
        if first:
            primal = primal * inverse
        gradient = scale * piece[inside, :]
        moved = primal - primal_step * (scale * cost_ref[part, :] - gradient)
        kind = kind_ref[part, :]
        moved = jnp.where(
            (kind == 1) | (kind == 3), jnp.maximum(moved, low_ref[part, :] * inverse), moved
        )
        moved = jnp.where(
            (kind == 2) | (kind == 3), jnp.minimum(moved, high_ref[part, :] * inverse), moved
        )
        shifted[part, :] = scale * (2.0 * moved - primal)
        moved_ref[part, :] = scale * moved if last else moved

    if last:
        copy_out = pltpu.make_async_copy(moved_ref, primal_out, written)
        copy_out.start()

    def visit(slots, ids):
        return product_terms(shifted, [col for _, col in ids], [turned[slot] for slot in slots])

    def finish(row, col, term):
        add_row(row_acc, row_place(row, count, across), term, jnp.add)

    for_slots(ids_ref, visit, finish)
    store_pieces(row_acc, row_out, count)
    if last:
        copy_out.wait()


def next_dual(first, image, inside, scale, demand, dual, dual_step):
    if first:
        dual = dual / scale
    row_image = scale * image[inside, :]
    return jnp.maximum(dual + dual_step * (scale * demand - row_image), 0.0)


def transposed_kernel(count, first, ids_ref, blocks, *refs):
    image, refs = refs[:2], refs[2:]
    scale_ref, demand_ref, dual_ref, cost_squares, demand_squares, dual_out = refs[:6]
    product_out, (weights, product_acc) = refs[6:10], refs[10:]
    mask, across = col_mask(), row_mask()
    size = count // CHUNKS
    product_acc[...] = jnp.zeros_like(product_acc)
    dual_step = STEP_SCALE * norm_ratio(cost_squares, demand_squares)
    for place in range(CHUNKS):
        part = chunk_rows(place ^ across, size)
        piece, inside = piece_chunk(image, place, size)
        scale = scale_ref[part, :]
        dual = next_dual(
            first, piece, inside, scale, demand_ref[part, :], dual_ref[part, :], dual_step
        )
        dual_out[part, :] = dual
        weights[part, :] = scale * dual

    def visit(slots, ids):
        return product_terms(weights, [row for row, _ in ids], [blocks[slot] for slot in slots])

    def finish(row, col, term):
        add_row(product_acc, col_place(col, count, mask), term, jnp.add)

    for_slots(ids_ref, visit, finish)
    store_pieces(product_acc, product_out, count)


def last_dual_kernel(count, first, *refs):
    image, refs = refs[:2], refs[2:]
    scale_ref, demand_ref, dual_ref, cost_squares, demand_squares, dual_out = refs
    across = row_mask()
    size = count // CHUNKS
    dual_step = STEP_SCALE * norm_ratio(cost_squares, demand_squares)
    for place in range(CHUNKS):
        part = chunk_rows(place ^ across, size)
        piece, inside = piece_chunk(image, place, size)
        scale = scale_ref[part, :]
        dual = next_dual(
            first, piece, inside, scale, demand_ref[part, :], dual_ref[part, :], dual_step
        )
        dual_out[part, :] = scale * dual


def vectors(*row_counts):
    return [jax.ShapeDtypeStruct((rows, 128), jnp.float32) for rows in row_counts]


def call_plain(kernel, operands, out_shape):
    return pl.pallas_call(
        kernel,
        out_shape=out_shape,
        in_specs=[pl.BlockSpec(memory_space=pltpu.VMEM)] * len(operands),
        out_specs=[pl.BlockSpec(memory_space=pltpu.VMEM)] * len(out_shape),
        compiler_params=pltpu.CompilerParams(vmem_limit_bytes=SMALL_VMEM),
    )(*operands)


def call_blocks(kernel, ids, values, operands, out_shape, scratch, first=False, last=False):
    width = values.shape[1]
    scratch_shapes = [pltpu.VMEM((rows, width), jnp.float32) for rows in scratch]
    if first:
        arrivals = pltpu.SemaphoreType.DMA((values.shape[0] // FIRST_GROUP,))
        scratch_shapes = [arrivals] + scratch_shapes
    out_specs = [pl.BlockSpec(memory_space=pltpu.VMEM)] * len(out_shape)
    if last:
        out_specs[0] = pl.BlockSpec(memory_space=pl.ANY)
        scratch_shapes = scratch_shapes + [
            pltpu.VMEM(out_shape[0].shape, out_shape[0].dtype),
            pltpu.SemaphoreType.DMA,
        ]
    return pl.pallas_call(
        kernel,
        out_shape=out_shape,
        in_specs=[pl.BlockSpec(memory_space=pltpu.SMEM)]
        + [pl.BlockSpec(memory_space=pl.ANY if first else pltpu.VMEM)]
        + [pl.BlockSpec(memory_space=pltpu.VMEM)] * len(operands),
        out_specs=out_specs,
        scratch_shapes=scratch_shapes,
        compiler_params=pltpu.CompilerParams(
            vmem_limit_bytes=FIRST_VMEM if first else BLOCK_VMEM
        ),
        cost_estimate=pl.CostEstimate(
            flops=2 * values.size, bytes_accessed=2 * values.size, transcendentals=0
        ),
    )(ids, values, *operands)


def swap(vector, axis, size, bit):
    return lax.ppermute(vector, axis, [(i, i ^ bit) for i in range(size)])


def after(values, *earlier):
    return lax.optimization_barrier((values, earlier))[0]


def halve_rows(pieces, groups, combine):
    near, far = pieces
    return combine(near, swap(far, "col", groups, ROW_HALVING))


def exchange_rows(near, groups, combine):
    bit = 1
    while bit < groups:
        if bit != ROW_HALVING:
            near = combine(near, swap(near, "col", groups, bit))
        bit *= 2
    return near


def join_rows(near, groups):
    return [near, swap(near, "col", groups, ROW_HALVING)]


def scatter_cols(pieces, groups, combine, tie=None):
    diagonal = swap(pieces[3], "row", groups, 3)
    first, second = pieces[1:3] if tie is None else after((pieces[1], pieces[2]), tie)
    first, second = swap(first, "row", groups, 1), swap(second, "row", groups, 2)
    return tree_of([pieces[0], first, second, diagonal], combine)


def exchange_cols(piece, groups, combine, tie=None):
    bit = QUARTERS
    while bit < groups:
        got = swap(piece, "row", groups, bit)
        piece = combine(piece, got if tie is None else after(got, tie))
        bit *= 2
    return piece


def gather_cols(piece, groups):
    diagonal = swap(piece, "row", groups, 3)
    return [piece, swap(piece, "row", groups, 1), swap(piece, "row", groups, 2), diagonal]


def sum_cols(vector, groups):
    parts = [vector] + [swap(vector, "col", groups, mask) for mask in range(1, groups)]
    return tree_sum(parts)


def per_device(
    row_groups,
    col_groups,
    block_values,
    block_rows,
    block_cols,
    cost_vec,
    demand,
    lower,
    upper,
    bound_kind,
    primal_start,
    dual_start,
):
    values = block_values[0, 0]
    width = values.shape[1]
    ids = jnp.concatenate([block_rows[0, 0], block_cols[0, 0]])
    row_length, col_length = demand.shape[0], cost_vec.shape[0]
    cost_vec, demand, lower, upper, bound_kind, primal_start, dual_start = [
        v.reshape(-1, width)
        for v in (cost_vec, demand, lower, upper, bound_kind, primal_start, dual_start)
    ]
    count = demand.shape[0]
    half, quarter, spare = count // 2, count // QUARTERS, count + 8
    row_pieces, col_pieces = vectors(half, half), vectors(*[quarter] * QUARTERS)
    whole = vectors(count)
    squares = vectors(8)

    def over_col(pieces, combine):
        near = exchange_rows(halve_rows(pieces, col_groups, combine), col_groups, combine)
        return join_rows(near, col_groups)

    def over_row(pieces, combine):
        share = scatter_cols(pieces, row_groups, combine)
        return gather_cols(exchange_cols(share, row_groups, combine), row_groups)

    block_shape = jax.ShapeDtypeStruct(values.shape, values.dtype)
    out = call_blocks(
        functools.partial(first_pass_kernel, count),
        ids,
        values,
        [],
        row_pieces + col_pieces + [block_shape],
        [spare] * 2,
        first=True,
    )
    blocks = out[6]
    near = halve_rows(out[:2], col_groups, jnp.maximum)
    *product_pieces, turned = call_blocks(
        functools.partial(first_product_kernel, count),
        ids,
        blocks,
        [after(dual_start, near)],
        col_pieces + [block_shape],
        [spare],
    )
    share = scatter_cols(out[2:6], row_groups, jnp.maximum, near)
    near = exchange_rows(near, col_groups, jnp.maximum)
    product = scatter_cols(after(product_pieces, near), row_groups, jnp.add)
    share = after(exchange_cols(share, row_groups, jnp.maximum), product_pieces)
    row_peaks = join_rows(near, col_groups)
    *col_pieces_2, row_scale = call_blocks(
        functools.partial(second_cols_kernel, count),
        ids,
        blocks,
        [turned] + after(row_peaks, share),
        col_pieces + whole,
        [spare],
    )
    col_peaks = gather_cols(share, row_groups)
    share = scatter_cols(after(col_pieces_2, col_peaks), row_groups, jnp.maximum)
    product = exchange_cols(after(product, col_pieces_2), row_groups, jnp.add)
    near, far, col_scale = call_blocks(
        functools.partial(second_rows_kernel, count),
        ids,
        blocks,
        [turned] + col_peaks,
        row_pieces + whole,
        [spare],
    )
    near, far = after((near, far), (share, product))
    near = exchange_rows(
        halve_rows([near, far], col_groups, jnp.maximum), col_groups, jnp.maximum
    )
    (demand_squares,) = call_plain(
        functools.partial(demand_kernel, count), [near, row_scale, demand], squares
    )
    demand_squares = demand_squares + swap(demand_squares, "col", col_groups, ROW_HALVING)
    (row_scale,) = call_plain(
        functools.partial(row_scale_kernel, count),
        join_rows(near, col_groups) + [row_scale],
        whole,
    )
    share = exchange_cols(share, row_groups, jnp.maximum, demand_squares)
    gathered = gather_cols(
        jnp.concatenate([share, demand_squares, product], axis=0), row_groups
    )
    col_scale, cost_squares, demand_squares = call_plain(
        functools.partial(col_scale_kernel, count),
        gathered + [col_scale, cost_vec],
        whole + squares + squares,
    )
    demand_squares = exchange_cols(demand_squares, row_groups, jnp.add)
    norms = [sum_cols(cost_squares, col_groups), demand_squares]

    def forward(first, last, product, primal):
        out = call_blocks(
            functools.partial(forward_kernel, count, first, last),
            ids,
            turned,
            product + [col_scale, cost_vec, lower, upper, bound_kind, primal] + norms,
            whole + row_pieces,
            [count, spare],
            last=last,
        )
        return out[0], over_col(out[1:], jnp.add)

    primal, image = forward(True, False, gathered, primal_start)
    out = call_blocks(
        functools.partial(transposed_kernel, count, True),
        ids,
        blocks,
        image + [row_scale, demand, dual_start] + norms,
        whole + col_pieces,
        [count, spare],
    )
    dual, product = out[0], over_row(out[1:], jnp.add)
    primal, image = forward(False, True, product, primal)
    (dual,) = call_plain(
        functools.partial(last_dual_kernel, count, False),
        image + [row_scale, demand, dual] + norms,
        whole,
    )
    return primal.reshape(col_length), dual.reshape(row_length)


def solution(mesh):
    def body(*args):
        return per_device(mesh.shape["row"], mesh.shape["col"], *args)

    return jax.shard_map(
        body,
        mesh=mesh,
        in_specs=(
            P("row", "col", None, None, None),
            P("row", "col", None),
            P("row", "col", None),
            P("col"),
            P("row"),
            P("col"),
            P("col"),
            P("col"),
            P("col"),
            P("row"),
        ),
        out_specs=(P("col"), P("row")),
        check_vma=False,
    )
```
